32 devices in a mesh: blk: 8 (over z, core), narrow: 4 (over y, x).
Axes of the slice: x: 2, y: 2, z: 4, core: 2. Of those that a mesh axis runs over, the one named last changes fastest.
Arguments:
- student_img: bfloat16 [4096, 1152], P(('blk', 'narrow')), may hold values from -6 to 6
- student_txt: bfloat16 [4096, 1152], P(('blk', 'narrow')), may hold values from -6 to 6
- teacher_img: bfloat16 [4096, 1536], P(('blk', 'narrow')), may hold values from -6 to 6
- teacher_txt: bfloat16 [4096, 1536], P(('blk', 'narrow')), may hold values from -6 to 6
Outputs:
- image_grad: float32 [4096, 1152], P(('blk', 'narrow'))
- text_grad: float32 [4096, 1152], P(('blk', 'narrow'))
The draws below stay inside these ranges and needn't reach their ends.
All inputs are finite; a program needn't handle non-finite values.
Results may differ from the reference program's by a relative error of at most 0.0097.
Values may be sent and summed in bfloat16 or wider, within the bound.
No kernel may reach another device: no remote copies, remote signals or barrier semaphores. Data moves between devices by JAX's collectives and lax.ppermute only.
A program may use at most 128 MiB of HBM per device.

```python
import math
import jax
import jax.numpy as jnp
from jax import lax

STUDENT_WIDTH = 1152
TEACHER_WIDTH = 1536
BATCH = 4096


def steps_of(own_key, extent, shards, smallest, top_value):
    def one(axis_at, shards_of):
        steps = jax.random.uniform(jax.random.fold_in(jax.random.fold_in(own_key, 6), axis_at), (shards_of,), jnp.float32, smallest / len(shards), top_value / len(shards))
        return jnp.repeat(jnp.exp(steps), extent[axis_at] // shards_of).reshape((-1,) + (1,) * (len(extent) - axis_at - 1))

    level = one(*shards[0])
    for cut in shards[1:]:
        level = level * one(*cut)
    return level


def noise(rng, extent, spread, limit, cuts=(), kind=jnp.bfloat16):
    array = jax.random.normal(rng, extent, jnp.float32) * spread
    if len(cuts) > 0:
        array = steps_of(rng, extent, cuts, -0.22, 0.18) * array
    return jnp.clip(array, min=-limit, max=limit).astype(kind)


def setup_inputs(seed: int = 0) -> dict:
    arg_keys = jax.random.split(jax.random.key(seed), 5)
    student_img = noise(arg_keys[0], (BATCH, STUDENT_WIDTH), 1.0, 6.0, ((0, 32),))
    student_txt = noise(arg_keys[1], (BATCH, STUDENT_WIDTH), 1.0, 6.0, ((0, 32),))
    teacher_img = noise(arg_keys[2], (BATCH, TEACHER_WIDTH), 1.0, 6.0, ((0, 32),))
    teacher_txt = noise(arg_keys[3], (BATCH, TEACHER_WIDTH), 1.0, 6.0, ((0, 32),))
    return {"student_img": student_img, "student_txt": student_txt, "teacher_img": teacher_img, "teacher_txt": teacher_txt}


epsilon = 1e-06
logit_scale = 100.0
logit_bias = -4.0

def unit_rows(raw_rows):
    raw_float = raw_rows.astype(jnp.float32)
    radius = jnp.sqrt(lax.optimization_barrier(jnp.sum(raw_float * raw_float, axis=1, keepdims=True)) + epsilon)
    return (raw_float / radius, radius)

def unit_back(grad_unit, unit_float, radius):
    along_unit = lax.optimization_barrier(jnp.sum(unit_float * grad_unit, axis=1, keepdims=True))
    return (grad_unit - unit_float * along_unit) / radius

def reference(student_img, student_txt, teacher_img, teacher_txt):
    img_float, img_radius = unit_rows(student_img)
    txt_float, txt_radius = unit_rows(student_txt)
    img_unit = img_float.astype(jnp.bfloat16)
    txt_unit = txt_float.astype(jnp.bfloat16)
    t_img_unit = unit_rows(teacher_img)[0].astype(jnp.bfloat16)
    t_txt_unit = unit_rows(teacher_txt)[0].astype(jnp.bfloat16)
    total_rows = student_img.shape[0]
    embed_width = student_img.shape[1]
    block_rows = math.gcd(total_rows, 512)
    col_ids = jnp.arange(total_rows, dtype=jnp.int32)[None, :]

    def one_block(txt_acc, block_index):
        first_row = (block_index * block_rows).astype(jnp.int32)
        img_block = lax.dynamic_slice_in_dim(img_unit, first_row, block_rows, 0)
        timg_block = lax.dynamic_slice_in_dim(t_img_unit, first_row, block_rows, 0)
        teacher_logit = logit_scale * jnp.dot(timg_block, t_txt_unit.T, preferred_element_type=jnp.float32) + logit_bias
        student_logit = logit_scale * jnp.dot(img_block, txt_unit.T, preferred_element_type=jnp.float32) + logit_bias
        row_ids = first_row + jnp.arange(block_rows, dtype=jnp.int32)[:, None]
        positive = jnp.where(row_ids == col_ids, 1.0, 0.0).astype(jnp.float32)
        pair_grad = (2.0 * jax.nn.sigmoid(student_logit) - jax.nn.sigmoid(teacher_logit) - positive).astype(jnp.bfloat16)
        img_grad = logit_scale * jnp.dot(pair_grad, txt_unit, preferred_element_type=jnp.float32)
        txt_acc = txt_acc + jnp.dot(pair_grad.T, img_block, preferred_element_type=jnp.float32)
        return (txt_acc, img_grad)
    txt_acc, img_blocks = lax.scan(one_block, jnp.zeros((total_rows, embed_width), jnp.float32), jnp.arange(total_rows // block_rows, dtype=jnp.int32))
    img_grad_unit = img_blocks.reshape(total_rows, embed_width)
    image_grad = unit_back(img_grad_unit, img_float, img_radius)
    text_grad = unit_back(logit_scale * txt_acc, txt_float, txt_radius)
    return (image_grad, text_grad)
```

```python
import functools
import jax
import jax.numpy as jnp
from jax import lax
from jax.experimental import pallas as pl
from jax.experimental.pallas import tpu as pltpu
from jax.sharding import PartitionSpec as P

epsilon = 1e-06
logit_scale = 100.0
logit_bias = -4.0

AXES = ("blk", "narrow")
ANY = pl.BlockSpec(memory_space=pl.ANY)
VMEM = pl.BlockSpec(memory_space=pltpu.VMEM)
f32 = jnp.float32
bf16 = jnp.bfloat16


def split_two(size):
    fast = int(size**0.5)
    while size % fast:
        fast -= 1
    return max(fast, size // fast), min(fast, size // fast)


class Plan:
    def __init__(self, mesh):
        blk, narrow = mesh.shape["blk"], mesh.shape["narrow"]
        core = 2 if blk % 2 == 0 else 1
        far, near = split_two(blk // core)
        large, small = split_two(narrow)
        self.digits = {"far": far, "near": near, "core": core, "row": small, "col": large}
        self.order = ["far", "near", "core", "row", "col"]

    def __getitem__(self, name):
        return self.digits[name]

    def place(self, index):
        out = {}
        for name in reversed(self.order):
            out[name] = index % self.digits[name]
            index //= self.digits[name]
        return out

    def index(self, place):
        out = 0
        for name in self.order:
            out = out * self.digits[name] + place[name]
        return out

    def send(self, x, name, by):
        total = 1
        for size in self.digits.values():
            total *= size
        pairs = []
        for src in range(total):
            place = self.place(src)
            place[name] = (place[name] + by) % self.digits[name]
            pairs.append((src, self.index(place)))
        return lax.ppermute(x, AXES, pairs)


def params(limit=56):
    return pltpu.CompilerParams(vmem_limit_bytes=limit * 2**20)


def tile_rows(rows, most):
    step = most
    while rows % step:
        step //= 2
    return step


def unit_kernel(count, *refs):
    for x_ref, out_ref in zip(refs[:count], refs[count:]):
        rows = x_ref.shape[0]
        step = tile_rows(rows, 32)

        def one(i, carry, x_ref=x_ref, out_ref=out_ref, step=step):
            at = pl.ds(pl.multiple_of(i * step, step), step)
            x = x_ref[at, :].astype(f32)
            scale = 1.0 / jnp.sqrt(jnp.sum(x * x, axis=1, keepdims=True) + epsilon)
            out_ref[at, :] = (x * scale).astype(bf16)
            return carry

        lax.fori_loop(0, rows // step, one, 0)


def unit_rows(*arrays):
    return pl.pallas_call(
        functools.partial(unit_kernel, len(arrays)),
        out_shape=[jax.ShapeDtypeStruct(a.shape, bf16) for a in arrays],
        in_specs=[VMEM] * len(arrays),
        out_specs=[VMEM] * len(arrays),
        compiler_params=params(16),
        cost_estimate=pl.CostEstimate(
            flops=4 * sum(a.size for a in arrays),
            bytes_accessed=4 * sum(a.size for a in arrays),
            transcendentals=0,
        ),
        name="unit_rows",
    )(*arrays)


def load_all(refs, targets, sems):
    copies = []
    for k, (ref, target) in enumerate(zip(refs, targets)):
        copies.append(pltpu.make_async_copy(ref, target, sems.at[k]))
        copies[-1].start()
    return copies


def teacher_kernel(images, texts, *refs):
    img_refs, txt_refs = refs[:images], refs[images : images + texts]
    p_ref, img, txt, sems = refs[images + texts :]
    rows = img_refs[0].shape[0]
    copies = load_all(
        img_refs + txt_refs,
        [img.at[pl.ds(k * rows, rows), :] for k in range(images)]
        + [txt.at[pl.ds(k * rows, rows), :] for k in range(texts)],
        sems,
    )
    for copy in copies:
        copy.wait()
    step = tile_rows(texts * rows, 256)

    def one(j, carry):
        at = pl.ds(pl.multiple_of(j * step, step), step)
        dots = lax.dot_general(img[...], txt[at, :], (((1,), (1,)), ((), ())), preferred_element_type=f32)
        p_ref[:, at] = jax.nn.sigmoid(logit_scale * dots + logit_bias)
        return carry

    lax.fori_loop(0, texts * rows // step, one, 0)
    own = lax.broadcasted_iota(jnp.int32, (rows, rows), 0) == lax.broadcasted_iota(jnp.int32, (rows, rows), 1)
    p_ref[:rows, :rows] = p_ref[:rows, :rows] + jnp.where(own, 1.0, 0.0).astype(f32)


def teacher_targets(img_blocks, txt_blocks):
    images, texts = len(img_blocks), len(txt_blocks)
    rows, width = img_blocks[0].shape
    return pl.pallas_call(
        functools.partial(teacher_kernel, images, texts),
        out_shape=jax.ShapeDtypeStruct((images * rows, texts * rows), f32),
        in_specs=[ANY] * (images + texts),
        out_specs=VMEM,
        scratch_shapes=[
            pltpu.VMEM((images * rows, width), bf16),
            pltpu.VMEM((texts * rows, width), bf16),
            pltpu.SemaphoreType.DMA((images + texts,)),
        ],
        compiler_params=params(),
        cost_estimate=pl.CostEstimate(
            flops=2 * images * texts * rows * rows * width,
            bytes_accessed=2 * (images + texts) * rows * width + 4 * images * texts * rows * rows,
            transcendentals=images * texts * rows * rows,
        ),
        name="teacher_targets",
    )(*img_blocks, *txt_blocks)


def pair_kernel(images, texts, img_out, txt_out, *refs):
    img_refs, txt_refs = refs[:images], refs[images : images + texts]
    p_ref, pair_ref = refs[images + texts : images + texts + 2]
    rest = refs[images + texts + 2 :]
    img_grads, rest = rest[: len(img_out)], rest[len(img_out) :]
    txt_grads, rest = rest[: len(txt_out)], rest[len(txt_out) :]
    img, txt, sems = rest
    rows = img_refs[0].shape[0]
    copies = load_all(
        img_refs + txt_refs,
        [img.at[pl.ds(k * rows, rows), :] for k in range(images)]
        + [txt.at[pl.ds(k * rows, rows), :] for k in range(texts)],
        sems,
    )
    for copy in copies:
        copy.wait()
    step = tile_rows(texts * rows, 256)

    def one(j, carry):
        at = pl.ds(pl.multiple_of(j * step, step), step)
        dots = lax.dot_general(img[...], txt[at, :], (((1,), (1,)), ((), ())), preferred_element_type=f32)
        pair_ref[:, at] = (2.0 * jax.nn.sigmoid(logit_scale * dots + logit_bias) - p_ref[:, at]).astype(bf16)
        return carry

    lax.fori_loop(0, texts * rows // step, one, 0)
    write_grads(rows, pair_ref, img, txt, img_out, img_grads, txt_out, txt_grads)


def write_grads(rows, pair_ref, img, txt, img_out, img_grads, txt_out, txt_grads):
    for spans, grads, other, axis in ((img_out, img_grads, txt, 1), (txt_out, txt_grads, img, 0)):
        for (first, count), grad in zip(spans, grads):
            size = count * rows
            step = tile_rows(size, 256)
            for k in range(0, size, step):
                at = slice(first * rows + k, first * rows + k + step)
                pair = pair_ref[at, :] if axis == 1 else pair_ref[:, at]
                part = lax.dot_general(pair, other[...], (((axis,), (0,)), ((), ())), preferred_element_type=f32)
                grad[k : k + step, :] = part.astype(grad.dtype)


def grad_shapes(rows, width, spans, dtype):
    return [jax.ShapeDtypeStruct((count * rows, width), dtype) for _, count in spans]


def pair_and_sent(img_blocks, txt_blocks, targets, img_out, txt_out):
    images, texts = len(img_blocks), len(txt_blocks)
    rows, width = img_blocks[0].shape
    shapes = [jax.ShapeDtypeStruct((images * rows, texts * rows), bf16)]
    shapes += grad_shapes(rows, width, img_out, bf16) + grad_shapes(rows, width, txt_out, bf16)
    return pl.pallas_call(
        functools.partial(pair_kernel, images, texts, img_out, txt_out),
        out_shape=shapes,
        in_specs=[ANY] * (images + texts) + [VMEM],
        out_specs=[VMEM] * len(shapes),
        scratch_shapes=[
            pltpu.VMEM((images * rows, width), bf16),
            pltpu.VMEM((texts * rows, width), bf16),
            pltpu.SemaphoreType.DMA((images + texts,)),
        ],
        compiler_params=params(),
        cost_estimate=pl.CostEstimate(
            flops=4 * images * texts * rows * rows * width,
            bytes_accessed=2 * (images + texts) * rows * width + 8 * images * texts * rows * rows,
            transcendentals=images * texts * rows * rows,
        ),
        name="pair_and_sent",
    )(*img_blocks, *txt_blocks, targets)


def kept_kernel(images, texts, img_out, txt_out, *refs):
    img_refs, txt_refs = refs[:images], refs[images : images + texts]
    pair_ref = refs[images + texts]
    rest = refs[images + texts + 1 :]
    img_grads, rest = rest[: len(img_out)], rest[len(img_out) :]
    txt_grads, rest = rest[: len(txt_out)], rest[len(txt_out) :]
    img, txt, sems = rest
    rows = img_refs[0].shape[0]
    copies = load_all(
        img_refs + txt_refs,
        [img.at[pl.ds(k * rows, rows), :] for k in range(images)]
        + [txt.at[pl.ds(k * rows, rows), :] for k in range(texts)],
        sems,
    )
    for copy in copies:
        copy.wait()
    write_grads(rows, pair_ref, img, txt, img_out, img_grads, txt_out, txt_grads)


def kept(img_blocks, txt_blocks, pair, img_out, txt_out):
    images, texts = len(img_blocks), len(txt_blocks)
    rows, width = img_blocks[0].shape
    shapes = grad_shapes(rows, width, img_out, f32) + grad_shapes(rows, width, txt_out, f32)
    return pl.pallas_call(
        functools.partial(kept_kernel, images, texts, img_out, txt_out),
        out_shape=shapes,
        in_specs=[ANY] * (images + texts) + [VMEM],
        out_specs=[VMEM] * len(shapes),
        scratch_shapes=[
            pltpu.VMEM((images * rows, width), bf16),
            pltpu.VMEM((texts * rows, width), bf16),
            pltpu.SemaphoreType.DMA((images + texts,)),
        ],
        compiler_params=params(),
        cost_estimate=pl.CostEstimate(
            flops=2 * images * texts * rows * rows * width,
            bytes_accessed=2 * (images + texts) * rows * width + 8 * images * texts * rows * rows,
            transcendentals=0,
        ),
        name="kept",
    )(*img_blocks, *txt_blocks, pair)


def final_kernel(parts, *refs):
    x_ref, part_refs, out_ref = refs[0], refs[1 : 1 + parts], refs[1 + parts]
    rows = x_ref.shape[0]
    step = tile_rows(rows, 16)

    def one(i, carry):
        at = pl.ds(pl.multiple_of(i * step, step), step)
        x = x_ref[at, :].astype(f32)
        inverse = 1.0 / jnp.sqrt(jnp.sum(x * x, axis=1, keepdims=True) + epsilon)
        unit = x * inverse
        grad = part_refs[0][at, :].astype(f32)
        for part in part_refs[1:]:
            grad = grad + part[at, :].astype(f32)
        grad = logit_scale * grad
        along = jnp.sum(unit * grad, axis=1, keepdims=True)
        out_ref[at, :] = (grad - unit * along) * inverse
        return carry

    lax.fori_loop(0, rows // step, one, 0)


def final(x, parts):
    return pl.pallas_call(
        functools.partial(final_kernel, len(parts)),
        out_shape=jax.ShapeDtypeStruct(x.shape, f32),
        in_specs=[VMEM] * (1 + len(parts)),
        out_specs=VMEM,
        compiler_params=params(16),
        cost_estimate=pl.CostEstimate(flops=10 * x.size, bytes_accessed=12 * x.size, transcendentals=0),
        name="final",
    )(x, *parts)


def gather(plan, block, first, second):
    blocks = {(0, 0): block}
    for a in range(1, plan[first]):
        blocks[0, a] = plan.send(block, first, a)
    for b in range(1, plan[second]):
        for a in range(plan[first]):
            blocks[b, a] = plan.send(blocks[0, a], second, b)
    return blocks


def body(plan, student_img, student_txt, teacher_img, teacher_txt):
    rows, width = student_img.shape
    far, near, core, row, col = (plan[k] for k in plan.order)
    t_img, t_txt = unit_rows(teacher_img, teacher_txt)
    s_img, s_txt = unit_rows(student_img, student_txt)

    def spread(img, txt):
        img_blocks = gather(plan, img, "near", "col")
        txt_blocks = gather(plan, txt, "far", "row")
        imgs = [img_blocks[b, a] for b in range(col) for a in range(near)]
        txts = [txt_blocks[b, a] for b in range(row) for a in range(far)]
        for c in range(1, core):
            txts = txts + [plan.send(txt_blocks[b, a], "core", c) for b in range(row) for a in range(far)]
        return imgs, txts

    t_imgs, t_txts = spread(t_img, t_txt)
    s_imgs, s_txts = spread(s_img, s_txt)
    targets = teacher_targets(t_imgs, t_txts)

    own_img, own_txt = near, row * far
    img_out = tuple((b * near + a, 1) for b in range(1, col) for a in range(near))
    txt_out = tuple((c * own_txt + b * far, far) for c in range(1, core) for b in range(row))
    out = pair_and_sent(s_imgs, s_txts, targets, img_out, txt_out)
    pair = out[0]
    img_sent = {(1 + k // near, k % near): v for k, v in enumerate(out[1 : 1 + len(img_out)])}
    txt_sent = {(1 + k // row, k % row): v for k, v in enumerate(out[1 + len(img_out) :])}

    txt_in = {key: plan.send(v, "core", -key[0]) for key, v in txt_sent.items()}
    img_in = {key: plan.send(v, "col", -key[0]) for key, v in img_sent.items()}

    stay = kept(s_imgs, s_txts, pair, tuple((a, 1) for a in range(near)), tuple((k, 1) for k in range(own_txt)))
    img_part = {a: stay[a] for a in range(near)}
    txt_part = {(b, a): stay[near + b * far + a] for b in range(row) for a in range(far)}

    def img_sum(a):
        total = img_part[a]
        for b in range(1, col):
            total = total + img_in[b, a].astype(f32)
        return total

    img_last = [plan.send(img_sum(a).astype(bf16), "near", -a) for a in range(1, near)]
    image_grad = final(student_img, [img_part[0]] + [img_in[b, 0] for b in range(1, col)] + img_last)

    for c in range(1, core):
        for b in range(row):
            for a in range(far):
                txt_part[b, a] = txt_part[b, a] + txt_in[c, b][a * rows : (a + 1) * rows].astype(f32)
    row_in = {
        (b, a): plan.send(txt_part[b, a].astype(bf16), "row", -b) for b in range(1, row) for a in range(far)
    }

    def txt_sum(a):
        total = txt_part[0, a]
        for b in range(1, row):
            total = total + row_in[b, a].astype(f32)
        return total

    txt_last = [plan.send(txt_sum(a).astype(bf16), "far", -a) for a in range(1, far)]
    text_grad = final(student_txt, [txt_part[0, 0]] + [row_in[b, 0] for b in range(1, row)] + txt_last)
    return image_grad, text_grad


def solution(mesh):
    spec = P(AXES, None)
    return jax.shard_map(
        functools.partial(body, Plan(mesh)), mesh=mesh, in_specs=(spec,) * 4, out_specs=(spec,) * 2, check_vma=False
    )
```

```python
import functools
import math
import jax
import jax.numpy as jnp
from jax import lax
from jax.experimental import pallas as pl
from jax.experimental.pallas import tpu as pltpu
from jax.sharding import PartitionSpec as P

epsilon = 1e-06
logit_scale = 100.0
logit_bias = -4.0

AXES = ("blk", "narrow")
ANY = pl.BlockSpec(memory_space=pl.ANY)
VMEM = pl.BlockSpec(memory_space=pltpu.VMEM)
f32 = jnp.float32
bf16 = jnp.bfloat16


def split_two(size):
    fast = int(size**0.5)
    while size % fast:
        fast -= 1
    return max(fast, size // fast), min(fast, size // fast)


class Plan:
    def __init__(self, mesh):
        blk, narrow = mesh.shape["blk"], mesh.shape["narrow"]
        core = 2 if blk % 2 == 0 else 1
        far, near = split_two(blk // core)
        large, small = split_two(narrow)
        self.digits = {"far": far, "near": near, "core": core, "row": small, "col": large}
        self.order = ["far", "near", "core", "row", "col"]

    def __getitem__(self, name):
        return self.digits[name]

    def place(self, index):
        out = {}
        for name in reversed(self.order):
            out[name] = index % self.digits[name]
            index //= self.digits[name]
        return out

    def index(self, place):
        out = 0
        for name in self.order:
            out = out * self.digits[name] + place[name]
        return out

    def send(self, x, name, by):
        total = 1
        for size in self.digits.values():
            total *= size
        pairs = []
        for src in range(total):
            place = self.place(src)
            place[name] = (place[name] + by) % self.digits[name]
            pairs.append((src, self.index(place)))
        return lax.ppermute(x, AXES, pairs)


def params(*held):
    total = sum(math.prod(shape) * size for shape, size in held)
    return pltpu.CompilerParams(vmem_limit_bytes=int(total) + 8 * 2**20)


def tile_rows(rows, most):
    step = most
    while rows % step:
        step //= 2
    return step


def load_all(refs, targets, sems, columns=None):
    copies = []
    for k, (ref, target) in enumerate(zip(refs, targets)):
        if columns is not None and ref.shape[1] != target.shape[1]:
            ref = ref.at[:, pl.ds(columns, target.shape[1])]
        copies.append(pltpu.make_async_copy(ref, target, sems.at[k]))
        copies[-1].start()
    return copies


def unit_kernel(count, *refs):
    x_refs, out_refs, both_refs = refs[:count], refs[count : 2 * count], refs[2 * count : 2 * count + count // 2]
    held, sems = refs[2 * count + count // 2 : -1], refs[-1]
    copies = load_all(x_refs, held, sems)
    for k, (copy, x_ref, out_ref) in enumerate(zip(copies, held, out_refs)):
        copy.wait()
        x = x_ref[...].astype(f32)
        scale = 1.0 / jnp.sqrt(jnp.sum(x * x, axis=1, keepdims=True) + epsilon)
        unit = (x * scale).astype(bf16)
        out_ref[...] = unit
        both, width = both_refs[k % (count // 2)], x.shape[1]
        if k < count // 2:
            both[:, :width] = unit
        else:
            both[:, both.shape[1] - width :] = unit


def unit_rows(*arrays):
    half = len(arrays) // 2
    both = [(a.shape[0], a.shape[1] + b.shape[1]) for a, b in zip(arrays[:half], arrays[half:])]
    return pl.pallas_call(
        functools.partial(unit_kernel, len(arrays)),
        out_shape=[jax.ShapeDtypeStruct(a.shape, bf16) for a in arrays]
        + [jax.ShapeDtypeStruct(shape, bf16) for shape in both],
        in_specs=[ANY] * len(arrays),
        out_specs=[VMEM] * (len(arrays) + half),
        scratch_shapes=[pltpu.VMEM(a.shape, bf16) for a in arrays]
        + [pltpu.SemaphoreType.DMA((len(arrays),))],
        compiler_params=params(*[(a.shape, 10) for a in arrays]),
        cost_estimate=pl.CostEstimate(
            flops=4 * sum(a.size for a in arrays),
            bytes_accessed=6 * sum(a.size for a in arrays),
            transcendentals=0,
        ),
        name="unit_rows",
    )(*arrays)


def teacher_kernel(images, texts, *refs):
    img_refs, txt_refs = refs[:images], refs[images : images + texts]
    p_ref, img, txt, sems = refs[images + texts :]
    rows = img_refs[0].shape[0]
    copies = load_all(
        img_refs + txt_refs,
        [img.at[pl.ds(k * rows, rows), :] for k in range(images)]
        + [txt.at[pl.ds(k * rows, rows), :] for k in range(texts)],
        sems,
        0,
    )
    for copy in copies:
        copy.wait()
    step = tile_rows(texts * rows, 256)

    def one(j, carry):
        at = pl.ds(pl.multiple_of(j * step, step), step)
        dots = lax.dot_general(img[...], txt[at, :], (((1,), (1,)), ((), ())), preferred_element_type=f32)
        p_ref[:, at] = jax.nn.sigmoid(logit_scale * dots + logit_bias)
        return carry

    lax.fori_loop(0, texts * rows // step, one, 0)
    own = lax.broadcasted_iota(jnp.int32, (rows, rows), 0) == lax.broadcasted_iota(jnp.int32, (rows, rows), 1)
    p_ref[:rows, :rows] = p_ref[:rows, :rows] + jnp.where(own, 1.0, 0.0).astype(f32)


def teacher_targets(img_blocks, txt_blocks):
    images, texts = len(img_blocks), len(txt_blocks)
    rows, width = img_blocks[0].shape
    return pl.pallas_call(
        functools.partial(teacher_kernel, images, texts),
        out_shape=jax.ShapeDtypeStruct((images * rows, texts * rows), f32),
        in_specs=[ANY] * (images + texts),
        out_specs=VMEM,
        scratch_shapes=[
            pltpu.VMEM((images * rows, width), bf16),
            pltpu.VMEM((texts * rows, width), bf16),
            pltpu.SemaphoreType.DMA((images + texts,)),
        ],
        compiler_params=params(((images + texts, rows, width), 2), ((images, rows, texts, rows), 4)),
        cost_estimate=pl.CostEstimate(
            flops=2 * images * texts * rows * rows * width,
            bytes_accessed=2 * (images + texts) * rows * width + 4 * images * texts * rows * rows,
            transcendentals=images * texts * rows * rows,
        ),
        name="teacher_targets",
    )(*img_blocks, *txt_blocks)


def write_grads(rows, pair, other, axis, first, grads):
    size = sum(g.shape[0] for g in grads)
    at = slice(first * rows, first * rows + size)
    part = pair[at, :] if axis == 1 else pair[:, at]
    part = lax.dot_general(part, other[...], (((axis,), (0,)), ((), ())), preferred_element_type=f32)
    done = 0
    for grad in grads:
        grad[...] = part[done : done + grad.shape[0], :].astype(grad.dtype)
        done += grad.shape[0]


def pair_kernel(images, texts, skip, img_first, txt_first, img_count, *refs):
    img_refs, txt_refs = refs[:images], refs[images : images + texts]
    p_ref, pair_ref, img, txt = refs[images + texts : images + texts + 4]
    grads, sems = refs[images + texts + 4 : -1], refs[-1]
    rows = img_refs[0].shape[0]
    copies = load_all(
        img_refs + txt_refs,
        [img.at[pl.ds(k * rows, rows), :] for k in range(images)]
        + [txt.at[pl.ds(k * rows, rows), :] for k in range(texts)],
        sems,
        skip,
    )
    for copy in copies[:images]:
        copy.wait()
    step = tile_rows(texts * rows, 256)
    for j in range(texts * rows // step):
        for copy in copies[images + j * step // rows : images + (j + 1) * step // rows]:
            copy.wait()
        at = slice(j * step, (j + 1) * step)
        dots = lax.dot_general(img[...], txt[at, :], (((1,), (1,)), ((), ())), preferred_element_type=f32)
        pair_ref[:, at] = (2.0 * jax.nn.sigmoid(logit_scale * dots + logit_bias) - p_ref[:, at]).astype(bf16)
    if img_count:
        write_grads(rows, pair_ref, txt, 1, img_first, grads[:img_count])
    if len(grads) > img_count:
        write_grads(rows, pair_ref, img, 0, txt_first, grads[img_count:])


def pair_and_sent(img_blocks, txt_blocks, skip, targets, img_first, img_out, txt_first, txt_out):
    images, texts = len(img_blocks), len(txt_blocks)
    rows, width = img_blocks[0].shape
    shapes = [jax.ShapeDtypeStruct((images * rows, texts * rows), bf16)]
    shapes += [jax.ShapeDtypeStruct((n * rows, width), bf16) for n in (images, texts) + img_out + txt_out]
    return pl.pallas_call(
        functools.partial(pair_kernel, images, texts, skip, img_first, txt_first, len(img_out)),
        out_shape=shapes,
        in_specs=[ANY] * (images + texts) + [VMEM],
        out_specs=[VMEM] * len(shapes),
        scratch_shapes=[pltpu.SemaphoreType.DMA((images + texts,))],
        compiler_params=params(
            ((images * rows, texts * rows), 6),
            ((images + texts, rows, width), 2),
            ((sum(img_out) + sum(txt_out), rows, width), 6),
        ),
        cost_estimate=pl.CostEstimate(
            flops=4 * images * texts * rows * rows * width,
            bytes_accessed=2 * (images + texts) * rows * width + 8 * images * texts * rows * rows,
            transcendentals=images * texts * rows * rows,
        ),
        name="pair_and_sent",
    )(*img_blocks, *txt_blocks, targets)


def grads_kernel(rows, img_first, img_count, txt_first, pair_ref, img, txt, *grads):
    if len(grads) > img_count:
        write_grads(rows, pair_ref, img, 0, txt_first, grads[img_count:])
    if img_count:
        write_grads(rows, pair_ref, txt, 1, img_first, grads[:img_count])


def some_grads(pair, img, txt, rows, img_first, img_out, txt_first, txt_out, dtype, name):
    width = img.shape[1]
    shapes = [jax.ShapeDtypeStruct((n * rows, width), dtype) for n in img_out + txt_out]
    out = pl.pallas_call(
        functools.partial(grads_kernel, rows, img_first, len(img_out), txt_first),
        out_shape=shapes,
        in_specs=[VMEM] * 3,
        out_specs=[VMEM] * len(shapes),
        compiler_params=params(
            (pair.shape, 2), (img.shape, 2), (txt.shape, 2), ((sum(img_out) + sum(txt_out), rows, width), 8)
        ),
        cost_estimate=pl.CostEstimate(
            flops=2 * pair.size * width,
            bytes_accessed=2 * (pair.size + img.size + txt.size) + 4 * len(shapes) * rows * width,
            transcendentals=0,
        ),
        name=name,
    )(pair, img, txt)
    return out[: len(img_out)], out[len(img_out) :]


def final_kernel(parts, *refs):
    x_ref, part_refs, out_ref = refs[0], refs[1 : 1 + parts], refs[1 + parts]
    x = x_ref[...].astype(f32)
    inverse = 1.0 / jnp.sqrt(jnp.sum(x * x, axis=1, keepdims=True) + epsilon)
    unit = x * inverse
    grad = part_refs[0][...].astype(f32)
    for part in part_refs[1:]:
        grad = grad + part[...].astype(f32)
    grad = logit_scale * grad
    along = jnp.sum(unit * grad, axis=1, keepdims=True)
    out_ref[...] = (grad - unit * along) * inverse


def final(x, parts):
    return pl.pallas_call(
        functools.partial(final_kernel, len(parts)),
        out_shape=jax.ShapeDtypeStruct(x.shape, f32),
        in_specs=[VMEM] * (1 + len(parts)),
        out_specs=VMEM,
        compiler_params=params((x.shape, 4 * (4 + len(parts)))),
        cost_estimate=pl.CostEstimate(flops=10 * x.size, bytes_accessed=12 * x.size, transcendentals=0),
        name="final",
    )(x, *parts)


def after(x, *others):
    others = [v for other in others for v in (other.values() if isinstance(other, dict) else [other])]
    return lax.optimization_barrier((x, *others))[0] if others else x


def body(plan, student_img, student_txt, teacher_img, teacher_txt):
    rows, width = student_img.shape
    far, near, core, row, col = (plan[k] for k in plan.order)

    def spread(x, name, *before):
        return {a: plan.send(after(x, *before), name, a) for a in range(1, plan[name])}

    def onward(blocks, name, *before):
        return {
            (b, a): plan.send(after(x, *before), name, b) for b in range(1, plan[name]) for a, x in blocks.items()
        }

    t_img, t_txt, s_img, s_txt, b_img, b_txt = unit_rows(teacher_img, teacher_txt, student_img, student_txt)
    t_far = spread(t_img, "far")
    t_near = spread(t_txt, "near")
    b_col = spread(b_img, "col")
    b_row = spread(b_txt, "row")
    b_core = spread(b_txt, "core")
    first = [t_far, t_near, b_col, b_row, b_core]
    s_far = spread(s_img, "far", *first)
    s_near = spread(s_txt, "near", *first)
    t_far_col = onward(t_far, "col", *first)
    t_near_row = onward(t_near, "row", *first)
    b_row_core = onward(b_row, "core", *first)
    second = [s_far, s_near, t_far_col, t_near_row, b_row_core]
    s_far_col = onward(s_far, "col", *second)
    s_near_row = onward(s_near, "row", *second)
    s_near_core = onward(s_near, "core", *second)
    t_near_core = onward(t_near, "core", *second)
    t_both_core = onward(t_near_row, "core", t_near_core)
    s_both_core = onward(s_near_row, "core", s_near_core)

    def images(own, by_far, by_col, by_both):
        blocks = {(0, 0): own, **by_both}
        blocks.update({(0, a): x for a, x in by_far.items()})
        blocks.update({(b, 0): x for b, x in by_col.items()})
        return [blocks[b, a] for b in range(col) for a in range(far)]

    def texts(own, by_near, by_row, by_both, by_core, by_core_near, by_core_row, by_core_both):
        blocks = {(0, 0, 0): own}
        blocks.update({(0, 0, a): x for a, x in by_near.items()})
        blocks.update({(0, b, 0): x for b, x in by_row.items()})
        blocks.update({(0, *key): x for key, x in by_both.items()})
        blocks.update({(c, 0, 0): x for c, x in by_core.items()})
        blocks.update({(c, 0, a): x for (c, a), x in by_core_near.items()})
        blocks.update({(c, b, 0): x for (c, b), x in by_core_row.items()})
        blocks.update({(c, *key): x for (c, key), x in by_core_both.items()})
        return [blocks[c, b, a] for c in range(core) for b in range(row) for a in range(near)]

    targets = teacher_targets(
        images(t_img, t_far, b_col, t_far_col),
        texts(t_txt, t_near, b_row, t_near_row, b_core, t_near_core, b_row_core, t_both_core),
    )
    s_imgs = images(s_img, s_far, b_col, s_far_col)
    s_txts = texts(s_txt, s_near, b_row, s_near_row, b_core, s_near_core, b_row_core, s_both_core)

    own_txt = row * near
    img_out = (1,) * (far * (col - 1))
    txt_out = (near,) * (row * (core - 1))
    skip = teacher_img.shape[1]
    out = pair_and_sent(s_imgs, s_txts, skip, targets, far, img_out, own_txt, txt_out)
    pair, img_pack, txt_pack = out[:3]
    out = out[3:]
    img_sent = {(1 + k // far, k % far): v for k, v in enumerate(out[: len(img_out)])}
    txt_sent = {(1 + k // row, k % row): v for k, v in enumerate(out[len(img_out) :])}
    img_part, txt_part = some_grads(pair, img_pack, txt_pack, rows, 0, (1,) * far, 0, (1,) * own_txt, f32, "kept")
    txt_part = {divmod(k, near): v for k, v in enumerate(txt_part)}

    img_in = {key: plan.send(v, "col", -key[0]) for key, v in img_sent.items() if key[1]}
    ahead = list(img_in.values())
    img_in.update({key: plan.send(after(v, *ahead), "col", -key[0]) for key, v in img_sent.items() if not key[1]})
    txt_in = {key: plan.send(v, "core", -key[0]) for key, v in txt_sent.items()}

    def img_sum(a):
        total = img_part[a]
        for b in range(1, col):
            total = total + img_in[b, a].astype(f32)
        return total

    img_last = [plan.send(img_sum(a).astype(bf16), "far", -a) for a in range(1, far)]
    image_grad = final(student_img, [img_part[0]] + [img_in[b, 0] for b in range(1, col)] + img_last)

    for c in range(1, core):
        for b in range(row):
            for a in range(near):
                txt_part[b, a] = txt_part[b, a] + txt_in[c, b][a * rows : (a + 1) * rows].astype(f32)
    row_in = {}
    for a in reversed(range(near)):
        ahead = list(row_in.values())
        for b in range(1, row):
            row_in[b, a] = plan.send(after(txt_part[b, a].astype(bf16), *ahead), "row", -b)

    def txt_sum(a):
        total = txt_part[0, a]
        for b in range(1, row):
            total = total + row_in[b, a].astype(f32)
        return total

    txt_last = [plan.send(txt_sum(a).astype(bf16), "near", -a) for a in range(1, near)]
    text_grad = final(student_txt, [txt_part[0, 0]] + [row_in[b, 0] for b in range(1, row)] + txt_last)
    return image_grad, text_grad


def solution(mesh):
    spec = P(AXES, None)
    return jax.shard_map(
        functools.partial(body, Plan(mesh)), mesh=mesh, in_specs=(spec,) * 4, out_specs=(spec,) * 2, check_vma=False
    )
```

```python
import functools
import math
import jax
import jax.numpy as jnp
from jax import lax
from jax.experimental import pallas as pl
from jax.experimental.pallas import tpu as pltpu
from jax.sharding import PartitionSpec as P

epsilon = 1e-06
logit_scale = 100.0
logit_bias = -4.0

AXES = ("blk", "narrow")
ANY = pl.BlockSpec(memory_space=pl.ANY)
VMEM = pl.BlockSpec(memory_space=pltpu.VMEM)
f32 = jnp.float32
bf16 = jnp.bfloat16


def split_two(size):
    fast = int(size**0.5)
    while size % fast:
        fast -= 1
    return max(fast, size // fast), min(fast, size // fast)


class Plan:
    def __init__(self, mesh):
        blk, narrow = mesh.shape["blk"], mesh.shape["narrow"]
        core = 2 if blk % 2 == 0 else 1
        far, near = split_two(blk // core)
        large, small = split_two(narrow)
        self.digits = {"far": far, "near": near, "core": core, "row": small, "col": large}
        self.order = ["far", "near", "core", "row", "col"]

    def __getitem__(self, name):
        return self.digits[name]

    def place(self, index):
        out = {}
        for name in reversed(self.order):
            out[name] = index % self.digits[name]
            index //= self.digits[name]
        return out

    def index(self, place):
        out = 0
        for name in self.order:
            out = out * self.digits[name] + place[name]
        return out

    def send(self, x, name, by):
        total = 1
        for size in self.digits.values():
            total *= size
        pairs = []
        for src in range(total):
            place = self.place(src)
            place[name] = (place[name] + by) % self.digits[name]
            pairs.append((src, self.index(place)))
        return lax.ppermute(x, AXES, pairs)


def params(*held):
    total = sum(math.prod(shape) * size for shape, size in held)
    return pltpu.CompilerParams(vmem_limit_bytes=int(total) + 8 * 2**20)


def tile_rows(rows, most):
    step = most
    while rows % step:
        step //= 2
    return step


def load_all(refs, targets, sems, columns=None):
    copies = []
    for k, (ref, target) in enumerate(zip(refs, targets)):
        if columns is not None and ref.shape[1] != target.shape[1]:
            ref = ref.at[:, pl.ds(columns, target.shape[1])]
        copies.append(pltpu.make_async_copy(ref, target, sems.at[k]))
        copies[-1].start()
    return copies


def unit_kernel(count, *refs):
    x_refs, out_refs, both_refs = refs[:count], refs[count : 2 * count], refs[2 * count : 2 * count + count // 2]
    held, sems = refs[2 * count + count // 2 : -1], refs[-1]
    copies = load_all(x_refs, held, sems)
    for k, (copy, x_ref, out_ref) in enumerate(zip(copies, held, out_refs)):
        copy.wait()
        x = x_ref[...].astype(f32)
        scale = 1.0 / jnp.sqrt(jnp.sum(x * x, axis=1, keepdims=True) + epsilon)
        unit = (x * scale).astype(bf16)
        out_ref[...] = unit
        both, width = both_refs[k % (count // 2)], x.shape[1]
        if k < count // 2:
            both[:, :width] = unit
        else:
            both[:, both.shape[1] - width :] = unit


def unit_rows(*arrays):
    half = len(arrays) // 2
    both = [(a.shape[0], a.shape[1] + b.shape[1]) for a, b in zip(arrays[:half], arrays[half:])]
    return pl.pallas_call(
        functools.partial(unit_kernel, len(arrays)),
        out_shape=[jax.ShapeDtypeStruct(a.shape, bf16) for a in arrays]
        + [jax.ShapeDtypeStruct(shape, bf16) for shape in both],
        in_specs=[pl.BlockSpec(memory_space=pltpu.HBM)] * len(arrays),
        out_specs=[VMEM] * (len(arrays) + half),
        scratch_shapes=[pltpu.VMEM(a.shape, bf16) for a in arrays]
        + [pltpu.SemaphoreType.DMA((len(arrays),))],
        compiler_params=params(*[(a.shape, 10) for a in arrays]),
        cost_estimate=pl.CostEstimate(
            flops=4 * sum(a.size for a in arrays),
            bytes_accessed=6 * sum(a.size for a in arrays),
            transcendentals=0,
        ),
        name="unit_rows",
    )(*arrays)


def teacher_kernel(images, texts, *refs):
    img_refs, txt_refs = refs[:images], refs[images : images + texts]
    p_ref, img, txt, sems = refs[images + texts :]
    rows = img_refs[0].shape[0]
    copies = load_all(
        img_refs + txt_refs,
        [img.at[pl.ds(k * rows, rows), :] for k in range(images)]
        + [txt.at[pl.ds(k * rows, rows), :] for k in range(texts)],
        sems,
        0,
    )
    for copy in copies:
        copy.wait()
    step = tile_rows(texts * rows, 256)

    def one(j, carry):
        at = pl.ds(pl.multiple_of(j * step, step), step)
        dots = lax.dot_general(img[...], txt[at, :], (((1,), (1,)), ((), ())), preferred_element_type=f32)
        p_ref[:, at] = jax.nn.sigmoid(logit_scale * dots + logit_bias)
        return carry

    lax.fori_loop(0, texts * rows // step, one, 0)
    own = lax.broadcasted_iota(jnp.int32, (rows, rows), 0) == lax.broadcasted_iota(jnp.int32, (rows, rows), 1)
    p_ref[:rows, :rows] = p_ref[:rows, :rows] + jnp.where(own, 1.0, 0.0).astype(f32)


def teacher_targets(img_blocks, txt_blocks):
    images, texts = len(img_blocks), len(txt_blocks)
    rows, width = img_blocks[0].shape
    return pl.pallas_call(
        functools.partial(teacher_kernel, images, texts),
        out_shape=jax.ShapeDtypeStruct((images * rows, texts * rows), f32),
        in_specs=[ANY] * (images + texts),
        out_specs=VMEM,
        scratch_shapes=[
            pltpu.VMEM((images * rows, width), bf16),
            pltpu.VMEM((texts * rows, width), bf16),
            pltpu.SemaphoreType.DMA((images + texts,)),
        ],
        compiler_params=params(((images + texts, rows, width), 2), ((images, rows, texts, rows), 4)),
        cost_estimate=pl.CostEstimate(
            flops=2 * images * texts * rows * rows * width,
            bytes_accessed=2 * (images + texts) * rows * width + 4 * images * texts * rows * rows,
            transcendentals=images * texts * rows * rows,
        ),
        name="teacher_targets",
    )(*img_blocks, *txt_blocks)


def write_grads(rows, pair, other, axis, first, grads):
    size = sum(g.shape[0] for g in grads)
    at = slice(first * rows, first * rows + size)
    part = pair[at, :] if axis == 1 else pair[:, at]
    part = lax.dot_general(part, other[...], (((axis,), (0,)), ((), ())), preferred_element_type=f32)
    done = 0
    for grad in grads:
        grad[...] = part[done : done + grad.shape[0], :].astype(grad.dtype)
        done += grad.shape[0]


def pair_kernel(images, texts, skip, img_first, txt_first, img_count, *refs):
    img_refs, txt_refs = refs[:images], refs[images : images + texts]
    p_ref, pair_ref, img, txt = refs[images + texts : images + texts + 4]
    grads, sems = refs[images + texts + 4 : -1], refs[-1]
    rows = img_refs[0].shape[0]
    copies = load_all(
        img_refs + txt_refs,
        [img.at[pl.ds(k * rows, rows), :] for k in range(images)]
        + [txt.at[pl.ds(k * rows, rows), :] for k in range(texts)],
        sems,
        skip,
    )
    for copy in copies[:images]:
        copy.wait()
    step = tile_rows(texts * rows, 256)
    for j in range(texts * rows // step):
        for copy in copies[images + j * step // rows : images + (j + 1) * step // rows]:
            copy.wait()
        at = slice(j * step, (j + 1) * step)
        dots = lax.dot_general(img[...], txt[at, :], (((1,), (1,)), ((), ())), preferred_element_type=f32)
        pair_ref[:, at] = (2.0 * jax.nn.sigmoid(logit_scale * dots + logit_bias) - p_ref[:, at]).astype(bf16)
    if img_count:
        write_grads(rows, pair_ref, txt, 1, img_first, grads[:img_count])
    if len(grads) > img_count:
        write_grads(rows, pair_ref, img, 0, txt_first, grads[img_count:])


def pair_and_sent(img_blocks, txt_blocks, skip, targets, img_first, img_out, txt_first, txt_out):
    images, texts = len(img_blocks), len(txt_blocks)
    rows, width = img_blocks[0].shape
    shapes = [jax.ShapeDtypeStruct((images * rows, texts * rows), bf16)]
    shapes += [jax.ShapeDtypeStruct((n * rows, width), bf16) for n in (images, texts) + img_out + txt_out]
    return pl.pallas_call(
        functools.partial(pair_kernel, images, texts, skip, img_first, txt_first, len(img_out)),
        out_shape=shapes,
        in_specs=[ANY] * (images + texts) + [VMEM],
        out_specs=[VMEM] * len(shapes),
        scratch_shapes=[pltpu.SemaphoreType.DMA((images + texts,))],
        compiler_params=params(
            ((images * rows, texts * rows), 6),
            ((images + texts, rows, width), 2),
            ((sum(img_out) + sum(txt_out), rows, width), 6),
        ),
        cost_estimate=pl.CostEstimate(
            flops=4 * images * texts * rows * rows * width,
            bytes_accessed=2 * (images + texts) * rows * width + 8 * images * texts * rows * rows,
            transcendentals=images * texts * rows * rows,
        ),
        name="pair_and_sent",
    )(*img_blocks, *txt_blocks, targets)


def grads_kernel(rows, img_first, img_count, txt_first, pair_ref, img, txt, *grads):
    if len(grads) > img_count:
        write_grads(rows, pair_ref, img, 0, txt_first, grads[img_count:])
    if img_count:
        write_grads(rows, pair_ref, txt, 1, img_first, grads[:img_count])


def some_grads(pair, img, txt, rows, img_first, img_out, txt_first, txt_out, dtype, name):
    width = img.shape[1]
    shapes = [jax.ShapeDtypeStruct((n * rows, width), dtype) for n in img_out + txt_out]
    out = pl.pallas_call(
        functools.partial(grads_kernel, rows, img_first, len(img_out), txt_first),
        out_shape=shapes,
        in_specs=[VMEM] * 3,
        out_specs=[VMEM] * len(shapes),
        compiler_params=params(
            (pair.shape, 2), (img.shape, 2), (txt.shape, 2), ((sum(img_out) + sum(txt_out), rows, width), 8)
        ),
        cost_estimate=pl.CostEstimate(
            flops=2 * pair.size * width,
            bytes_accessed=2 * (pair.size + img.size + txt.size) + 4 * len(shapes) * rows * width,
            transcendentals=0,
        ),
        name=name,
    )(pair, img, txt)
    return out[: len(img_out)], out[len(img_out) :]


def final_kernel(parts, *refs):
    x_ref, part_refs, out_ref = refs[0], refs[1 : 1 + parts], refs[1 + parts]
    x = x_ref[...].astype(f32)
    inverse = 1.0 / jnp.sqrt(jnp.sum(x * x, axis=1, keepdims=True) + epsilon)
    unit = x * inverse
    grad = part_refs[0][...].astype(f32)
    for part in part_refs[1:]:
        grad = grad + part[...].astype(f32)
    grad = logit_scale * grad
    along = jnp.sum(unit * grad, axis=1, keepdims=True)
    out_ref[...] = (grad - unit * along) * inverse


def final(x, parts):
    return pl.pallas_call(
        functools.partial(final_kernel, len(parts)),
        out_shape=jax.ShapeDtypeStruct(x.shape, f32),
        in_specs=[VMEM] * (1 + len(parts)),
        out_specs=VMEM,
        compiler_params=params((x.shape, 4 * (4 + len(parts)))),
        cost_estimate=pl.CostEstimate(flops=10 * x.size, bytes_accessed=12 * x.size, transcendentals=0),
        name="final",
    )(x, *parts)


def after(x, *others):
    others = [v for other in others for v in (other.values() if isinstance(other, dict) else [other])]
    return lax.optimization_barrier((x, *others))[0] if others else x


def body(plan, student_img, student_txt, teacher_img, teacher_txt):
    rows, width = student_img.shape
    far, near, core, row, col = (plan[k] for k in plan.order)

    def spread(x, name, *before):
        return {a: plan.send(after(x, *before), name, a) for a in range(1, plan[name])}

    def onward(blocks, name, *before):
        return {
            (b, a): plan.send(after(x, *before), name, b) for b in range(1, plan[name]) for a, x in blocks.items()
        }

    t_img, t_txt, s_img, s_txt, b_img, b_txt = unit_rows(teacher_img, teacher_txt, student_img, student_txt)
    t_far = spread(t_img, "far")
    t_near = spread(t_txt, "near")
    b_col = spread(b_img, "col")
    b_row = spread(b_txt, "row")
    b_core = spread(b_txt, "core")
    first = [t_far, t_near, b_col, b_row, b_core]
    s_far = spread(s_img, "far", *first)
    s_near = spread(s_txt, "near", *first)
    t_far_col = onward(t_far, "col", *first)
    t_near_row = onward(t_near, "row", *first)
    b_row_core = onward(b_row, "core", *first)
    second = [s_far, s_near, t_far_col, t_near_row, b_row_core]
    s_far_col = onward(s_far, "col", *second)
    s_near_row = onward(s_near, "row", *second)
    s_near_core = onward(s_near, "core", *second)
    t_near_core = onward(t_near, "core", *second)
    t_both_core = onward(t_near_row, "core", t_near_core)

    def images(own, by_far, by_col, by_both):
        blocks = {(0, 0): own, **by_both}
        blocks.update({(0, a): x for a, x in by_far.items()})
        blocks.update({(b, 0): x for b, x in by_col.items()})
        return [blocks[b, a] for b in range(col) for a in range(far)]

    def texts(own, by_near, by_row, by_both, by_core, by_core_near, by_core_row, by_core_both):
        blocks = {(0, 0, 0): own}
        blocks.update({(0, 0, a): x for a, x in by_near.items()})
        blocks.update({(0, b, 0): x for b, x in by_row.items()})
        blocks.update({(0, *key): x for key, x in by_both.items()})
        blocks.update({(c, 0, 0): x for c, x in by_core.items()})
        blocks.update({(c, 0, a): x for (c, a), x in by_core_near.items()})
        blocks.update({(c, b, 0): x for (c, b), x in by_core_row.items()})
        blocks.update({(c, *key): x for (c, key), x in by_core_both.items()})
        return [blocks[c, b, a] for c in range(core) for b in range(row) for a in range(near)]

    targets = teacher_targets(
        images(t_img, t_far, b_col, t_far_col),
        texts(t_txt, t_near, b_row, t_near_row, b_core, t_near_core, b_row_core, t_both_core),
    )
    s_both_core = onward(s_near_row, "core", s_near_core, targets)
    s_imgs = images(s_img, s_far, b_col, s_far_col)
    s_txts = texts(s_txt, s_near, b_row, s_near_row, b_core, s_near_core, b_row_core, s_both_core)

    own_txt = row * near
    img_out = (1,) * (far * (col - 1))
    txt_out = (near,) * (row * (core - 1))
    skip = teacher_img.shape[1]
    out = pair_and_sent(s_imgs, s_txts, skip, targets, far, img_out, own_txt, txt_out)
    pair, img_pack, txt_pack = out[:3]
    out = out[3:]
    img_sent = {(1 + k // far, k % far): v for k, v in enumerate(out[: len(img_out)])}
    txt_sent = {(1 + k // row, k % row): v for k, v in enumerate(out[len(img_out) :])}
    img_part, txt_part = some_grads(pair, img_pack, txt_pack, rows, 0, (1,) * far, 0, (1,) * own_txt, f32, "kept")
    txt_part = {divmod(k, near): v for k, v in enumerate(txt_part)}

    img_in = {key: plan.send(v, "col", -key[0]) for key, v in img_sent.items() if key[1]}
    txt_in = {key: plan.send(v, "core", -key[0]) for key, v in txt_sent.items()}

    for c in range(1, core):
        for b in range(row):
            for a in range(near):
                txt_part[b, a] = txt_part[b, a] + txt_in[c, b][a * rows : (a + 1) * rows].astype(f32)
    row_in = {}
    for b in range(1, row):
        for a in range(1, near):
            row_in[b, a] = plan.send(txt_part[b, a].astype(bf16), "row", -b)
    ahead = list(row_in.values())
    for b in range(1, row):
        row_in[b, 0] = plan.send(after(txt_part[b, 0].astype(bf16), *ahead), "row", -b)
    for b in range(1, col):
        img_in[b, 0] = plan.send(after(img_sent[b, 0], *ahead), "col", -b)

    def img_sum(a):
        total = img_part[a]
        for b in range(1, col):
            total = total + img_in[b, a].astype(f32)
        return total

    img_last = [plan.send(img_sum(a).astype(bf16), "far", -a) for a in range(1, far)]
    image_grad = final(student_img, [img_part[0]] + [img_in[b, 0] for b in range(1, col)] + img_last)

    def txt_sum(a):
        total = txt_part[0, a]
        for b in range(1, row):
            total = total + row_in[b, a].astype(f32)
        return total

    txt_last = [plan.send(txt_sum(a).astype(bf16), "near", -a) for a in range(1, near)]
    text_grad = final(student_txt, [txt_part[0, 0]] + [row_in[b, 0] for b in range(1, row)] + txt_last)
    return image_grad, text_grad


def solution(mesh):
    spec = P(AXES, None)
    return jax.shard_map(
        functools.partial(body, Plan(mesh)), mesh=mesh, in_specs=(spec,) * 4, out_specs=(spec,) * 2, check_vma=False
    )
```

```python
import functools
import math
import jax
import jax.numpy as jnp
from jax import lax
from jax.experimental import pallas as pl
from jax.experimental.pallas import tpu as pltpu
from jax.sharding import PartitionSpec as P

epsilon = 1e-06
logit_scale = 100.0
logit_bias = -4.0

AXES = ("blk", "narrow")
ANY = pl.BlockSpec(memory_space=pl.ANY)
VMEM = pl.BlockSpec(memory_space=pltpu.VMEM)
f32 = jnp.float32
bf16 = jnp.bfloat16


def split_two(size):
    fast = int(size**0.5)
    while size % fast:
        fast -= 1
    return max(fast, size // fast), min(fast, size // fast)


class Plan:
    def __init__(self, mesh):
        blk, narrow = mesh.shape["blk"], mesh.shape["narrow"]
        core = 2 if blk % 2 == 0 else 1
        far, near = split_two(blk // core)
        large, small = split_two(narrow)
        self.digits = {"far": far, "near": near, "core": core, "row": small, "col": large}
        self.order = ["far", "near", "core", "row", "col"]

    def __getitem__(self, name):
        return self.digits[name]

    def place(self, index):
        out = {}
        for name in reversed(self.order):
            out[name] = index % self.digits[name]
            index //= self.digits[name]
        return out

    def index(self, place):
        out = 0
        for name in self.order:
            out = out * self.digits[name] + place[name]
        return out

    def send(self, x, name, by):
        total = 1
        for size in self.digits.values():
            total *= size
        pairs = []
        for src in range(total):
            place = self.place(src)
            place[name] = (place[name] + by) % self.digits[name]
            pairs.append((src, self.index(place)))
        return lax.ppermute(x, AXES, pairs)


def params(*held):
    total = sum(math.prod(shape) * size for shape, size in held)
    return pltpu.CompilerParams(vmem_limit_bytes=int(total) + 8 * 2**20)


def tile_rows(rows, most):
    step = most
    while rows % step:
        step //= 2
    return step


def load_all(refs, targets, sems, columns=None):
    copies = []
    for k, (ref, target) in enumerate(zip(refs, targets)):
        if columns is not None and ref.shape[1] != target.shape[1]:
            ref = ref.at[:, pl.ds(columns, target.shape[1])]
        copies.append(pltpu.make_async_copy(ref, target, sems.at[k]))
        copies[-1].start()
    return copies


def unit_kernel(count, *refs):
    x_refs, out_refs, both_refs = refs[:count], refs[count : 2 * count], refs[2 * count : 2 * count + count // 2]
    held, sems = refs[2 * count + count // 2 : -1], refs[-1]
    copies = load_all(x_refs, held, sems)
    for k, (copy, x_ref, out_ref) in enumerate(zip(copies, held, out_refs)):
        copy.wait()
        x = x_ref[...].astype(f32)
        scale = 1.0 / jnp.sqrt(jnp.sum(x * x, axis=1, keepdims=True) + epsilon)
        unit = (x * scale).astype(bf16)
        out_ref[...] = unit
        both, width = both_refs[k % (count // 2)], x.shape[1]
        if k < count // 2:
            both[:, :width] = unit
        else:
            both[:, both.shape[1] - width :] = unit


def unit_rows(*arrays):
    half = len(arrays) // 2
    both = [(a.shape[0], a.shape[1] + b.shape[1]) for a, b in zip(arrays[:half], arrays[half:])]
    return pl.pallas_call(
        functools.partial(unit_kernel, len(arrays)),
        out_shape=[jax.ShapeDtypeStruct(a.shape, bf16) for a in arrays]
        + [jax.ShapeDtypeStruct(shape, bf16) for shape in both],
        in_specs=[ANY] * len(arrays),
        out_specs=[VMEM] * (len(arrays) + half),
        scratch_shapes=[pltpu.VMEM(a.shape, bf16) for a in arrays]
        + [pltpu.SemaphoreType.DMA((len(arrays),))],
        compiler_params=pltpu.CompilerParams(vmem_limit_bytes=60 * 2**20),
        cost_estimate=pl.CostEstimate(
            flops=4 * sum(a.size for a in arrays),
            bytes_accessed=6 * sum(a.size for a in arrays),
            transcendentals=0,
        ),
        name="unit_rows",
    )(*arrays)


def teacher_kernel(images, texts, *refs):
    img_refs, txt_refs = refs[:images], refs[images : images + texts]
    p_ref, img, txt, sems = refs[images + texts :]
    rows = img_refs[0].shape[0]
    copies = load_all(
        img_refs + txt_refs,
        [img.at[pl.ds(k * rows, rows), :] for k in range(images)]
        + [txt.at[pl.ds(k * rows, rows), :] for k in range(texts)],
        sems,
        0,
    )
    for copy in copies:
        copy.wait()
    step = tile_rows(texts * rows, 256)

    def one(j, carry):
        at = pl.ds(pl.multiple_of(j * step, step), step)
        dots = lax.dot_general(img[...], txt[at, :], (((1,), (1,)), ((), ())), preferred_element_type=f32)
        p_ref[:, at] = jax.nn.sigmoid(logit_scale * dots + logit_bias)
        return carry

    lax.fori_loop(0, texts * rows // step, one, 0)
    own = lax.broadcasted_iota(jnp.int32, (rows, rows), 0) == lax.broadcasted_iota(jnp.int32, (rows, rows), 1)
    p_ref[:rows, :rows] = p_ref[:rows, :rows] + jnp.where(own, 1.0, 0.0).astype(f32)


def teacher_targets(img_blocks, txt_blocks):
    images, texts = len(img_blocks), len(txt_blocks)
    rows, width = img_blocks[0].shape
    return pl.pallas_call(
        functools.partial(teacher_kernel, images, texts),
        out_shape=jax.ShapeDtypeStruct((images * rows, texts * rows), f32),
        in_specs=[ANY] * (images + texts),
        out_specs=VMEM,
        scratch_shapes=[
            pltpu.VMEM((images * rows, width), bf16),
            pltpu.VMEM((texts * rows, width), bf16),
            pltpu.SemaphoreType.DMA((images + texts,)),
        ],
        compiler_params=params(((images + texts, rows, width), 2), ((images, rows, texts, rows), 4)),
        cost_estimate=pl.CostEstimate(
            flops=2 * images * texts * rows * rows * width,
            bytes_accessed=2 * (images + texts) * rows * width + 4 * images * texts * rows * rows,
            transcendentals=images * texts * rows * rows,
        ),
        name="teacher_targets",
    )(*img_blocks, *txt_blocks)


def write_grads(rows, pair, other, axis, first, grads):
    size = sum(g.shape[0] for g in grads)
    at = slice(first * rows, first * rows + size)
    part = pair[at, :] if axis == 1 else pair[:, at]
    part = lax.dot_general(part, other[...], (((axis,), (0,)), ((), ())), preferred_element_type=f32)
    done = 0
    for grad in grads:
        grad[...] = part[done : done + grad.shape[0], :].astype(grad.dtype)
        done += grad.shape[0]


def pair_kernel(images, texts, skip, img_first, txt_first, img_count, *refs):
    img_refs, txt_refs = refs[:images], refs[images : images + texts]
    p_ref, pair_ref, img, txt = refs[images + texts : images + texts + 4]
    grads, sems = refs[images + texts + 4 : -1], refs[-1]
    rows = img_refs[0].shape[0]
    copies = load_all(
        img_refs + txt_refs,
        [img.at[pl.ds(k * rows, rows), :] for k in range(images)]
        + [txt.at[pl.ds(k * rows, rows), :] for k in range(texts)],
        sems,
        skip,
    )
    for copy in copies[:images]:
        copy.wait()
    step = tile_rows(texts * rows, 256)
    for j in range(texts * rows // step):
        for copy in copies[images + j * step // rows : images + (j + 1) * step // rows]:
            copy.wait()
        at = slice(j * step, (j + 1) * step)
        dots = lax.dot_general(img[...], txt[at, :], (((1,), (1,)), ((), ())), preferred_element_type=f32)
        pair_ref[:, at] = (2.0 * jax.nn.sigmoid(logit_scale * dots + logit_bias) - p_ref[:, at]).astype(bf16)
    if img_count:
        write_grads(rows, pair_ref, txt, 1, img_first, grads[:img_count])
    if len(grads) > img_count:
        write_grads(rows, pair_ref, img, 0, txt_first, grads[img_count:])


def pair_and_sent(img_blocks, txt_blocks, skip, targets, img_first, img_out, txt_first, txt_out):
    images, texts = len(img_blocks), len(txt_blocks)
    rows, width = img_blocks[0].shape
    shapes = [jax.ShapeDtypeStruct((images * rows, texts * rows), bf16)]
    shapes += [jax.ShapeDtypeStruct((n * rows, width), bf16) for n in (images, texts) + img_out + txt_out]
    return pl.pallas_call(
        functools.partial(pair_kernel, images, texts, skip, img_first, txt_first, len(img_out)),
        out_shape=shapes,
        in_specs=[ANY] * (images + texts) + [VMEM],
        out_specs=[VMEM] * len(shapes),
        scratch_shapes=[pltpu.SemaphoreType.DMA((images + texts,))],
        compiler_params=params(
            ((images * rows, texts * rows), 6),
            ((images + texts, rows, width), 2),
            ((sum(img_out) + sum(txt_out), rows, width), 6),
        ),
        cost_estimate=pl.CostEstimate(
            flops=4 * images * texts * rows * rows * width,
            bytes_accessed=2 * (images + texts) * rows * width + 8 * images * texts * rows * rows,
            transcendentals=images * texts * rows * rows,
        ),
        name="pair_and_sent",
    )(*img_blocks, *txt_blocks, targets)


def grads_kernel(rows, img_first, img_count, txt_first, pair_ref, img, txt, *grads):
    if len(grads) > img_count:
        write_grads(rows, pair_ref, img, 0, txt_first, grads[img_count:])
    if img_count:
        write_grads(rows, pair_ref, txt, 1, img_first, grads[:img_count])


def some_grads(pair, img, txt, rows, img_first, img_out, txt_first, txt_out, dtype, name):
    width = img.shape[1]
    shapes = [jax.ShapeDtypeStruct((n * rows, width), dtype) for n in img_out + txt_out]
    out = pl.pallas_call(
        functools.partial(grads_kernel, rows, img_first, len(img_out), txt_first),
        out_shape=shapes,
        in_specs=[VMEM] * 3,
        out_specs=[VMEM] * len(shapes),
        compiler_params=params(
            (pair.shape, 2), (img.shape, 2), (txt.shape, 2), ((sum(img_out) + sum(txt_out), rows, width), 8)
        ),
        cost_estimate=pl.CostEstimate(
            flops=2 * pair.size * width,
            bytes_accessed=2 * (pair.size + img.size + txt.size) + 4 * len(shapes) * rows * width,
            transcendentals=0,
        ),
        name=name,
    )(pair, img, txt)
    return out[: len(img_out)], out[len(img_out) :]


def final_kernel(parts, *refs):
    x_ref, part_refs, out_ref = refs[0], refs[1 : 1 + parts], refs[1 + parts]
    x = x_ref[...].astype(f32)
    inverse = 1.0 / jnp.sqrt(jnp.sum(x * x, axis=1, keepdims=True) + epsilon)
    unit = x * inverse
    grad = part_refs[0][...].astype(f32)
    for part in part_refs[1:]:
        grad = grad + part[...].astype(f32)
    grad = logit_scale * grad
    along = jnp.sum(unit * grad, axis=1, keepdims=True)
    out_ref[...] = (grad - unit * along) * inverse


def final(x, parts):
    return pl.pallas_call(
        functools.partial(final_kernel, len(parts)),
        out_shape=jax.ShapeDtypeStruct(x.shape, f32),
        in_specs=[VMEM] * (1 + len(parts)),
        out_specs=VMEM,
        compiler_params=params((x.shape, 4 * (4 + len(parts)))),
        cost_estimate=pl.CostEstimate(flops=10 * x.size, bytes_accessed=12 * x.size, transcendentals=0),
        name="final",
    )(x, *parts)


def token_kernel(*refs):
    refs[-1][...] = jnp.zeros_like(refs[-1])


def token(*arrays, flops):
    return pl.pallas_call(
        token_kernel,
        out_shape=jax.ShapeDtypeStruct((8, 128), f32),
        in_specs=[ANY] * len(arrays),
        out_specs=VMEM,
        cost_estimate=pl.CostEstimate(flops=flops, bytes_accessed=0, transcendentals=0),
        name="token",
    )(*arrays)


def after(x, *others):
    others = [v for other in others for v in (other.values() if isinstance(other, dict) else [other])]
    return lax.optimization_barrier((x, *others))[0] if others else x


def body(plan, student_img, student_txt, teacher_img, teacher_txt):
    rows, width = student_img.shape
    far, near, core, row, col = (plan[k] for k in plan.order)

    def spread(x, name, *before):
        return {a: plan.send(after(x, *before), name, a) for a in range(1, plan[name])}

    def onward(blocks, name, *before):
        return {
            (b, a): plan.send(after(x, *before), name, b) for b in range(1, plan[name]) for a, x in blocks.items()
        }

    t_img, t_txt, s_img, s_txt, b_img, b_txt = unit_rows(teacher_img, teacher_txt, student_img, student_txt)
    t_far = spread(t_img, "far")
    t_near = spread(t_txt, "near")
    b_col = spread(b_img, "col")
    b_row = spread(b_txt, "row")
    b_core = spread(b_txt, "core")
    first = [token(*t_far.values(), *t_near.values(), flops=10000000000), b_col, b_row, b_core]
    s_far = spread(s_img, "far", *first)
    s_near = spread(s_txt, "near", *first)
    t_far_col = onward(t_far, "col", *first)
    t_near_row = onward(t_near, "row", *first)
    b_row_core = onward(b_row, "core", *first)
    second = [token(*s_far.values(), *s_near.values(), flops=10000000000), t_far_col, t_near_row, b_row_core]
    s_far_col = onward(s_far, "col", *second)
    s_near_row = onward(s_near, "row", *second)
    s_near_core = onward(s_near, "core", *second)
    t_near_core = onward(t_near, "core", *second)
    t_both_core = onward(t_near_row, "core", *second)

    def images(own, by_far, by_col, by_both):
        blocks = {(0, 0): own, **by_both}
        blocks.update({(0, a): x for a, x in by_far.items()})
        blocks.update({(b, 0): x for b, x in by_col.items()})
        return [blocks[b, a] for b in range(col) for a in range(far)]

    def texts(own, by_near, by_row, by_both, by_core, by_core_near, by_core_row, by_core_both):
        blocks = {(0, 0, 0): own}
        blocks.update({(0, 0, a): x for a, x in by_near.items()})
        blocks.update({(0, b, 0): x for b, x in by_row.items()})
        blocks.update({(0, *key): x for key, x in by_both.items()})
        blocks.update({(c, 0, 0): x for c, x in by_core.items()})
        blocks.update({(c, 0, a): x for (c, a), x in by_core_near.items()})
        blocks.update({(c, b, 0): x for (c, b), x in by_core_row.items()})
        blocks.update({(c, *key): x for (c, key), x in by_core_both.items()})
        return [blocks[c, b, a] for c in range(core) for b in range(row) for a in range(near)]

    targets = teacher_targets(
        images(t_img, t_far, b_col, t_far_col),
        texts(t_txt, t_near, b_row, t_near_row, b_core, t_near_core, b_row_core, t_both_core),
    )
    s_both_core = onward(s_near_row, "core", s_near_core, targets)
    s_imgs = images(s_img, s_far, b_col, s_far_col)
    s_txts = texts(s_txt, s_near, b_row, s_near_row, b_core, s_near_core, b_row_core, s_both_core)

    own_txt = row * near
    img_out = (1,) * (far * (col - 1))
    txt_out = (near,) * (row * (core - 1))
    skip = teacher_img.shape[1]
    out = pair_and_sent(s_imgs, s_txts, skip, targets, far, img_out, own_txt, txt_out)
    pair, img_pack, txt_pack = out[:3]
    out = out[3:]
    img_sent = {(1 + k // far, k % far): v for k, v in enumerate(out[: len(img_out)])}
    txt_sent = {(1 + k // row, k % row): v for k, v in enumerate(out[len(img_out) :])}
    img_part, txt_part = some_grads(pair, img_pack, txt_pack, rows, 0, (1,) * far, 0, (1,) * own_txt, f32, "kept")
    txt_part = {divmod(k, near): v for k, v in enumerate(txt_part)}

    img_in = {key: plan.send(v, "col", -key[0]) for key, v in img_sent.items() if key[1]}
    txt_in = {key: plan.send(v, "core", -key[0]) for key, v in txt_sent.items()}

    for c in range(1, core):
        for b in range(row):
            for a in range(near):
                txt_part[b, a] = txt_part[b, a] + txt_in[c, b][a * rows : (a + 1) * rows].astype(f32)
    row_in = {}
    for b in range(1, row):
        for a in range(1, near):
            row_in[b, a] = plan.send(txt_part[b, a].astype(bf16), "row", -b)
    ahead = list(row_in.values())
    for b in range(1, row):
        row_in[b, 0] = plan.send(after(txt_part[b, 0].astype(bf16), *ahead), "row", -b)
    for b in range(1, col):
        img_in[b, 0] = plan.send(after(img_sent[b, 0], *ahead), "col", -b)

    def img_sum(a):
        total = img_part[a]
        for b in range(1, col):
            total = total + img_in[b, a].astype(f32)
        return total

    img_last = [plan.send(img_sum(a).astype(bf16), "far", -a) for a in range(1, far)]
    image_grad = final(student_img, [img_part[0]] + [img_in[b, 0] for b in range(1, col)] + img_last)

    def txt_sum(a):
        total = txt_part[0, a]
        for b in range(1, row):
            total = total + row_in[b, a].astype(f32)
        return total

    txt_last = [plan.send(txt_sum(a).astype(bf16), "near", -a) for a in range(1, near)]
    text_grad = final(student_txt, [txt_part[0, 0]] + [row_in[b, 0] for b in range(1, row)] + txt_last)
    return image_grad, text_grad


def solution(mesh):
    spec = P(AXES, None)
    return jax.shard_map(
        functools.partial(body, Plan(mesh)), mesh=mesh, in_specs=(spec,) * 4, out_specs=(spec,) * 2, check_vma=False
    )
```

```python
import functools
import math
import jax
import jax.numpy as jnp
from jax import lax
from jax.experimental import pallas as pl
from jax.experimental.pallas import tpu as pltpu
from jax.sharding import PartitionSpec as P

epsilon = 1e-06
logit_scale = 100.0
logit_bias = -4.0

AXES = ("blk", "narrow")
ANY = pl.BlockSpec(memory_space=pl.ANY)
VMEM = pl.BlockSpec(memory_space=pltpu.VMEM)
f32 = jnp.float32
bf16 = jnp.bfloat16


def split_two(size):
    fast = int(size**0.5)
    while size % fast:
        fast -= 1
    return max(fast, size // fast), min(fast, size // fast)


class Plan:
    def __init__(self, mesh):
        blk, narrow = mesh.shape["blk"], mesh.shape["narrow"]
        core = 2 if blk % 2 == 0 else 1
        far, near = split_two(blk // core)
        large, small = split_two(narrow)
        self.digits = {"far": far, "near": near, "core": core, "row": small, "col": large}
        self.order = ["far", "near", "core", "row", "col"]

    def __getitem__(self, name):
        return self.digits[name]

    def place(self, index):
        out = {}
        for name in reversed(self.order):
            out[name] = index % self.digits[name]
            index //= self.digits[name]
        return out

    def index(self, place):
        out = 0
        for name in self.order:
            out = out * self.digits[name] + place[name]
        return out

    def send(self, x, name, by):
        total = 1
        for size in self.digits.values():
            total *= size
        pairs = []
        for src in range(total):
            place = self.place(src)
            place[name] = (place[name] + by) % self.digits[name]
            pairs.append((src, self.index(place)))
        return lax.ppermute(x, AXES, pairs)


def params(*held):
    total = sum(math.prod(shape) * size for shape, size in held)
    return pltpu.CompilerParams(vmem_limit_bytes=int(total) + 8 * 2**20)


def tile_rows(rows, most):
    step = most
    while rows % step:
        step //= 2
    return step


def load_all(refs, targets, sems, columns=None):
    copies = []
    for k, (ref, target) in enumerate(zip(refs, targets)):
        if columns is not None and ref.shape[1] != target.shape[1]:
            ref = ref.at[:, pl.ds(columns, target.shape[1])]
        copies.append(pltpu.make_async_copy(ref, target, sems.at[k]))
        copies[-1].start()
    return copies


def unit_kernel(count, *refs):
    x_refs, out_refs, both_refs = refs[:count], refs[count : 2 * count], refs[2 * count : 2 * count + count // 2]
    held, sems = refs[2 * count + count // 2 : -1], refs[-1]
    copies = load_all(x_refs, held, sems)
    for k, (copy, x_ref, out_ref) in enumerate(zip(copies, held, out_refs)):
        copy.wait()
        x = x_ref[...].astype(f32)
        scale = 1.0 / jnp.sqrt(jnp.sum(x * x, axis=1, keepdims=True) + epsilon)
        unit = (x * scale).astype(bf16)
        out_ref[...] = unit
        both, width = both_refs[k % (count // 2)], x.shape[1]
        if k < count // 2:
            both[:, :width] = unit
        else:
            both[:, both.shape[1] - width :] = unit


def unit_rows(*arrays):
    half = len(arrays) // 2
    both = [(a.shape[0], a.shape[1] + b.shape[1]) for a, b in zip(arrays[:half], arrays[half:])]
    return pl.pallas_call(
        functools.partial(unit_kernel, len(arrays)),
        out_shape=[jax.ShapeDtypeStruct(a.shape, bf16) for a in arrays]
        + [jax.ShapeDtypeStruct(shape, bf16) for shape in both],
        in_specs=[ANY] * len(arrays),
        out_specs=[VMEM] * (len(arrays) + half),
        scratch_shapes=[pltpu.VMEM(a.shape, bf16) for a in arrays]
        + [pltpu.SemaphoreType.DMA((len(arrays),))],
        compiler_params=pltpu.CompilerParams(vmem_limit_bytes=60 * 2**20),
        cost_estimate=pl.CostEstimate(
            flops=4 * sum(a.size for a in arrays),
            bytes_accessed=6 * sum(a.size for a in arrays),
            transcendentals=0,
        ),
        name="unit_rows",
    )(*arrays)


def teacher_kernel(images, texts, *refs):
    img_refs, txt_refs = refs[:images], refs[images : images + texts]
    p_ref, img, txt, sems = refs[images + texts :]
    rows = img_refs[0].shape[0]
    copies = load_all(
        img_refs + txt_refs,
        [img.at[pl.ds(k * rows, rows), :] for k in range(images)]
        + [txt.at[pl.ds(k * rows, rows), :] for k in range(texts)],
        sems,
        0,
    )
    for copy in copies:
        copy.wait()
    step = tile_rows(texts * rows, 256)

    def one(j, carry):
        at = pl.ds(pl.multiple_of(j * step, step), step)
        dots = lax.dot_general(img[...], txt[at, :], (((1,), (1,)), ((), ())), preferred_element_type=f32)
        p_ref[:, at] = jax.nn.sigmoid(logit_scale * dots + logit_bias)
        return carry

    lax.fori_loop(0, texts * rows // step, one, 0)
    own = lax.broadcasted_iota(jnp.int32, (rows, rows), 0) == lax.broadcasted_iota(jnp.int32, (rows, rows), 1)
    p_ref[:rows, :rows] = p_ref[:rows, :rows] + jnp.where(own, 1.0, 0.0).astype(f32)


def teacher_targets(img_blocks, txt_blocks):
    images, texts = len(img_blocks), len(txt_blocks)
    rows, width = img_blocks[0].shape
    return pl.pallas_call(
        functools.partial(teacher_kernel, images, texts),
        out_shape=jax.ShapeDtypeStruct((images * rows, texts * rows), f32),
        in_specs=[ANY] * (images + texts),
        out_specs=VMEM,
        scratch_shapes=[
            pltpu.VMEM((images * rows, width), bf16),
            pltpu.VMEM((texts * rows, width), bf16),
            pltpu.SemaphoreType.DMA((images + texts,)),
        ],
        compiler_params=params(((images + texts, rows, width), 2), ((images, rows, texts, rows), 4)),
        cost_estimate=pl.CostEstimate(
            flops=2 * images * texts * rows * rows * width,
            bytes_accessed=2 * (images + texts) * rows * width + 4 * images * texts * rows * rows,
            transcendentals=images * texts * rows * rows,
        ),
        name="teacher_targets",
    )(*img_blocks, *txt_blocks)


def write_grads(rows, pair, other, axis, first, grads):
    size = sum(g.shape[0] for g in grads)
    at = slice(first * rows, first * rows + size)
    part = pair[at, :] if axis == 1 else pair[:, at]
    part = lax.dot_general(part, other[...], (((axis,), (0,)), ((), ())), preferred_element_type=f32)
    done = 0
    for grad in grads:
        grad[...] = part[done : done + grad.shape[0], :].astype(grad.dtype)
        done += grad.shape[0]


def pair_kernel(images, texts, skip, img_first, txt_first, img_count, *refs):
    img_refs, txt_refs = refs[:images], refs[images : images + texts]
    p_ref, pair_ref, img, txt = refs[images + texts : images + texts + 4]
    grads, sems = refs[images + texts + 4 : -1], refs[-1]
    rows = img_refs[0].shape[0]
    copies = load_all(
        img_refs + txt_refs,
        [img.at[pl.ds(k * rows, rows), :] for k in range(images)]
        + [txt.at[pl.ds(k * rows, rows), :] for k in range(texts)],
        sems,
        skip,
    )
    for copy in copies[:images]:
        copy.wait()
    step = tile_rows(texts * rows, 256)
    for j in range(texts * rows // step):
        for copy in copies[images + j * step // rows : images + (j + 1) * step // rows]:
            copy.wait()
        at = slice(j * step, (j + 1) * step)
        dots = lax.dot_general(img[...], txt[at, :], (((1,), (1,)), ((), ())), preferred_element_type=f32)
        pair_ref[:, at] = (2.0 * jax.nn.sigmoid(logit_scale * dots + logit_bias) - p_ref[:, at]).astype(bf16)
    if img_count:
        write_grads(rows, pair_ref, txt, 1, img_first, grads[:img_count])
    if len(grads) > img_count:
        write_grads(rows, pair_ref, img, 0, txt_first, grads[img_count:])


def pair_and_sent(img_blocks, txt_blocks, skip, targets, img_first, img_out, txt_first, txt_out):
    images, texts = len(img_blocks), len(txt_blocks)
    rows, width = img_blocks[0].shape
    shapes = [jax.ShapeDtypeStruct((images * rows, texts * rows), bf16)]
    shapes += [jax.ShapeDtypeStruct((n, width), bf16) for n in (images * rows, texts * rows) + img_out + txt_out]
    return pl.pallas_call(
        functools.partial(pair_kernel, images, texts, skip, img_first, txt_first, len(img_out)),
        out_shape=shapes,
        in_specs=[ANY] * (images + texts) + [VMEM],
        out_specs=[VMEM] * len(shapes),
        scratch_shapes=[pltpu.SemaphoreType.DMA((images + texts,))],
        compiler_params=params(
            ((images * rows, texts * rows), 6),
            ((images + texts, rows, width), 2),
            ((sum(img_out) + sum(txt_out), width), 6),
        ),
        cost_estimate=pl.CostEstimate(
            flops=4 * images * texts * rows * rows * width,
            bytes_accessed=2 * (images + texts) * rows * width + 8 * images * texts * rows * rows,
            transcendentals=images * texts * rows * rows,
        ),
        name="pair_and_sent",
    )(*img_blocks, *txt_blocks, targets)


def grads_kernel(rows, img_first, img_count, txt_first, pair_ref, img, txt, *grads):
    if len(grads) > img_count:
        write_grads(rows, pair_ref, img, 0, txt_first, grads[img_count:])
    if img_count:
        write_grads(rows, pair_ref, txt, 1, img_first, grads[:img_count])


def some_grads(pair, img, txt, rows, img_first, img_out, txt_first, txt_out, dtype, name):
    width = img.shape[1]
    shapes = [jax.ShapeDtypeStruct((n * rows, width), dtype) for n in img_out + txt_out]
    out = pl.pallas_call(
        functools.partial(grads_kernel, rows, img_first, len(img_out), txt_first),
        out_shape=shapes,
        in_specs=[VMEM] * 3,
        out_specs=[VMEM] * len(shapes),
        compiler_params=params(
            (pair.shape, 2), (img.shape, 2), (txt.shape, 2), ((sum(img_out) + sum(txt_out), rows, width), 8)
        ),
        cost_estimate=pl.CostEstimate(
            flops=2 * pair.size * width,
            bytes_accessed=2 * (pair.size + img.size + txt.size) + 4 * len(shapes) * rows * width,
            transcendentals=0,
        ),
        name=name,
    )(pair, img, txt)
    return out[: len(img_out)], out[len(img_out) :]


def final_kernel(counts, *refs):
    x_ref, out_ref = refs[0], refs[-1]
    pieces, at = [], 1
    for count in counts:
        pieces.append(refs[at : at + count])
        at += count
    most = max(counts)
    step = x_ref.shape[0] // most
    for k in range(most):
        rows = slice(k * step, (k + 1) * step)
        x = x_ref[rows, :].astype(f32)
        inverse = 1.0 / jnp.sqrt(jnp.sum(x * x, axis=1, keepdims=True) + epsilon)
        unit = x * inverse
        grad = None
        for part in pieces:
            term = (part[0][rows, :] if len(part) == 1 else part[k][...]).astype(f32)
            grad = term if grad is None else grad + term
        grad = logit_scale * grad
        along = jnp.sum(unit * grad, axis=1, keepdims=True)
        out_ref[rows, :] = (grad - unit * along) * inverse


def final(x, parts):
    counts = tuple(len(part) for part in parts)
    operands = [x] + [v for part in parts for v in part]
    return pl.pallas_call(
        functools.partial(final_kernel, counts),
        out_shape=jax.ShapeDtypeStruct(x.shape, f32),
        in_specs=[VMEM] * len(operands),
        out_specs=VMEM,
        compiler_params=params((x.shape, 4 * (4 + len(parts)))),
        cost_estimate=pl.CostEstimate(flops=10 * x.size, bytes_accessed=12 * x.size, transcendentals=0),
        name="final",
    )(*operands)


def token_kernel(*refs):
    refs[-1][...] = jnp.zeros_like(refs[-1])


def token(*arrays, flops):
    return pl.pallas_call(
        token_kernel,
        out_shape=jax.ShapeDtypeStruct((8, 128), f32),
        in_specs=[ANY] * len(arrays),
        out_specs=VMEM,
        cost_estimate=pl.CostEstimate(flops=flops, bytes_accessed=0, transcendentals=0),
        name="token",
    )(*arrays)


def after(x, *others):
    others = [v for other in others for v in (other.values() if isinstance(other, dict) else [other])]
    return lax.optimization_barrier((x, *others))[0] if others else x


def body(plan, student_img, student_txt, teacher_img, teacher_txt):
    rows, width = student_img.shape
    far, near, core, row, col = (plan[k] for k in plan.order)

    def spread(x, name, *before):
        return {a: plan.send(after(x, *before), name, a) for a in range(1, plan[name])}

    def onward(blocks, name, *before):
        return {
            (b, a): plan.send(after(x, *before), name, b) for b in range(1, plan[name]) for a, x in blocks.items()
        }

    t_img, t_txt, s_img, s_txt, b_img, b_txt = unit_rows(teacher_img, teacher_txt, student_img, student_txt)
    t_far = spread(t_img, "far")
    t_near = spread(t_txt, "near")
    b_col = spread(b_img, "col")
    b_row = spread(b_txt, "row")
    b_core = spread(b_txt, "core")
    first = [b_col, b_row, b_core]
    teacher_z = token(*t_far.values(), *t_near.values(), flops=10000000000)
    s_far = spread(s_img, "far", teacher_z)
    s_near = spread(s_txt, "near", teacher_z)
    t_far_col = onward(t_far, "col", *first)
    t_near_row = onward(t_near, "row", *first)
    b_row_core = onward(b_row, "core", *first)
    second = [token(*s_far.values(), *s_near.values(), flops=10000000000), t_far_col, t_near_row, b_row_core]
    s_far_col = onward(s_far, "col", *second)
    s_near_row = onward(s_near, "row", *second)
    s_near_core = onward(s_near, "core", *second)
    t_near_core = onward(t_near, "core", *second)
    t_both_core = onward(t_near_row, "core", *second)

    def images(own, by_far, by_col, by_both):
        blocks = {(0, 0): own, **by_both}
        blocks.update({(0, a): x for a, x in by_far.items()})
        blocks.update({(b, 0): x for b, x in by_col.items()})
        return [blocks[b, a] for b in range(col) for a in range(far)]

    def texts(own, by_near, by_row, by_both, by_core, by_core_near, by_core_row, by_core_both):
        blocks = {(0, 0, 0): own}
        blocks.update({(0, 0, a): x for a, x in by_near.items()})
        blocks.update({(0, b, 0): x for b, x in by_row.items()})
        blocks.update({(0, *key): x for key, x in by_both.items()})
        blocks.update({(c, 0, 0): x for c, x in by_core.items()})
        blocks.update({(c, 0, a): x for (c, a), x in by_core_near.items()})
        blocks.update({(c, b, 0): x for (c, b), x in by_core_row.items()})
        blocks.update({(c, *key): x for (c, key), x in by_core_both.items()})
        return [blocks[c, b, a] for c in range(core) for b in range(row) for a in range(near)]

    targets = teacher_targets(
        images(t_img, t_far, b_col, t_far_col),
        texts(t_txt, t_near, b_row, t_near_row, b_core, t_near_core, b_row_core, t_both_core),
    )
    s_both_core = onward(s_near_row, "core", s_near_core, targets)
    s_imgs = images(s_img, s_far, b_col, s_far_col)
    s_txts = texts(s_txt, s_near, b_row, s_near_row, b_core, s_near_core, b_row_core, s_both_core)

    own_txt = row * near
    pieces = 1 if rows % (16 * 1) == 0 else 1
    cut = rows // pieces

    def piece(x, i):
        return x[i * cut : (i + 1) * cut]

    onward_keys = [(b, a) for b in range(1, col) for a in range(1, far)]
    last_keys = [(b, 0) for b in range(1, col)]
    img_out = tuple(n for b in range(1, col) for a in range(far) for n in ((cut,) * pieces if a else (rows,)))
    txt_out = (near * rows,) * (row * (core - 1))
    skip = teacher_img.shape[1]
    out = pair_and_sent(s_imgs, s_txts, skip, targets, far, img_out, own_txt, txt_out)
    pair, img_pack, txt_pack = out[:3]
    img_list, txt_list = list(out[3 : 3 + len(img_out)]), out[3 + len(img_out) :]
    img_sent = {}
    for b in range(1, col):
        for a in range(far):
            img_sent[b, a] = [img_list.pop(0) for _ in range(pieces if a else 1)]
    txt_sent = {(1 + k // row, k % row): v for k, v in enumerate(txt_list)}
    img_part, txt_part = some_grads(pair, img_pack, txt_pack, rows, 0, (1,) * far, 0, (1,) * own_txt, f32, "kept")
    txt_part = {divmod(k, near): v for k, v in enumerate(txt_part)}

    img_in = {key: [plan.send(v, "col", -key[0]) for v in img_sent[key]] for key in onward_keys}
    txt_in = {key: plan.send(v, "core", -key[0]) for key, v in txt_sent.items()}

    for c in range(1, core):
        for b in range(row):
            for a in range(near):
                txt_part[b, a] = txt_part[b, a] + txt_in[c, b][a * rows : (a + 1) * rows].astype(f32)
    row_in = {
        (b, a): [plan.send(piece(txt_part[b, a], i).astype(bf16), "row", -b) for i in range(pieces)]
        for b in range(1, row)
        for a in range(1, near)
    }

    def summed(own, arrived, i):
        total = piece(own, i)
        for v in arrived:
            total = total + v[i].astype(f32)
        return total.astype(bf16)

    txt_ready = [
        [summed(txt_part[0, a], [row_in[b, a] for b in range(1, row)], i) for i in range(pieces)]
        for a in range(1, near)
    ]
    txt_last = [[plan.send(v, "near", -a) for v in part] for a, part in zip(range(1, near), txt_ready)]
    img_last = [
        [
            plan.send(summed(img_part[a], [img_in[b, a] for b in range(1, col)], i), "far", -a)
            for i in range(pieces)
        ]
        for a in range(1, far)
    ]
    col_ahead = list(txt_in.values())
    row_ahead = [v for key in onward_keys for v in img_in[key]]
    for key in last_keys:
        img_in[key] = [plan.send(after(img_sent[key][0], *col_ahead), "col", -key[0])]
    for b in range(1, row):
        row_in[b, 0] = [plan.send(after(txt_part[b, 0].astype(bf16), *row_ahead), "row", -b)]
    img_own, txt_own = img_part[0], txt_part[0, 0]
    image_grad = final(student_img, [[img_own]] + [img_in[b, 0] for b in range(1, col)] + img_last)
    text_grad = final(student_txt, [[txt_own]] + [row_in[b, 0] for b in range(1, row)] + txt_last)
    return image_grad, text_grad


def solution(mesh):
    spec = P(AXES, None)
    return jax.shard_map(
        functools.partial(body, Plan(mesh)), mesh=mesh, in_specs=(spec,) * 4, out_specs=(spec,) * 2, check_vma=False
    )
```

```python
import functools
import math
import jax
import jax.numpy as jnp
from jax import lax
from jax.experimental import pallas as pl
from jax.experimental.pallas import tpu as pltpu
from jax.sharding import PartitionSpec as P

epsilon = 1e-06
logit_scale = 100.0
logit_bias = -4.0

AXES = ("blk", "narrow")
ANY = pl.BlockSpec(memory_space=pl.ANY)
VMEM = pl.BlockSpec(memory_space=pltpu.VMEM)
f32 = jnp.float32
bf16 = jnp.bfloat16


def split_two(size):
    fast = int(size**0.5)
    while size % fast:
        fast -= 1
    return max(fast, size // fast), min(fast, size // fast)


class Plan:
    def __init__(self, mesh):
        blk, narrow = mesh.shape["blk"], mesh.shape["narrow"]
        core = 2 if blk % 2 == 0 else 1
        far, near = split_two(blk // core)
        large, small = split_two(narrow)
        self.digits = {"far": far, "near": near, "core": core, "row": small, "col": large}
        self.order = ["far", "near", "core", "row", "col"]

    def __getitem__(self, name):
        return self.digits[name]

    def place(self, index):
        out = {}
        for name in reversed(self.order):
            out[name] = index % self.digits[name]
            index //= self.digits[name]
        return out

    def index(self, place):
        out = 0
        for name in self.order:
            out = out * self.digits[name] + place[name]
        return out

    def send(self, x, name, by):
        total = 1
        for size in self.digits.values():
            total *= size
        pairs = []
        for src in range(total):
            place = self.place(src)
            place[name] = (place[name] + by) % self.digits[name]
            pairs.append((src, self.index(place)))
        return lax.ppermute(x, AXES, pairs)


def params(*held):
    total = sum(math.prod(shape) * size for shape, size in held)
    return pltpu.CompilerParams(vmem_limit_bytes=int(total) + 8 * 2**20)


def tile_rows(rows, most):
    step = most
    while rows % step:
        step //= 2
    return step


def load_all(refs, targets, sems, columns=None):
    copies = []
    for k, (ref, target) in enumerate(zip(refs, targets)):
        if columns is not None and ref.shape[1] != target.shape[1]:
            ref = ref.at[:, pl.ds(columns, target.shape[1])]
        copies.append(pltpu.make_async_copy(ref, target, sems.at[k]))
        copies[-1].start()
    return copies


def unit_kernel(count, *refs):
    x_refs, out_refs, both_refs = refs[:count], refs[count : 2 * count], refs[2 * count : 2 * count + count // 2]
    held, sems = refs[2 * count + count // 2 : -1], refs[-1]
    copies = load_all(x_refs, held, sems)
    for k, (copy, x_ref, out_ref) in enumerate(zip(copies, held, out_refs)):
        copy.wait()
        x = x_ref[...].astype(f32)
        scale = 1.0 / jnp.sqrt(jnp.sum(x * x, axis=1, keepdims=True) + epsilon)
        unit = (x * scale).astype(bf16)
        out_ref[...] = unit
        both, width = both_refs[k % (count // 2)], x.shape[1]
        if k < count // 2:
            both[:, :width] = unit
        else:
            both[:, both.shape[1] - width :] = unit


def unit_rows(*arrays):
    half = len(arrays) // 2
    both = [(a.shape[0], a.shape[1] + b.shape[1]) for a, b in zip(arrays[:half], arrays[half:])]
    return pl.pallas_call(
        functools.partial(unit_kernel, len(arrays)),
        out_shape=[jax.ShapeDtypeStruct(a.shape, bf16) for a in arrays]
        + [jax.ShapeDtypeStruct(shape, bf16) for shape in both],
        in_specs=[ANY] * len(arrays),
        out_specs=[VMEM] * (len(arrays) + half),
        scratch_shapes=[pltpu.VMEM(a.shape, bf16) for a in arrays]
        + [pltpu.SemaphoreType.DMA((len(arrays),))],
        compiler_params=pltpu.CompilerParams(vmem_limit_bytes=int(60 * 2**20)),
        cost_estimate=pl.CostEstimate(
            flops=4 * sum(a.size for a in arrays),
            bytes_accessed=6 * sum(a.size for a in arrays),
            transcendentals=0,
        ),
        name="unit_rows",
    )(*arrays)


def pack(refs, target, columns):
    rows, width = refs[0].shape[0], target.shape[1]
    for k, ref in enumerate(refs):
        first = columns if ref.shape[1] != width else 0
        target[k * rows : (k + 1) * rows, :] = ref[:, first : first + width]


def teacher_kernel(images, texts, *refs):
    img_refs, txt_refs = refs[:images], refs[images : images + texts]
    p_ref, img, txt = refs[images + texts :]
    rows = img_refs[0].shape[0]
    pack(img_refs, img, 0)
    pack(txt_refs, txt, 0)
    step = tile_rows(texts * rows, 256)

    def one(j, carry):
        at = pl.ds(pl.multiple_of(j * step, step), step)
        dots = lax.dot_general(img[...], txt[at, :], (((1,), (1,)), ((), ())), preferred_element_type=f32)
        p_ref[:, at] = jax.nn.sigmoid(logit_scale * dots + logit_bias)
        return carry

    lax.fori_loop(0, texts * rows // step, one, 0)
    own = lax.broadcasted_iota(jnp.int32, (rows, rows), 0) == lax.broadcasted_iota(jnp.int32, (rows, rows), 1)
    p_ref[:rows, :rows] = p_ref[:rows, :rows] + jnp.where(own, 1.0, 0.0).astype(f32)


def teacher_targets(img_blocks, txt_blocks):
    images, texts = len(img_blocks), len(txt_blocks)
    rows, width = img_blocks[0].shape
    return pl.pallas_call(
        functools.partial(teacher_kernel, images, texts),
        out_shape=jax.ShapeDtypeStruct((images * rows, texts * rows), f32),
        in_specs=[VMEM] * (images + texts),
        out_specs=VMEM,
        scratch_shapes=[
            pltpu.VMEM((images * rows, width), bf16),
            pltpu.VMEM((texts * rows, width), bf16),
        ],
        compiler_params=params(((images + texts, rows, width), 2), ((images, rows, texts, rows), 4), *[(v.shape, 2) for v in (*img_blocks, *txt_blocks)]),
        cost_estimate=pl.CostEstimate(
            flops=2 * images * texts * rows * rows * width,
            bytes_accessed=2 * (images + texts) * rows * width + 4 * images * texts * rows * rows,
            transcendentals=images * texts * rows * rows,
        ),
        name="teacher_targets",
    )(*img_blocks, *txt_blocks)


def write_grads(rows, pair, other, axis, first, grads):
    size = sum(g.shape[0] for g in grads)
    at = slice(first * rows, first * rows + size)
    part = pair[at, :] if axis == 1 else pair[:, at]
    part = lax.dot_general(part, other[...], (((axis,), (0,)), ((), ())), preferred_element_type=f32)
    done = 0
    for grad in grads:
        grad[...] = part[done : done + grad.shape[0], :].astype(grad.dtype)
        done += grad.shape[0]


def pair_kernel(images, texts, skip, img_first, txt_first, img_count, *refs):
    img_refs, txt_refs = refs[:images], refs[images : images + texts]
    p_ref, pair_ref, img, txt = refs[images + texts : images + texts + 4]
    grads = refs[images + texts + 4 :]
    rows = img_refs[0].shape[0]
    pack(img_refs, img, skip)
    pack(txt_refs, txt, skip)
    step = tile_rows(texts * rows, 256)
    for j in range(texts * rows // step):
        at = slice(j * step, (j + 1) * step)
        dots = lax.dot_general(img[...], txt[at, :], (((1,), (1,)), ((), ())), preferred_element_type=f32)
        pair_ref[:, at] = (2.0 * jax.nn.sigmoid(logit_scale * dots + logit_bias) - p_ref[:, at]).astype(bf16)
    if img_count:
        write_grads(rows, pair_ref, txt, 1, img_first, grads[:img_count])
    if len(grads) > img_count:
        write_grads(rows, pair_ref, img, 0, txt_first, grads[img_count:])


def pair_and_sent(img_blocks, txt_blocks, skip, targets, img_first, img_out, txt_first, txt_out):
    images, texts = len(img_blocks), len(txt_blocks)
    rows, width = img_blocks[0].shape
    shapes = [jax.ShapeDtypeStruct((images * rows, texts * rows), bf16)]
    shapes += [jax.ShapeDtypeStruct((n, width), bf16) for n in (images * rows, texts * rows) + img_out + txt_out]
    return pl.pallas_call(
        functools.partial(pair_kernel, images, texts, skip, img_first, txt_first, len(img_out)),
        out_shape=shapes,
        in_specs=[VMEM] * (images + texts + 1),
        out_specs=[VMEM] * len(shapes),
        compiler_params=params(
            ((images * rows, texts * rows), 6),
            ((images + texts, rows, width), 2),
            *[(v.shape, 2) for v in (*img_blocks, *txt_blocks)],
            ((sum(img_out) + sum(txt_out), width), 6),
        ),
        cost_estimate=pl.CostEstimate(
            flops=4 * images * texts * rows * rows * width,
            bytes_accessed=2 * (images + texts) * rows * width + 8 * images * texts * rows * rows,
            transcendentals=images * texts * rows * rows,
        ),
        name="pair_and_sent",
    )(*img_blocks, *txt_blocks, targets)


def grads_kernel(rows, img_first, img_count, txt_first, pair_ref, img, txt, *grads):
    if len(grads) > img_count:
        write_grads(rows, pair_ref, img, 0, txt_first, grads[img_count:])
    if img_count:
        write_grads(rows, pair_ref, txt, 1, img_first, grads[:img_count])


def some_grads(pair, img, txt, rows, img_first, img_out, txt_first, txt_out, dtype, name):
    width = img.shape[1]
    shapes = [jax.ShapeDtypeStruct((n * rows, width), dtype) for n in img_out + txt_out]
    out = pl.pallas_call(
        functools.partial(grads_kernel, rows, img_first, len(img_out), txt_first),
        out_shape=shapes,
        in_specs=[VMEM] * 3,
        out_specs=[VMEM] * len(shapes),
        compiler_params=params(
            (pair.shape, 2), (img.shape, 2), (txt.shape, 2), ((sum(img_out) + sum(txt_out), rows, width), 8)
        ),
        cost_estimate=pl.CostEstimate(
            flops=2 * pair.size * width,
            bytes_accessed=2 * (pair.size + img.size + txt.size) + 4 * len(shapes) * rows * width,
            transcendentals=0,
        ),
        name=name,
    )(pair, img, txt)
    return out[: len(img_out)], out[len(img_out) :]


def final_kernel(counts, *refs):
    x_ref, out_ref = refs[0], refs[-1]
    pieces, at = [], 1
    for count in counts:
        pieces.append(refs[at : at + count])
        at += count
    most = max(counts)
    step = x_ref.shape[0] // most
    for k in range(most):
        rows = slice(k * step, (k + 1) * step)
        x = x_ref[rows, :].astype(f32)
        inverse = 1.0 / jnp.sqrt(jnp.sum(x * x, axis=1, keepdims=True) + epsilon)
        unit = x * inverse
        grad = None
        for part in pieces:
            term = (part[0][rows, :] if len(part) == 1 else part[k][...]).astype(f32)
            grad = term if grad is None else grad + term
        grad = logit_scale * grad
        along = jnp.sum(unit * grad, axis=1, keepdims=True)
        out_ref[rows, :] = (grad - unit * along) * inverse


def final(x, parts):
    counts = tuple(len(part) for part in parts)
    operands = [x] + [v for part in parts for v in part]
    return pl.pallas_call(
        functools.partial(final_kernel, counts),
        out_shape=jax.ShapeDtypeStruct(x.shape, f32),
        in_specs=[VMEM] * len(operands),
        out_specs=VMEM,
        compiler_params=params((x.shape, 4 * (4 + len(parts)))),
        cost_estimate=pl.CostEstimate(flops=10 * x.size, bytes_accessed=12 * x.size, transcendentals=0),
        name="final",
    )(*operands)


def token_kernel(*refs):
    refs[-1][...] = jnp.zeros_like(refs[-1])


def token(*arrays, flops):
    return pl.pallas_call(
        token_kernel,
        out_shape=jax.ShapeDtypeStruct((8, 128), f32),
        in_specs=[ANY] * len(arrays),
        out_specs=VMEM,
        cost_estimate=pl.CostEstimate(flops=flops, bytes_accessed=0, transcendentals=0),
        name="token",
    )(*arrays)


def after(x, *others):
    others = [v for other in others for v in (other.values() if isinstance(other, dict) else [other])]
    return lax.optimization_barrier((x, *others))[0] if others else x


def body(plan, student_img, student_txt, teacher_img, teacher_txt):
    rows, width = student_img.shape
    far, near, core, row, col = (plan[k] for k in plan.order)

    def spread(x, name, *before):
        return {a: plan.send(after(x, *before), name, a) for a in range(1, plan[name])}

    def onward(blocks, name, *before):
        return {
            (b, a): plan.send(after(x, *before), name, b) for b in range(1, plan[name]) for a, x in blocks.items()
        }

    t_img, t_txt, s_img, s_txt, b_img, b_txt = unit_rows(teacher_img, teacher_txt, student_img, student_txt)
    t_far = spread(t_img, "far")
    t_near = spread(t_txt, "near")
    b_col = spread(b_img, "col")
    b_row = spread(b_txt, "row")
    b_core = spread(b_txt, "core")
    first = [b_col, b_row, b_core]
    teacher_z = token(*t_far.values(), *t_near.values(), flops=10000000000)
    s_far = spread(s_img, "far", teacher_z)
    s_near = spread(s_txt, "near", teacher_z)
    t_far_col = onward(t_far, "col", *first)
    t_near_row = onward(t_near, "row", *first)
    b_row_core = onward(b_row, "core", *first)
    second = [token(*s_far.values(), *s_near.values(), flops=10000000000), t_far_col, t_near_row, b_row_core]
    s_far_col = onward(s_far, "col", *second)
    s_near_row = onward(s_near, "row", *second)
    s_near_core = onward(s_near, "core", *second)
    t_near_core = onward(t_near, "core", *second)
    t_both_core = onward(t_near_row, "core", *second)

    def images(own, by_far, by_col, by_both):
        blocks = {(0, 0): own, **by_both}
        blocks.update({(0, a): x for a, x in by_far.items()})
        blocks.update({(b, 0): x for b, x in by_col.items()})
        return [blocks[b, a] for b in range(col) for a in range(far)]

    def texts(own, by_near, by_row, by_both, by_core, by_core_near, by_core_row, by_core_both):
        blocks = {(0, 0, 0): own}
        blocks.update({(0, 0, a): x for a, x in by_near.items()})
        blocks.update({(0, b, 0): x for b, x in by_row.items()})
        blocks.update({(0, *key): x for key, x in by_both.items()})
        blocks.update({(c, 0, 0): x for c, x in by_core.items()})
        blocks.update({(c, 0, a): x for (c, a), x in by_core_near.items()})
        blocks.update({(c, b, 0): x for (c, b), x in by_core_row.items()})
        blocks.update({(c, *key): x for (c, key), x in by_core_both.items()})
        return [blocks[c, b, a] for c in range(core) for b in range(row) for a in range(near)]

    targets = teacher_targets(
        images(t_img, t_far, b_col, t_far_col),
        texts(t_txt, t_near, b_row, t_near_row, b_core, t_near_core, b_row_core, t_both_core),
    )
    s_both_core = onward(s_near_row, "core", s_near_core, targets)
    s_imgs = images(s_img, s_far, b_col, s_far_col)
    s_txts = texts(s_txt, s_near, b_row, s_near_row, b_core, s_near_core, b_row_core, s_both_core)

    own_txt = row * near
    pieces = 1 if rows % (16 * 1) == 0 else 1
    cut = rows // pieces

    def piece(x, i):
        return x[i * cut : (i + 1) * cut]

    onward_keys = [(b, a) for b in range(1, col) for a in range(1, far)]
    last_keys = [(b, 0) for b in range(1, col)]
    img_out = tuple(n for b in range(1, col) for a in range(far) for n in ((cut,) * pieces if a else (rows,)))
    txt_out = (near * rows,) * (row * (core - 1))
    skip = teacher_img.shape[1]
    out = pair_and_sent(s_imgs, s_txts, skip, targets, far, img_out, own_txt, txt_out)
    pair, img_pack, txt_pack = out[:3]
    img_list, txt_list = list(out[3 : 3 + len(img_out)]), out[3 + len(img_out) :]
    img_sent = {}
    for b in range(1, col):
        for a in range(far):
            img_sent[b, a] = [img_list.pop(0) for _ in range(pieces if a else 1)]
    txt_sent = {(1 + k // row, k % row): v for k, v in enumerate(txt_list)}
    img_part, txt_part = some_grads(pair, img_pack, txt_pack, rows, 0, (1,) * far, 0, (1,) * own_txt, f32, "kept")
    txt_part = {divmod(k, near): v for k, v in enumerate(txt_part)}

    img_in = {key: [plan.send(v, "col", -key[0]) for v in img_sent[key]] for key in onward_keys}
    txt_in = {key: plan.send(v, "core", -key[0]) for key, v in txt_sent.items()}

    for c in range(1, core):
        for b in range(row):
            for a in range(near):
                txt_part[b, a] = txt_part[b, a] + txt_in[c, b][a * rows : (a + 1) * rows].astype(f32)
    row_in = {
        (b, a): [plan.send(piece(txt_part[b, a], i).astype(bf16), "row", -b) for i in range(pieces)]
        for b in range(1, row)
        for a in range(1, near)
    }

    def summed(own, arrived, i):
        total = piece(own, i)
        for v in arrived:
            total = total + v[i].astype(f32)
        return total.astype(bf16)

    txt_ready = [
        [summed(txt_part[0, a], [row_in[b, a] for b in range(1, row)], i) for i in range(pieces)]
        for a in range(1, near)
    ]
    txt_last = [[plan.send(v, "near", -a) for v in part] for a, part in zip(range(1, near), txt_ready)]
    img_last = [
        [
            plan.send(summed(img_part[a], [img_in[b, a] for b in range(1, col)], i), "far", -a)
            for i in range(pieces)
        ]
        for a in range(1, far)
    ]
    col_ahead = list(txt_in.values())
    row_ahead = [v for key in onward_keys for v in img_in[key]]
    for key in last_keys:
        img_in[key] = [plan.send(after(img_sent[key][0], *col_ahead), "col", -key[0])]
    for b in range(1, row):
        row_in[b, 0] = [plan.send(after(txt_part[b, 0].astype(bf16), *row_ahead), "row", -b)]
    img_own, txt_own = img_part[0], txt_part[0, 0]
    image_grad = final(student_img, [[img_own]] + [img_in[b, 0] for b in range(1, col)] + img_last)
    text_grad = final(student_txt, [[txt_own]] + [row_in[b, 0] for b in range(1, row)] + txt_last)
    return image_grad, text_grad


def solution(mesh):
    spec = P(AXES, None)
    return jax.shard_map(
        functools.partial(body, Plan(mesh)), mesh=mesh, in_specs=(spec,) * 4, out_specs=(spec,) * 2, check_vma=False
    )
```

```python
import functools
import math
import jax
import jax.numpy as jnp
from jax import lax
from jax.experimental import pallas as pl
from jax.experimental.pallas import tpu as pltpu
from jax.sharding import PartitionSpec as P

epsilon = 1e-06
logit_scale = 100.0
logit_bias = -4.0

AXES = ("blk", "narrow")
ANY = pl.BlockSpec(memory_space=pl.ANY)
VMEM = pl.BlockSpec(memory_space=pltpu.VMEM)
f32 = jnp.float32
bf16 = jnp.bfloat16


def split_two(size):
    fast = int(size**0.5)
    while size % fast:
        fast -= 1
    return max(fast, size // fast), min(fast, size // fast)


class Plan:
    def __init__(self, mesh):
        blk, narrow = mesh.shape["blk"], mesh.shape["narrow"]
        core = 2 if blk % 2 == 0 else 1
        far, near = split_two(blk // core)
        large, small = split_two(narrow)
        self.digits = {"far": far, "near": near, "core": core, "row": small, "col": large}
        self.order = ["far", "near", "core", "row", "col"]

    def __getitem__(self, name):
        return self.digits[name]

    def place(self, index):
        out = {}
        for name in reversed(self.order):
            out[name] = index % self.digits[name]
            index //= self.digits[name]
        return out

    def index(self, place):
        out = 0
        for name in self.order:
            out = out * self.digits[name] + place[name]
        return out

    def send(self, x, name, by):
        total = 1
        for size in self.digits.values():
            total *= size
        pairs = []
        for src in range(total):
            place = self.place(src)
            place[name] = (place[name] + by) % self.digits[name]
            pairs.append((src, self.index(place)))
        return lax.ppermute(x, AXES, pairs)


def params(*held):
    total = sum(math.prod(shape) * size for shape, size in held)
    return pltpu.CompilerParams(vmem_limit_bytes=int(total) + 8 * 2**20)


def tile_rows(rows, most):
    step = most
    while rows % step:
        step //= 2
    return step


def load_all(refs, targets, sems, columns=None):
    copies = []
    for k, (ref, target) in enumerate(zip(refs, targets)):
        if columns is not None and ref.shape[1] != target.shape[1]:
            ref = ref.at[:, pl.ds(columns, target.shape[1])]
        copies.append(pltpu.make_async_copy(ref, target, sems.at[k]))
        copies[-1].start()
    return copies


def unit_kernel(count, *refs):
    x_refs, out_refs, both_refs = refs[:count], refs[count : 2 * count], refs[2 * count : 2 * count + count // 2]
    held, sems = refs[2 * count + count // 2 : -1], refs[-1]
    copies = load_all(x_refs, held, sems)
    for k, (copy, x_ref, out_ref) in enumerate(zip(copies, held, out_refs)):
        copy.wait()
        x = x_ref[...].astype(f32)
        scale = 1.0 / jnp.sqrt(jnp.sum(x * x, axis=1, keepdims=True) + epsilon)
        unit = (x * scale).astype(bf16)
        out_ref[...] = unit
        both, width = both_refs[k % (count // 2)], x.shape[1]
        if k < count // 2:
            both[:, :width] = unit
        else:
            both[:, both.shape[1] - width :] = unit


def unit_rows(*arrays):
    half = len(arrays) // 2
    both = [(a.shape[0], a.shape[1] + b.shape[1]) for a, b in zip(arrays[:half], arrays[half:])]
    return pl.pallas_call(
        functools.partial(unit_kernel, len(arrays)),
        out_shape=[jax.ShapeDtypeStruct(a.shape, bf16) for a in arrays]
        + [jax.ShapeDtypeStruct(shape, bf16) for shape in both],
        in_specs=[ANY] * len(arrays),
        out_specs=[VMEM] * (len(arrays) + half),
        scratch_shapes=[pltpu.VMEM(a.shape, bf16) for a in arrays]
        + [pltpu.SemaphoreType.DMA((len(arrays),))],
        compiler_params=pltpu.CompilerParams(vmem_limit_bytes=int(60 * 2**20)),
        cost_estimate=pl.CostEstimate(
            flops=4 * sum(a.size for a in arrays),
            bytes_accessed=6 * sum(a.size for a in arrays),
            transcendentals=0,
        ),
        name="unit_rows",
    )(*arrays)


def pack(refs, target, columns):
    rows, width = refs[0].shape[0], target.shape[1]
    for k, ref in enumerate(refs):
        first = columns if ref.shape[1] != width else 0
        target[k * rows : (k + 1) * rows, :] = ref[:, first : first + width]


def teacher_kernel(images, texts, *refs):
    img_refs, txt_refs = refs[:images], refs[images : images + texts]
    p_ref, img, txt = refs[images + texts :]
    rows = img_refs[0].shape[0]
    pack(img_refs, img, 0)
    pack(txt_refs, txt, 0)
    step = tile_rows(texts * rows, 256)

    def one(j, carry):
        at = pl.ds(pl.multiple_of(j * step, step), step)
        dots = lax.dot_general(img[...], txt[at, :], (((1,), (1,)), ((), ())), preferred_element_type=f32)
        p_ref[:, at] = jax.nn.sigmoid(logit_scale * dots + logit_bias)
        return carry

    lax.fori_loop(0, texts * rows // step, one, 0)
    own = lax.broadcasted_iota(jnp.int32, (rows, rows), 0) == lax.broadcasted_iota(jnp.int32, (rows, rows), 1)
    p_ref[:rows, :rows] = p_ref[:rows, :rows] + jnp.where(own, 1.0, 0.0).astype(f32)


def teacher_targets(img_blocks, txt_blocks):
    images, texts = len(img_blocks), len(txt_blocks)
    rows, width = img_blocks[0].shape
    return pl.pallas_call(
        functools.partial(teacher_kernel, images, texts),
        out_shape=jax.ShapeDtypeStruct((images * rows, texts * rows), f32),
        in_specs=[VMEM] * (images + texts),
        out_specs=VMEM,
        scratch_shapes=[
            pltpu.VMEM((images * rows, width), bf16),
            pltpu.VMEM((texts * rows, width), bf16),
        ],
        compiler_params=params(((images + texts, rows, width), 2), ((images, rows, texts, rows), 4), *[(v.shape, 2) for v in (*img_blocks, *txt_blocks)]),
        cost_estimate=pl.CostEstimate(
            flops=2 * images * texts * rows * rows * width,
            bytes_accessed=2 * (images + texts) * rows * width + 4 * images * texts * rows * rows,
            transcendentals=images * texts * rows * rows,
        ),
        name="teacher_targets",
    )(*img_blocks, *txt_blocks)


def image_grads(pair, txt, rows, first, count):
    part = lax.dot_general(
        pair[first * rows : (first + count) * rows, :], txt, (((1,), (0,)), ((), ())), preferred_element_type=f32
    )
    return [part[k * rows : (k + 1) * rows, :] for k in range(count)]


def text_grads(pair, img, rows, first, count):
    part = lax.dot_general(
        pair[:, first * rows : (first + count) * rows], img, (((0,), (0,)), ((), ())), preferred_element_type=f32
    )
    return [part[k * rows : (k + 1) * rows, :] for k in range(count)]


def pair_kernel(images, texts, far, skip, half, own_txt, *refs):
    img_refs, txt_refs = refs[:images], refs[images : images + texts]
    p_ref, pair_ref, img, txt = refs[images + texts : images + texts + 4]
    outs = list(refs[images + texts + 4 :])
    rows, col = img_refs[0].shape[0], images // far
    pack(img_refs, img, skip)
    pack(txt_refs, txt, skip)
    step = tile_rows(texts * rows, 256)
    for j in range(texts * rows // step):
        at = slice(j * step, (j + 1) * step)
        dots = lax.dot_general(img[...], txt[at, :], (((1,), (1,)), ((), ())), preferred_element_type=f32)
        pair_ref[:, at] = (2.0 * jax.nn.sigmoid(logit_scale * dots + logit_bias) - p_ref[:, at]).astype(bf16)
    others = image_grads(pair_ref, txt[...], rows, far, far * (col - 1)) if col > 1 else []
    hops = [outs.pop(0) for _ in range(far * (col - 1))]
    kept = [outs.pop(0) for _ in range(col - 1)]
    longs = [outs.pop(0) for _ in range(far - 1)]
    for k, grad in enumerate(others):
        b, a = 1 + k // far, k % far
        hops[k][...] = grad[:, :half].astype(bf16)
        if a:
            longs[a - 1][b * rows : (b + 1) * rows, :] = grad[:, half:].astype(bf16)
        else:
            kept[b - 1][...] = grad[:, half:]
    if far > 1:
        for a, grad in enumerate(image_grads(pair_ref, txt[:, half:], rows, 1, far - 1)):
            longs[a][:rows, :] = grad.astype(bf16)
    if outs:
        count = outs[0].shape[0] // rows
        grads = text_grads(pair_ref, img[...], rows, own_txt, len(outs) * count)
        for k, grad in enumerate(grads):
            outs[k // count][(k % count) * rows : (k % count + 1) * rows, :] = grad.astype(bf16)


def pair_and_sent(img_blocks, txt_blocks, far, near, own_txt, skip, half, targets):
    images, texts = len(img_blocks), len(txt_blocks)
    rows, width = img_blocks[-1].shape
    col = images // far
    shapes = [((images * rows, texts * rows), bf16), ((images * rows, width), bf16), ((texts * rows, width), bf16)]
    shapes += [((rows, half), bf16)] * (far * (col - 1))
    shapes += [((rows, width - half), f32)] * (col - 1)
    shapes += [((col * rows, width - half), bf16)] * (far - 1)
    shapes += [((near * rows, width), bf16)] * ((texts - own_txt) // near)
    out = pl.pallas_call(
        functools.partial(pair_kernel, images, texts, far, skip, half, own_txt),
        out_shape=[jax.ShapeDtypeStruct(*shape) for shape in shapes],
        in_specs=[VMEM] * (images + texts + 1),
        out_specs=[VMEM] * len(shapes),
        compiler_params=params(
            ((images * rows, texts * rows), 6),
            ((images + texts, rows, width), 6),
            *[(v.shape, 2) for v in (*img_blocks, *txt_blocks)],
        ),
        cost_estimate=pl.CostEstimate(
            flops=4 * images * texts * rows * rows * width,
            bytes_accessed=2 * (images + texts) * rows * width + 8 * images * texts * rows * rows,
            transcendentals=images * texts * rows * rows,
        ),
        name="pair_and_sent",
    )(*img_blocks, *txt_blocks, targets)
    out = list(out)
    cut = [3, 3 + far * (col - 1), 3 + (far + 1) * (col - 1), 3 + (far + 1) * (col - 1) + far - 1]
    return out[:3], out[cut[0] : cut[1]], out[cut[1] : cut[2]], out[cut[2] : cut[3]], out[cut[3] :]


def kept_kernel(half, pair, img, txt, *outs):
    rows = outs[0].shape[0]
    far = len(outs) - 1
    outs[-1][...] = lax.dot_general(
        pair[:, : outs[-1].shape[0]], img[...], (((0,), (0,)), ((), ())), preferred_element_type=f32
    )
    for out, grad in zip(outs, image_grads(pair, txt[...], rows, 0, far)):
        out[...] = grad[:, : out.shape[1]]


def kept_grads(pair, img, txt, rows, far, own_txt, half):
    width = img.shape[1]
    shapes = [(rows, width)] + [(rows, half)] * (far - 1) + [(own_txt * rows, width)]
    return pl.pallas_call(
        functools.partial(kept_kernel, half),
        out_shape=[jax.ShapeDtypeStruct(shape, f32) for shape in shapes],
        in_specs=[VMEM] * 3,
        out_specs=[VMEM] * len(shapes),
        compiler_params=params((pair.shape, 2), (img.shape, 2), (txt.shape, 2), *[(v, 8) for v in shapes]),
        cost_estimate=pl.CostEstimate(
            flops=2 * pair.size * width,
            bytes_accessed=2 * (pair.size + img.size + txt.size) + 4 * own_txt * rows * width,
            transcendentals=0,
        ),
        name="kept",
    )(pair, img, txt)


def text_sums_kernel(row, near, half, cores, own_ref, *refs):
    arrived, outs = refs[: cores * row], list(refs[cores * row :])
    rows = own_ref.shape[0] // (row * near)
    hops = [outs.pop(0) for _ in range(near * (row - 1))]
    kept = [outs.pop(0) for _ in range(row - 1)]
    stay = [outs.pop(0) for _ in range(near)]
    for b in range(row):
        for a in range(near):
            k = b * near + a
            total = own_ref[k * rows : (k + 1) * rows, :]
            for c in range(cores):
                total = total + arrived[c * row + b][a * rows : (a + 1) * rows, :].astype(f32)
            if b:
                hops[(b - 1) * near + a][...] = total[:, :half].astype(bf16)
            else:
                stay[a][...] = total[:, : stay[a].shape[1]]
            if a:
                outs[a - 1][b * rows : (b + 1) * rows, :] = total[:, half:].astype(bf16)
            elif b:
                kept[b - 1][...] = total[:, half:]


def text_sums(own, arrived, rows, row, near, half):
    width = own.shape[1]
    shapes = [((rows, half), bf16)] * (near * (row - 1)) + [((rows, width - half), f32)] * (row - 1)
    shapes += [((rows, width), f32)] + [((rows, half), f32)] * (near - 1)
    shapes += [((row * rows, width - half), bf16)] * (near - 1)
    out = list(
        pl.pallas_call(
            functools.partial(text_sums_kernel, row, near, half, len(arrived) // row),
            out_shape=[jax.ShapeDtypeStruct(*shape) for shape in shapes],
            in_specs=[VMEM] * (1 + len(arrived)),
            out_specs=[VMEM] * len(shapes),
            compiler_params=params((own.shape, 16)),
            cost_estimate=pl.CostEstimate(flops=2 * own.size, bytes_accessed=10 * own.size, transcendentals=0),
            name="text_sums",
        )(own, *arrived)
    )
    cut = [near * (row - 1), (near + 1) * (row - 1), (near + 1) * (row - 1) + near]
    return out[: cut[0]], out[cut[0] : cut[1]], out[cut[1] : cut[2]], out[cut[2] :]


def final_kernel(half, lows, x_ref, own_ref, *refs):
    parts, out_ref = refs[:-1], refs[-1]
    rows = x_ref.shape[0]
    x = x_ref[...].astype(f32)
    inverse = 1.0 / jnp.sqrt(jnp.sum(x * x, axis=1, keepdims=True) + epsilon)
    sides, along = [], 0.0
    for at, refs_at in ((slice(0, half), parts[:lows]), (slice(half, None), parts[lows:])):
        unit = x[:, at] * inverse
        grad = own_ref[:, at]
        for part in refs_at:
            grad = grad + part[:rows, :].astype(f32)
        grad = logit_scale * grad
        along = along + jnp.sum(unit * grad, axis=1, keepdims=True)
        sides.append((at, unit, grad))
    for at, unit, grad in sides:
        out_ref[:, at] = (grad - unit * along) * inverse


def final(x, own, lows, highs, half):
    operands = [x, own, *lows, *highs]
    return pl.pallas_call(
        functools.partial(final_kernel, half, len(lows)),
        out_shape=jax.ShapeDtypeStruct(x.shape, f32),
        in_specs=[VMEM] * len(operands),
        out_specs=VMEM,
        compiler_params=params((x.shape, 4 * (4 + len(operands)))),
        cost_estimate=pl.CostEstimate(flops=10 * x.size, bytes_accessed=12 * x.size, transcendentals=0),
        name="final",
    )(*operands)


def token_kernel(*refs):
    refs[-1][...] = jnp.zeros_like(refs[-1])


def token(*arrays, flops):
    return pl.pallas_call(
        token_kernel,
        out_shape=jax.ShapeDtypeStruct((8, 128), f32),
        in_specs=[ANY] * len(arrays),
        out_specs=VMEM,
        cost_estimate=pl.CostEstimate(flops=flops, bytes_accessed=0, transcendentals=0),
        name="token",
    )(*arrays)


def after(x, *others):
    others = [v for other in others for v in (other.values() if isinstance(other, dict) else [other])]
    return lax.optimization_barrier((x, *others))[0] if others else x


def body(plan, student_img, student_txt, teacher_img, teacher_txt):
    rows, width = student_img.shape
    far, near, core, row, col = (plan[k] for k in plan.order)

    def spread(x, name, *before):
        return {a: plan.send(after(x, *before), name, a) for a in range(1, plan[name])}

    def onward(blocks, name, *before):
        return {
            (b, a): plan.send(after(x, *before), name, b) for b in range(1, plan[name]) for a, x in blocks.items()
        }

    t_img, t_txt, s_img, s_txt, b_img, b_txt = unit_rows(teacher_img, teacher_txt, student_img, student_txt)
    t_far = spread(t_img, "far")
    t_near = spread(t_txt, "near")
    b_col = spread(b_img, "col")
    b_row = spread(b_txt, "row")
    b_core = spread(b_txt, "core")
    first = [b_col, b_row, b_core]
    teacher_z = token(*t_far.values(), *t_near.values(), flops=10000000000)
    s_far = spread(s_img, "far", teacher_z)
    s_near = spread(s_txt, "near", teacher_z)
    t_far_col = onward(t_far, "col", *first)
    t_near_row = onward(t_near, "row", *first)
    b_row_core = onward(b_row, "core", *first)
    second = [token(*s_far.values(), *s_near.values(), flops=10000000000), t_far_col, t_near_row, b_row_core]
    s_far_col = onward(s_far, "col", *second)
    s_near_row = onward(s_near, "row", *second)
    s_near_core = onward(s_near, "core", *second)
    t_near_core = onward(t_near, "core", *second)
    t_both_core = onward(t_near_row, "core", *second)

    def images(own, by_far, by_col, by_both):
        blocks = {(0, 0): own, **by_both}
        blocks.update({(0, a): x for a, x in by_far.items()})
        blocks.update({(b, 0): x for b, x in by_col.items()})
        return [blocks[b, a] for b in range(col) for a in range(far)]

    def texts(own, by_near, by_row, by_both, by_core, by_core_near, by_core_row, by_core_both):
        blocks = {(0, 0, 0): own}
        blocks.update({(0, 0, a): x for a, x in by_near.items()})
        blocks.update({(0, b, 0): x for b, x in by_row.items()})
        blocks.update({(0, *key): x for key, x in by_both.items()})
        blocks.update({(c, 0, 0): x for c, x in by_core.items()})
        blocks.update({(c, 0, a): x for (c, a), x in by_core_near.items()})
        blocks.update({(c, b, 0): x for (c, b), x in by_core_row.items()})
        blocks.update({(c, *key): x for (c, key), x in by_core_both.items()})
        return [blocks[c, b, a] for c in range(core) for b in range(row) for a in range(near)]

    targets = teacher_targets(
        images(t_img, t_far, b_col, t_far_col),
        texts(t_txt, t_near, b_row, t_near_row, b_core, t_near_core, b_row_core, t_both_core),
    )
    s_both_core = onward(s_near_row, "core", s_near_core, targets)
    s_imgs = images(s_img, s_far, b_col, s_far_col)
    s_txts = texts(s_txt, s_near, b_row, s_near_row, b_core, s_near_core, b_row_core, s_both_core)

    own_txt = row * near
    half = width // 128 * 2 // 3 * 128
    skip = teacher_img.shape[1]
    packed, img_hops, img_kept, img_longs, txt_out = pair_and_sent(
        s_imgs, s_txts, far, near, own_txt, skip, half, targets
    )
    pair, img_pack, txt_pack = packed
    img_in = {}
    for b in range(1, col):
        for a in range(1, far):
            img_in[b, a] = plan.send(img_hops[(b - 1) * far + a], "col", -b)
    long_in = [plan.send(v, "far", -1 - k) for k, v in enumerate(img_longs)]
    txt_in = [plan.send(v, "core", -1 - k // row) for k, v in enumerate(txt_out)]
    *img_stay, txt_own = kept_grads(pair, img_pack, txt_pack, rows, far, own_txt, half)
    txt_hops, txt_kept, txt_stay, txt_longs = text_sums(txt_own, txt_in, rows, row, near, half)

    row_in = {}
    for b in range(1, row):
        for a in range(1, near):
            row_in[b, a] = plan.send(txt_hops[(b - 1) * near + a], "row", -b)
    txt_long_in = [plan.send(v, "near", -1 - k) for k, v in enumerate(txt_longs)]

    def total(own, arrived):
        for v in arrived:
            own = own + v.astype(f32)
        return own.astype(bf16)

    img_last = [
        plan.send(total(after(img_stay[a], *txt_hops, *txt_longs), [img_in[b, a] for b in range(1, col)]), "far", -a) for a in range(1, far)
    ]
    txt_last = [
        plan.send(total(txt_stay[a], [row_in[b, a] for b in range(1, row)]), "near", -a) for a in range(1, near)
    ]
    img_side = [
        plan.send(total(after(img_kept[b - 1], *row_in.values()), [v[b * rows : (b + 1) * rows] for v in long_in]), "col", -b)
        for b in range(1, col)
    ]
    txt_side = [
        plan.send(total(txt_kept[b - 1], [v[b * rows : (b + 1) * rows] for v in txt_long_in]), "row", -b)
        for b in range(1, row)
    ]
    col_ahead = list(row_in.values())
    row_ahead = list(img_in.values())
    img_ends = [plan.send(after(img_hops[(b - 1) * far], *col_ahead), "col", -b) for b in range(1, col)]
    txt_ends = [plan.send(after(txt_hops[(b - 1) * near], *row_ahead), "row", -b) for b in range(1, row)]
    image_grad = final(student_img, img_stay[0], img_ends + img_last, img_side + long_in, half)
    text_grad = final(student_txt, txt_stay[0], txt_ends + txt_last, txt_side + txt_long_in, half)
    return image_grad, text_grad


def solution(mesh):
    spec = P(AXES, None)
    return jax.shard_map(
        functools.partial(body, Plan(mesh)), mesh=mesh, in_specs=(spec,) * 4, out_specs=(spec,) * 2, check_vma=False
    )
```

```python
import functools
import math
import jax
import jax.numpy as jnp
from jax import lax
from jax.experimental import pallas as pl
from jax.experimental.pallas import tpu as pltpu
from jax.sharding import PartitionSpec as P

epsilon = 1e-06
logit_scale = 100.0
logit_bias = -4.0

AXES = ("blk", "narrow")
ANY = pl.BlockSpec(memory_space=pl.ANY)
VMEM = pl.BlockSpec(memory_space=pltpu.VMEM)
f32 = jnp.float32
bf16 = jnp.bfloat16


def split_two(size):
    fast = int(size**0.5)
    while size % fast:
        fast -= 1
    return max(fast, size // fast), min(fast, size // fast)


class Plan:
    def __init__(self, mesh):
        blk, narrow = mesh.shape["blk"], mesh.shape["narrow"]
        core = 2 if blk % 2 == 0 else 1
        far, near = split_two(blk // core)
        large, small = split_two(narrow)
        self.digits = {"far": far, "near": near, "core": core, "row": small, "col": large}
        self.order = ["far", "near", "core", "row", "col"]

    def __getitem__(self, name):
        return self.digits[name]

    def place(self, index):
        out = {}
        for name in reversed(self.order):
            out[name] = index % self.digits[name]
            index //= self.digits[name]
        return out

    def index(self, place):
        out = 0
        for name in self.order:
            out = out * self.digits[name] + place[name]
        return out

    def send(self, x, name, by):
        total = 1
        for size in self.digits.values():
            total *= size
        pairs = []
        for src in range(total):
            place = self.place(src)
            place[name] = (place[name] + by) % self.digits[name]
            pairs.append((src, self.index(place)))
        return lax.ppermute(x, AXES, pairs)


def params(*held):
    total = sum(math.prod(shape) * size for shape, size in held)
    return pltpu.CompilerParams(vmem_limit_bytes=int(total) + 8 * 2**20)


def tile_rows(rows, most):
    step = most
    while rows % step:
        step //= 2
    return step


def load_all(refs, targets, sems, columns=None):
    copies = []
    for k, (ref, target) in enumerate(zip(refs, targets)):
        if columns is not None and ref.shape[1] != target.shape[1]:
            ref = ref.at[:, pl.ds(columns, target.shape[1])]
        copies.append(pltpu.make_async_copy(ref, target, sems.at[k]))
        copies[-1].start()
    return copies


def unit_kernel(count, *refs):
    x_refs, out_refs, both_refs = refs[:count], refs[count : 2 * count], refs[2 * count : 2 * count + count // 2]
    held, sems = refs[2 * count + count // 2 : -1], refs[-1]
    copies = load_all(x_refs, held, sems)
    for k, (copy, x_ref, out_ref) in enumerate(zip(copies, held, out_refs)):
        copy.wait()
        x = x_ref[...].astype(f32)
        scale = 1.0 / jnp.sqrt(jnp.sum(x * x, axis=1, keepdims=True) + epsilon)
        unit = (x * scale).astype(bf16)
        out_ref[...] = unit
        both, width = both_refs[k % (count // 2)], x.shape[1]
        if k < count // 2:
            both[:, :width] = unit
        else:
            both[:, both.shape[1] - width :] = unit


def unit_rows(*arrays):
    half = len(arrays) // 2
    both = [(a.shape[0], a.shape[1] + b.shape[1]) for a, b in zip(arrays[:half], arrays[half:])]
    return pl.pallas_call(
        functools.partial(unit_kernel, len(arrays)),
        out_shape=[jax.ShapeDtypeStruct(a.shape, bf16) for a in arrays]
        + [jax.ShapeDtypeStruct(shape, bf16) for shape in both],
        in_specs=[ANY] * len(arrays),
        out_specs=[VMEM] * (len(arrays) + half),
        scratch_shapes=[pltpu.VMEM(a.shape, bf16) for a in arrays]
        + [pltpu.SemaphoreType.DMA((len(arrays),))],
        compiler_params=pltpu.CompilerParams(vmem_limit_bytes=int(60 * 2**20)),
        cost_estimate=pl.CostEstimate(
            flops=4 * sum(a.size for a in arrays),
            bytes_accessed=6 * sum(a.size for a in arrays),
            transcendentals=0,
        ),
        name="unit_rows",
    )(*arrays)


def pack(refs, target, columns):
    rows, width = refs[0].shape[0], target.shape[1]
    for k, ref in enumerate(refs):
        first = columns if ref.shape[1] != width else 0
        target[k * rows : (k + 1) * rows, :] = ref[:, first : first + width]


def teacher_kernel(images, texts, *refs):
    img_refs, txt_refs = refs[:images], refs[images : images + texts]
    p_ref, img, txt = refs[images + texts :]
    rows = img_refs[0].shape[0]
    pack(img_refs, img, 0)
    pack(txt_refs, txt, 0)
    step = tile_rows(texts * rows, 256)

    def one(j, carry):
        at = pl.ds(pl.multiple_of(j * step, step), step)
        dots = lax.dot_general(img[...], txt[at, :], (((1,), (1,)), ((), ())), preferred_element_type=f32)
        p_ref[:, at] = jax.nn.sigmoid(logit_scale * dots + logit_bias)
        return carry

    lax.fori_loop(0, texts * rows // step, one, 0)
    own = lax.broadcasted_iota(jnp.int32, (rows, rows), 0) == lax.broadcasted_iota(jnp.int32, (rows, rows), 1)
    p_ref[:rows, :rows] = p_ref[:rows, :rows] + jnp.where(own, 1.0, 0.0).astype(f32)


def teacher_targets(img_blocks, txt_blocks):
    images, texts = len(img_blocks), len(txt_blocks)
    rows, width = img_blocks[0].shape
    return pl.pallas_call(
        functools.partial(teacher_kernel, images, texts),
        out_shape=jax.ShapeDtypeStruct((images * rows, texts * rows), f32),
        in_specs=[VMEM] * (images + texts),
        out_specs=VMEM,
        scratch_shapes=[
            pltpu.VMEM((images * rows, width), bf16),
            pltpu.VMEM((texts * rows, width), bf16),
        ],
        compiler_params=params(((images + texts, rows, width), 2), ((images, rows, texts, rows), 4), *[(v.shape, 2) for v in (*img_blocks, *txt_blocks)]),
        cost_estimate=pl.CostEstimate(
            flops=2 * images * texts * rows * rows * width,
            bytes_accessed=2 * (images + texts) * rows * width + 4 * images * texts * rows * rows,
            transcendentals=images * texts * rows * rows,
        ),
        name="teacher_targets",
    )(*img_blocks, *txt_blocks)


def image_grads(pair, txt, rows, first, count):
    part = lax.dot_general(
        pair[first * rows : (first + count) * rows, :], txt, (((1,), (0,)), ((), ())), preferred_element_type=f32
    )
    return [part[k * rows : (k + 1) * rows, :] for k in range(count)]


def text_grads(pair, img, rows, first, count):
    part = lax.dot_general(
        pair[:, first * rows : (first + count) * rows], img, (((0,), (0,)), ((), ())), preferred_element_type=f32
    )
    return [part[k * rows : (k + 1) * rows, :] for k in range(count)]


def pair_kernel(images, texts, far, skip, half, own_txt, *refs):
    img_refs, txt_refs = refs[:images], refs[images : images + texts]
    p_ref, pair_ref, img, txt = refs[images + texts : images + texts + 4]
    outs = list(refs[images + texts + 4 :])
    rows, col = img_refs[0].shape[0], images // far
    pack(img_refs, img, skip)
    pack(txt_refs, txt, skip)
    step = tile_rows(texts * rows, 256)
    for j in range(texts * rows // step):
        at = slice(j * step, (j + 1) * step)
        dots = lax.dot_general(img[...], txt[at, :], (((1,), (1,)), ((), ())), preferred_element_type=f32)
        pair_ref[:, at] = (2.0 * jax.nn.sigmoid(logit_scale * dots + logit_bias) - p_ref[:, at]).astype(bf16)
    others = image_grads(pair_ref, txt[...], rows, far, far * (col - 1)) if col > 1 else []
    hops = [outs.pop(0) for _ in range(far * (col - 1))]
    kept = [outs.pop(0) for _ in range(col - 1)]
    longs = [outs.pop(0) for _ in range(far - 1)]
    for k, grad in enumerate(others):
        b, a = 1 + k // far, k % far
        hops[k][...] = grad[:, :half].astype(bf16)
        if a:
            longs[a - 1][b * rows : (b + 1) * rows, :] = grad[:, half:].astype(bf16)
        else:
            kept[b - 1][...] = grad[:, half:]
    if far > 1:
        for a, grad in enumerate(image_grads(pair_ref, txt[:, half:], rows, 1, far - 1)):
            longs[a][:rows, :] = grad.astype(bf16)
    if outs:
        count = outs[0].shape[0] // rows
        grads = text_grads(pair_ref, img[...], rows, own_txt, len(outs) * count)
        for k, grad in enumerate(grads):
            outs[k // count][(k % count) * rows : (k % count + 1) * rows, :] = grad.astype(bf16)


def pair_and_sent(img_blocks, txt_blocks, far, near, own_txt, skip, half, targets):
    images, texts = len(img_blocks), len(txt_blocks)
    rows, width = img_blocks[-1].shape
    col = images // far
    shapes = [((images * rows, texts * rows), bf16), ((images * rows, width), bf16), ((texts * rows, width), bf16)]
    shapes += [((rows, half), bf16)] * (far * (col - 1))
    shapes += [((rows, width - half), f32)] * (col - 1)
    shapes += [((col * rows, width - half), bf16)] * (far - 1)
    shapes += [((near * rows, width), bf16)] * ((texts - own_txt) // near)
    out = pl.pallas_call(
        functools.partial(pair_kernel, images, texts, far, skip, half, own_txt),
        out_shape=[jax.ShapeDtypeStruct(*shape) for shape in shapes],
        in_specs=[VMEM] * (images + texts + 1),
        out_specs=[VMEM] * len(shapes),
        compiler_params=params(
            ((images * rows, texts * rows), 6),
            ((images + texts, rows, width), 6),
            *[(v.shape, 2) for v in (*img_blocks, *txt_blocks)],
        ),
        cost_estimate=pl.CostEstimate(
            flops=4 * images * texts * rows * rows * width,
            bytes_accessed=2 * (images + texts) * rows * width + 8 * images * texts * rows * rows,
            transcendentals=images * texts * rows * rows,
        ),
        name="pair_and_sent",
    )(*img_blocks, *txt_blocks, targets)
    out = list(out)
    cut = [3, 3 + far * (col - 1), 3 + (far + 1) * (col - 1), 3 + (far + 1) * (col - 1) + far - 1]
    return out[:3], out[cut[0] : cut[1]], out[cut[1] : cut[2]], out[cut[2] : cut[3]], out[cut[3] :]


def kept_kernel(half, pair, img, txt, *outs):
    rows = outs[0].shape[0]
    far = len(outs) - 1
    outs[-1][...] = lax.dot_general(
        pair[:, : outs[-1].shape[0]], img[...], (((0,), (0,)), ((), ())), preferred_element_type=f32
    )
    for out, grad in zip(outs, image_grads(pair, txt[...], rows, 0, far)):
        out[...] = grad[:, : out.shape[1]]


def kept_grads(pair, img, txt, rows, far, own_txt, half):
    width = img.shape[1]
    shapes = [(rows, width)] + [(rows, half)] * (far - 1) + [(own_txt * rows, width)]
    return pl.pallas_call(
        functools.partial(kept_kernel, half),
        out_shape=[jax.ShapeDtypeStruct(shape, f32) for shape in shapes],
        in_specs=[VMEM] * 3,
        out_specs=[VMEM] * len(shapes),
        compiler_params=params((pair.shape, 2), (img.shape, 2), (txt.shape, 2), *[(v, 8) for v in shapes]),
        cost_estimate=pl.CostEstimate(
            flops=2 * pair.size * width,
            bytes_accessed=2 * (pair.size + img.size + txt.size) + 4 * own_txt * rows * width,
            transcendentals=0,
        ),
        name="kept",
    )(pair, img, txt)


def text_sums_kernel(row, near, half, cores, own_ref, *refs):
    arrived, outs = refs[: cores * row], list(refs[cores * row :])
    rows = own_ref.shape[0] // (row * near)
    hops = [outs.pop(0) for _ in range(near * (row - 1))]
    kept = [outs.pop(0) for _ in range(row - 1)]
    stay = [outs.pop(0) for _ in range(near)]
    for b in range(row):
        for a in range(near):
            k = b * near + a
            total = own_ref[k * rows : (k + 1) * rows, :]
            for c in range(cores):
                total = total + arrived[c * row + b][a * rows : (a + 1) * rows, :].astype(f32)
            if b:
                hops[(b - 1) * near + a][...] = total[:, :half].astype(bf16)
            else:
                stay[a][...] = total[:, : stay[a].shape[1]]
            if a:
                outs[a - 1][b * rows : (b + 1) * rows, :] = total[:, half:].astype(bf16)
            elif b:
                kept[b - 1][...] = total[:, half:]


def text_sums(own, arrived, rows, row, near, half):
    width = own.shape[1]
    shapes = [((rows, half), bf16)] * (near * (row - 1)) + [((rows, width - half), f32)] * (row - 1)
    shapes += [((rows, width), f32)] + [((rows, half), f32)] * (near - 1)
    shapes += [((row * rows, width - half), bf16)] * (near - 1)
    out = list(
        pl.pallas_call(
            functools.partial(text_sums_kernel, row, near, half, len(arrived) // row),
            out_shape=[jax.ShapeDtypeStruct(*shape) for shape in shapes],
            in_specs=[VMEM] * (1 + len(arrived)),
            out_specs=[VMEM] * len(shapes),
            compiler_params=params((own.shape, 16)),
            cost_estimate=pl.CostEstimate(flops=2 * own.size, bytes_accessed=10 * own.size, transcendentals=0),
            name="text_sums",
        )(own, *arrived)
    )
    cut = [near * (row - 1), (near + 1) * (row - 1), (near + 1) * (row - 1) + near]
    return out[: cut[0]], out[cut[0] : cut[1]], out[cut[1] : cut[2]], out[cut[2] :]


def final_kernel(half, lows, x_ref, own_ref, *refs):
    parts, out_ref = refs[:-1], refs[-1]
    rows = x_ref.shape[0]
    x = x_ref[...].astype(f32)
    inverse = 1.0 / jnp.sqrt(jnp.sum(x * x, axis=1, keepdims=True) + epsilon)
    sides, along = [], 0.0
    for at, refs_at in ((slice(0, half), parts[:lows]), (slice(half, None), parts[lows:])):
        unit = x[:, at] * inverse
        grad = own_ref[:, at]
        for part in refs_at:
            grad = grad + part[:rows, :].astype(f32)
        grad = logit_scale * grad
        along = along + jnp.sum(unit * grad, axis=1, keepdims=True)
        sides.append((at, unit, grad))
    for at, unit, grad in sides:
        out_ref[:, at] = (grad - unit * along) * inverse


def final(x, own, lows, highs, half):
    operands = [x, own, *lows, *highs]
    return pl.pallas_call(
        functools.partial(final_kernel, half, len(lows)),
        out_shape=jax.ShapeDtypeStruct(x.shape, f32),
        in_specs=[VMEM] * len(operands),
        out_specs=VMEM,
        compiler_params=params((x.shape, 4 * (4 + len(operands)))),
        cost_estimate=pl.CostEstimate(flops=10 * x.size, bytes_accessed=12 * x.size, transcendentals=0),
        name="final",
    )(*operands)


def token_kernel(*refs):
    refs[-1][...] = jnp.zeros_like(refs[-1])


def token(*arrays, flops):
    return pl.pallas_call(
        token_kernel,
        out_shape=jax.ShapeDtypeStruct((8, 128), f32),
        in_specs=[ANY] * len(arrays),
        out_specs=VMEM,
        cost_estimate=pl.CostEstimate(flops=flops, bytes_accessed=0, transcendentals=0),
        name="token",
    )(*arrays)


def after(x, *others):
    others = [v for other in others for v in (other.values() if isinstance(other, dict) else [other])]
    return lax.optimization_barrier((x, *others))[0] if others else x


def body(plan, student_img, student_txt, teacher_img, teacher_txt):
    rows, width = student_img.shape
    far, near, core, row, col = (plan[k] for k in plan.order)

    def spread(x, name, *before):
        return {a: plan.send(after(x, *before), name, a) for a in range(1, plan[name])}

    def onward(blocks, name, *before):
        return {
            (b, a): plan.send(after(x, *before), name, b) for b in range(1, plan[name]) for a, x in blocks.items()
        }

    t_img, t_txt, s_img, s_txt, b_img, b_txt = unit_rows(teacher_img, teacher_txt, student_img, student_txt)
    t_far = spread(t_img, "far")
    t_near = spread(t_txt, "near")
    b_col = spread(b_img, "col")
    b_row = spread(b_txt, "row")
    b_core = spread(b_txt, "core")
    first = [b_col, b_row, b_core]
    teacher_z = token(*t_far.values(), *t_near.values(), flops=10000000000)
    s_far = spread(s_img, "far", teacher_z)
    s_near = spread(s_txt, "near", teacher_z)
    t_far_col = onward(t_far, "col", *first)
    t_near_row = onward(t_near, "row", *first)
    b_row_core = onward(b_row, "core", *first)
    second = [token(*s_far.values(), *s_near.values(), flops=10000000000), t_far_col, t_near_row, b_row_core]
    s_far_col = onward(s_far, "col", *second)
    s_near_row = onward(s_near, "row", *second)
    s_near_core = onward(s_near, "core", *second)
    t_near_core = onward(t_near, "core", *second)
    t_both_core = onward(t_near_row, "core", *second)

    def images(own, by_far, by_col, by_both):
        blocks = {(0, 0): own, **by_both}
        blocks.update({(0, a): x for a, x in by_far.items()})
        blocks.update({(b, 0): x for b, x in by_col.items()})
        return [blocks[b, a] for b in range(col) for a in range(far)]

    def texts(own, by_near, by_row, by_both, by_core, by_core_near, by_core_row, by_core_both):
        blocks = {(0, 0, 0): own}
        blocks.update({(0, 0, a): x for a, x in by_near.items()})
        blocks.update({(0, b, 0): x for b, x in by_row.items()})
        blocks.update({(0, *key): x for key, x in by_both.items()})
        blocks.update({(c, 0, 0): x for c, x in by_core.items()})
        blocks.update({(c, 0, a): x for (c, a), x in by_core_near.items()})
        blocks.update({(c, b, 0): x for (c, b), x in by_core_row.items()})
        blocks.update({(c, *key): x for (c, key), x in by_core_both.items()})
        return [blocks[c, b, a] for c in range(core) for b in range(row) for a in range(near)]

    targets = teacher_targets(
        images(t_img, t_far, b_col, t_far_col),
        texts(t_txt, t_near, b_row, t_near_row, b_core, t_near_core, b_row_core, t_both_core),
    )
    s_both_core = onward(s_near_row, "core", s_near_core, targets)
    s_imgs = images(s_img, s_far, b_col, s_far_col)
    s_txts = texts(s_txt, s_near, b_row, s_near_row, b_core, s_near_core, b_row_core, s_both_core)

    own_txt = row * near
    half = width // 128 * 2 // 3 * 128
    skip = teacher_img.shape[1]
    packed, img_hops, img_kept, img_longs, txt_out = pair_and_sent(
        s_imgs, s_txts, far, near, own_txt, skip, half, targets
    )
    pair, img_pack, txt_pack = packed
    img_in = {}
    for b in range(1, col):
        for a in range(1, far):
            img_in[b, a] = plan.send(img_hops[(b - 1) * far + a], "col", -b)
    long_in = [plan.send(v, "far", -1 - k) for k, v in enumerate(img_longs)]
    txt_in = [plan.send(v, "core", -1 - k // row) for k, v in enumerate(txt_out)]
    *img_stay, txt_own = kept_grads(pair, img_pack, txt_pack, rows, far, own_txt, half)
    txt_hops, txt_kept, txt_stay, txt_longs = text_sums(txt_own, txt_in, rows, row, near, half)

    row_in = {}
    for b in range(1, row):
        for a in range(1, near):
            row_in[b, a] = plan.send(txt_hops[(b - 1) * near + a], "row", -b)
    txt_long_in = [plan.send(v, "near", -1 - k) for k, v in enumerate(txt_longs)]

    def total(own, arrived):
        for v in arrived:
            own = own + v.astype(f32)
        return own.astype(bf16)

    img_last = [
        plan.send(total(after(img_stay[a], *txt_hops, *txt_longs), [img_in[b, a] for b in range(1, col)]), "far", -a) for a in range(1, far)
    ]
    txt_last = [
        plan.send(total(txt_stay[a], [row_in[b, a] for b in range(1, row)]), "near", -a) for a in range(1, near)
    ]
    img_side = [
        plan.send(total(after(img_kept[b - 1], *[*txt_long_in, *row_in.values()]), [v[b * rows : (b + 1) * rows] for v in long_in]), "col", -b)
        for b in range(1, col)
    ]
    txt_side = [
        plan.send(total(after(txt_kept[b - 1], *row_in.values()), [v[b * rows : (b + 1) * rows] for v in txt_long_in]), "row", -b)
        for b in range(1, row)
    ]
    col_ahead = list(row_in.values())
    row_ahead = list(img_in.values())
    img_ends = [plan.send(after(img_hops[(b - 1) * far], *col_ahead), "col", -b) for b in range(1, col)]
    txt_ends = [plan.send(after(txt_hops[(b - 1) * near], *row_ahead), "row", -b) for b in range(1, row)]
    image_grad = final(student_img, img_stay[0], img_ends + img_last, img_side + long_in, half)
    text_grad = final(student_txt, txt_stay[0], txt_ends + txt_last, txt_side + txt_long_in, half)
    return image_grad, text_grad


def solution(mesh):
    spec = P(AXES, None)
    return jax.shard_map(
        functools.partial(body, Plan(mesh)), mesh=mesh, in_specs=(spec,) * 4, out_specs=(spec,) * 2, check_vma=False
    )
```

```python
import functools
import math
import jax
import jax.numpy as jnp
from jax import lax
from jax.experimental import pallas as pl
from jax.experimental.pallas import tpu as pltpu
from jax.sharding import PartitionSpec as P

epsilon = 1e-06
logit_scale = 100.0
logit_bias = -4.0

AXES = ("blk", "narrow")
ANY = pl.BlockSpec(memory_space=pl.ANY)
VMEM = pl.BlockSpec(memory_space=pltpu.VMEM)
f32 = jnp.float32
bf16 = jnp.bfloat16


def split_two(size):
    fast = int(size**0.5)
    while size % fast:
        fast -= 1
    return max(fast, size // fast), min(fast, size // fast)


class Plan:
    def __init__(self, mesh):
        blk, narrow = mesh.shape["blk"], mesh.shape["narrow"]
        core = 2 if blk % 2 == 0 else 1
        far, near = split_two(blk // core)
        large, small = split_two(narrow)
        self.digits = {"far": far, "near": near, "core": core, "row": small, "col": large}
        self.order = ["far", "near", "core", "row", "col"]

    def __getitem__(self, name):
        return self.digits[name]

    def place(self, index):
        out = {}
        for name in reversed(self.order):
            out[name] = index % self.digits[name]
            index //= self.digits[name]
        return out

    def index(self, place):
        out = 0
        for name in self.order:
            out = out * self.digits[name] + place[name]
        return out

    def send(self, x, name, by):
        total = 1
        for size in self.digits.values():
            total *= size
        pairs = []
        for src in range(total):
            place = self.place(src)
            place[name] = (place[name] + by) % self.digits[name]
            pairs.append((src, self.index(place)))
        return lax.ppermute(x, AXES, pairs)


def params(*held):
    total = sum(math.prod(shape) * size for shape, size in held)
    return pltpu.CompilerParams(vmem_limit_bytes=int(total) + 8 * 2**20)


def tile_rows(rows, most):
    step = most
    while rows % step:
        step //= 2
    return step


def load_all(refs, targets, sems, columns=None):
    copies = []
    for k, (ref, target) in enumerate(zip(refs, targets)):
        if columns is not None and ref.shape[1] != target.shape[1]:
            ref = ref.at[:, pl.ds(columns, target.shape[1])]
        copies.append(pltpu.make_async_copy(ref, target, sems.at[k]))
        copies[-1].start()
    return copies


def unit_kernel(count, *refs):
    x_refs, out_refs, both_refs = refs[:count], refs[count : 2 * count], refs[2 * count : 2 * count + count // 2]
    held, sems = refs[2 * count + count // 2 : -1], refs[-1]
    copies = load_all(x_refs, held, sems)
    for k, (copy, x_ref, out_ref) in enumerate(zip(copies, held, out_refs)):
        copy.wait()
        x = x_ref[...].astype(f32)
        scale = 1.0 / jnp.sqrt(jnp.sum(x * x, axis=1, keepdims=True) + epsilon)
        unit = (x * scale).astype(bf16)
        out_ref[...] = unit
        both, width = both_refs[k % (count // 2)], x.shape[1]
        if k < count // 2:
            both[:, :width] = unit
        else:
            both[:, both.shape[1] - width :] = unit


def unit_rows(*arrays):
    half = len(arrays) // 2
    both = [(a.shape[0], a.shape[1] + b.shape[1]) for a, b in zip(arrays[:half], arrays[half:])]
    return pl.pallas_call(
        functools.partial(unit_kernel, len(arrays)),
        out_shape=[jax.ShapeDtypeStruct(a.shape, bf16) for a in arrays]
        + [jax.ShapeDtypeStruct(shape, bf16) for shape in both],
        in_specs=[ANY] * len(arrays),
        out_specs=[VMEM] * (len(arrays) + half),
        scratch_shapes=[pltpu.VMEM(a.shape, bf16) for a in arrays]
        + [pltpu.SemaphoreType.DMA((len(arrays),))],
        compiler_params=pltpu.CompilerParams(vmem_limit_bytes=int(60 * 2**20)),
        cost_estimate=pl.CostEstimate(
            flops=4 * sum(a.size for a in arrays),
            bytes_accessed=6 * sum(a.size for a in arrays),
            transcendentals=0,
        ),
        name="unit_rows",
    )(*arrays)


def pack(refs, target, columns):
    rows, width = refs[0].shape[0], target.shape[1]
    for k, ref in enumerate(refs):
        first = columns if ref.shape[1] != width else 0
        target[k * rows : (k + 1) * rows, :] = ref[:, first : first + width]


def teacher_kernel(images, texts, *refs):
    img_refs, txt_refs = refs[:images], refs[images : images + texts]
    p_ref, img, txt = refs[images + texts :]
    rows = img_refs[0].shape[0]
    pack(img_refs, img, 0)
    pack(txt_refs, txt, 0)
    step = tile_rows(texts * rows, 256)

    def one(j, carry):
        at = pl.ds(pl.multiple_of(j * step, step), step)
        dots = lax.dot_general(img[...], txt[at, :], (((1,), (1,)), ((), ())), preferred_element_type=f32)
        p_ref[:, at] = jax.nn.sigmoid(logit_scale * dots + logit_bias)
        return carry

    lax.fori_loop(0, texts * rows // step, one, 0)
    own = lax.broadcasted_iota(jnp.int32, (rows, rows), 0) == lax.broadcasted_iota(jnp.int32, (rows, rows), 1)
    p_ref[:rows, :rows] = p_ref[:rows, :rows] + jnp.where(own, 1.0, 0.0).astype(f32)


def teacher_targets(img_blocks, txt_blocks):
    images, texts = len(img_blocks), len(txt_blocks)
    rows, width = img_blocks[0].shape
    return pl.pallas_call(
        functools.partial(teacher_kernel, images, texts),
        out_shape=jax.ShapeDtypeStruct((images * rows, texts * rows), f32),
        in_specs=[VMEM] * (images + texts),
        out_specs=VMEM,
        scratch_shapes=[
            pltpu.VMEM((images * rows, width), bf16),
            pltpu.VMEM((texts * rows, width), bf16),
        ],
        compiler_params=params(((images + texts, rows, width), 2), ((images, rows, texts, rows), 4), *[(v.shape, 2) for v in (*img_blocks, *txt_blocks)]),
        cost_estimate=pl.CostEstimate(
            flops=2 * images * texts * rows * rows * width,
            bytes_accessed=2 * (images + texts) * rows * width + 4 * images * texts * rows * rows,
            transcendentals=images * texts * rows * rows,
        ),
        name="teacher_targets",
    )(*img_blocks, *txt_blocks)


def image_grads(pair, txt, rows, first, count):
    part = lax.dot_general(
        pair[first * rows : (first + count) * rows, :], txt, (((1,), (0,)), ((), ())), preferred_element_type=f32
    )
    return [part[k * rows : (k + 1) * rows, :] for k in range(count)]


def text_grads(pair, img, rows, first, count):
    part = lax.dot_general(
        pair[:, first * rows : (first + count) * rows], img, (((0,), (0,)), ((), ())), preferred_element_type=f32
    )
    return [part[k * rows : (k + 1) * rows, :] for k in range(count)]


def pair_kernel(images, texts, far, skip, half, own_txt, *refs):
    img_refs, txt_refs = refs[:images], refs[images : images + texts]
    p_ref, pair_ref, img, txt = refs[images + texts : images + texts + 4]
    outs = list(refs[images + texts + 4 :])
    rows, col = img_refs[0].shape[0], images // far
    pack(img_refs, img, skip)
    pack(txt_refs, txt, skip)
    step = tile_rows(texts * rows, 256)
    for j in range(texts * rows // step):
        at = slice(j * step, (j + 1) * step)
        dots = lax.dot_general(img[...], txt[at, :], (((1,), (1,)), ((), ())), preferred_element_type=f32)
        pair_ref[:, at] = (2.0 * jax.nn.sigmoid(logit_scale * dots + logit_bias) - p_ref[:, at]).astype(bf16)
    others = image_grads(pair_ref, txt[...], rows, far, far * (col - 1)) if col > 1 else []
    hops = [outs.pop(0) for _ in range(far * (col - 1))]
    kept = [outs.pop(0) for _ in range(col - 1)]
    longs = [outs.pop(0) for _ in range(far - 1)]
    for k, grad in enumerate(others):
        b, a = 1 + k // far, k % far
        hops[k][...] = grad[:, :half].astype(bf16)
        if a:
            longs[a - 1][b * rows : (b + 1) * rows, :] = grad[:, half:].astype(bf16)
        else:
            kept[b - 1][...] = grad[:, half:]
    if far > 1:
        for a, grad in enumerate(image_grads(pair_ref, txt[:, half:], rows, 1, far - 1)):
            longs[a][:rows, :] = grad.astype(bf16)
    if outs:
        count = outs[0].shape[0] // rows
        grads = text_grads(pair_ref, img[...], rows, own_txt, len(outs) * count)
        for k, grad in enumerate(grads):
            outs[k // count][(k % count) * rows : (k % count + 1) * rows, :] = grad.astype(bf16)


def pair_and_sent(img_blocks, txt_blocks, far, near, own_txt, skip, half, targets):
    images, texts = len(img_blocks), len(txt_blocks)
    rows, width = img_blocks[-1].shape
    col = images // far
    shapes = [((images * rows, texts * rows), bf16), ((images * rows, width), bf16), ((texts * rows, width), bf16)]
    shapes += [((rows, half), bf16)] * (far * (col - 1))
    shapes += [((rows, width - half), f32)] * (col - 1)
    shapes += [((col * rows, width - half), bf16)] * (far - 1)
    shapes += [((near * rows, width), bf16)] * ((texts - own_txt) // near)
    out = pl.pallas_call(
        functools.partial(pair_kernel, images, texts, far, skip, half, own_txt),
        out_shape=[jax.ShapeDtypeStruct(*shape) for shape in shapes],
        in_specs=[VMEM] * (images + texts + 1),
        out_specs=[VMEM] * len(shapes),
        compiler_params=params(
            ((images * rows, texts * rows), 6),
            ((images + texts, rows, width), 6),
            *[(v.shape, 2) for v in (*img_blocks, *txt_blocks)],
        ),
        cost_estimate=pl.CostEstimate(
            flops=4 * images * texts * rows * rows * width,
            bytes_accessed=2 * (images + texts) * rows * width + 8 * images * texts * rows * rows,
            transcendentals=images * texts * rows * rows,
        ),
        name="pair_and_sent",
    )(*img_blocks, *txt_blocks, targets)
    out = list(out)
    cut = [3, 3 + far * (col - 1), 3 + (far + 1) * (col - 1), 3 + (far + 1) * (col - 1) + far - 1]
    return out[:3], out[cut[0] : cut[1]], out[cut[1] : cut[2]], out[cut[2] : cut[3]], out[cut[3] :]


def kept_kernel(of_texts, pair, other, *outs):
    rows = outs[0].shape[0]
    if of_texts:
        outs[0][...] = lax.dot_general(
            pair[:, :rows], other[...], (((0,), (0,)), ((), ())), preferred_element_type=f32
        )
    else:
        for out, grad in zip(outs, image_grads(pair, other[...], rows, 0, len(outs))):
            out[...] = grad[:, : out.shape[1]]


def kept_grads(pair, other, shapes, of_texts):
    return pl.pallas_call(
        functools.partial(kept_kernel, of_texts),
        out_shape=[jax.ShapeDtypeStruct(shape, f32) for shape in shapes],
        in_specs=[VMEM] * 2,
        out_specs=[VMEM] * len(shapes),
        compiler_params=params((pair.shape, 2), (other.shape, 2), *[(v, 8) for v in shapes]),
        cost_estimate=pl.CostEstimate(
            flops=pair.size * other.shape[1],
            bytes_accessed=2 * (pair.size + other.size) + 4 * sum(math.prod(v) for v in shapes),
            transcendentals=0,
        ),
        name="kept_texts" if of_texts else "kept_images",
    )(pair, other)


def text_sums_kernel(row, near, half, cores, own_ref, *refs):
    arrived, outs = refs[: cores * row], list(refs[cores * row :])
    rows = own_ref.shape[0] // (row * near)
    hops = [outs.pop(0) for _ in range(near * (row - 1))]
    kept = [outs.pop(0) for _ in range(row - 1)]
    stay = [outs.pop(0) for _ in range(near)]
    for b in range(row):
        for a in range(near):
            k = b * near + a
            total = own_ref[k * rows : (k + 1) * rows, :]
            for c in range(cores):
                total = total + arrived[c * row + b][a * rows : (a + 1) * rows, :].astype(f32)
            if b:
                hops[(b - 1) * near + a][...] = total[:, :half].astype(bf16)
            else:
                stay[a][...] = total[:, : stay[a].shape[1]]
            if a:
                outs[a - 1][b * rows : (b + 1) * rows, :] = total[:, half:].astype(bf16)
            elif b:
                kept[b - 1][...] = total[:, half:]


def text_sums(own, arrived, rows, row, near, half):
    width = own.shape[1]
    shapes = [((rows, half), bf16)] * (near * (row - 1)) + [((rows, width - half), f32)] * (row - 1)
    shapes += [((rows, width), f32)] + [((rows, half), f32)] * (near - 1)
    shapes += [((row * rows, width - half), bf16)] * (near - 1)
    out = list(
        pl.pallas_call(
            functools.partial(text_sums_kernel, row, near, half, len(arrived) // row),
            out_shape=[jax.ShapeDtypeStruct(*shape) for shape in shapes],
            in_specs=[VMEM] * (1 + len(arrived)),
            out_specs=[VMEM] * len(shapes),
            compiler_params=params((own.shape, 16)),
            cost_estimate=pl.CostEstimate(flops=2 * own.size, bytes_accessed=10 * own.size, transcendentals=0),
            name="text_sums",
        )(own, *arrived)
    )
    cut = [near * (row - 1), (near + 1) * (row - 1), (near + 1) * (row - 1) + near]
    return out[: cut[0]], out[cut[0] : cut[1]], out[cut[1] : cut[2]], out[cut[2] :]


def final_kernel(half, lows, x_ref, own_ref, *refs):
    parts, out_ref = refs[:-1], refs[-1]
    rows = x_ref.shape[0]
    x = x_ref[...].astype(f32)
    inverse = 1.0 / jnp.sqrt(jnp.sum(x * x, axis=1, keepdims=True) + epsilon)
    sides, along = [], 0.0
    for at, refs_at in ((slice(0, half), parts[:lows]), (slice(half, None), parts[lows:])):
        unit = x[:, at] * inverse
        grad = own_ref[:, at]
        for part in refs_at:
            grad = grad + part[:rows, :].astype(f32)
        grad = logit_scale * grad
        along = along + jnp.sum(unit * grad, axis=1, keepdims=True)
        sides.append((at, unit, grad))
    for at, unit, grad in sides:
        out_ref[:, at] = (grad - unit * along) * inverse


def final(x, own, lows, highs, half):
    operands = [x, own, *lows, *highs]
    return pl.pallas_call(
        functools.partial(final_kernel, half, len(lows)),
        out_shape=jax.ShapeDtypeStruct(x.shape, f32),
        in_specs=[VMEM] * len(operands),
        out_specs=VMEM,
        compiler_params=params((x.shape, 4 * (4 + len(operands)))),
        cost_estimate=pl.CostEstimate(flops=10 * x.size, bytes_accessed=12 * x.size, transcendentals=0),
        name="final",
    )(*operands)


def token_kernel(*refs):
    refs[-1][...] = jnp.zeros_like(refs[-1])


def token(*arrays, flops):
    return pl.pallas_call(
        token_kernel,
        out_shape=jax.ShapeDtypeStruct((8, 128), f32),
        in_specs=[ANY] * len(arrays),
        out_specs=VMEM,
        cost_estimate=pl.CostEstimate(flops=flops, bytes_accessed=0, transcendentals=0),
        name="token",
    )(*arrays)


def after(x, *others):
    others = [v for other in others for v in (other.values() if isinstance(other, dict) else [other])]
    return lax.optimization_barrier((x, *others))[0] if others else x


def body(plan, student_img, student_txt, teacher_img, teacher_txt):
    rows, width = student_img.shape
    far, near, core, row, col = (plan[k] for k in plan.order)

    def spread(x, name, *before):
        return {a: plan.send(after(x, *before), name, a) for a in range(1, plan[name])}

    def onward(blocks, name, *before):
        return {
            (b, a): plan.send(after(x, *before), name, b) for b in range(1, plan[name]) for a, x in blocks.items()
        }

    t_img, t_txt, s_img, s_txt, b_img, b_txt = unit_rows(teacher_img, teacher_txt, student_img, student_txt)
    t_far = spread(t_img, "far")
    t_near = spread(t_txt, "near")
    b_col = spread(b_img, "col")
    b_row = spread(b_txt, "row")
    b_core = spread(b_txt, "core")
    first = [b_col, b_row, b_core]
    teacher_z = token(*t_far.values(), *t_near.values(), flops=10000000000)
    s_far = spread(s_img, "far", teacher_z)
    s_near = spread(s_txt, "near", teacher_z)
    t_far_col = onward(t_far, "col", *first)
    t_near_row = onward(t_near, "row", *first)
    b_row_core = onward(b_row, "core", *first)
    second = [token(*s_far.values(), *s_near.values(), flops=10000000000), t_far_col, t_near_row, b_row_core]
    s_far_col = onward(s_far, "col", *second)
    s_near_row = onward(s_near, "row", *second)
    s_near_core = onward(s_near, "core", *second)
    t_near_core = onward(t_near, "core", *second)
    t_both_core = onward(t_near_row, "core", *second)

    def images(own, by_far, by_col, by_both):
        blocks = {(0, 0): own, **by_both}
        blocks.update({(0, a): x for a, x in by_far.items()})
        blocks.update({(b, 0): x for b, x in by_col.items()})
        return [blocks[b, a] for b in range(col) for a in range(far)]

    def texts(own, by_near, by_row, by_both, by_core, by_core_near, by_core_row, by_core_both):
        blocks = {(0, 0, 0): own}
        blocks.update({(0, 0, a): x for a, x in by_near.items()})
        blocks.update({(0, b, 0): x for b, x in by_row.items()})
        blocks.update({(0, *key): x for key, x in by_both.items()})
        blocks.update({(c, 0, 0): x for c, x in by_core.items()})
        blocks.update({(c, 0, a): x for (c, a), x in by_core_near.items()})
        blocks.update({(c, b, 0): x for (c, b), x in by_core_row.items()})
        blocks.update({(c, *key): x for (c, key), x in by_core_both.items()})
        return [blocks[c, b, a] for c in range(core) for b in range(row) for a in range(near)]

    targets = teacher_targets(
        images(t_img, t_far, b_col, t_far_col),
        texts(t_txt, t_near, b_row, t_near_row, b_core, t_near_core, b_row_core, t_both_core),
    )
    s_both_core = onward(s_near_row, "core", s_near_core, targets)
    s_imgs = images(s_img, s_far, b_col, s_far_col)
    s_txts = texts(s_txt, s_near, b_row, s_near_row, b_core, s_near_core, b_row_core, s_both_core)

    own_txt = row * near
    half = width // 128 * 2 // 3 * 128
    skip = teacher_img.shape[1]
    packed, img_hops, img_kept, img_longs, txt_out = pair_and_sent(
        s_imgs, s_txts, far, near, own_txt, skip, half, targets
    )
    pair, img_pack, txt_pack = packed
    img_in = {}
    for b in range(1, col):
        for a in range(1, far):
            img_in[b, a] = plan.send(img_hops[(b - 1) * far + a], "col", -b)
    long_in = [plan.send(v, "far", -1 - k) for k, v in enumerate(img_longs)]
    txt_in = [plan.send(v, "core", -1 - k // row) for k, v in enumerate(txt_out)]
    (txt_own,) = kept_grads(pair, img_pack, [(own_txt * rows, width)], True)
    txt_hops, txt_kept, txt_stay, txt_longs = text_sums(txt_own, txt_in, rows, row, near, half)
    img_stay = kept_grads(after(pair, *txt_hops), txt_pack, [(rows, width)] + [(rows, half)] * (far - 1), False)

    row_in = {}
    for b in range(1, row):
        for a in range(1, near):
            row_in[b, a] = plan.send(txt_hops[(b - 1) * near + a], "row", -b)
    txt_long_in = [plan.send(v, "near", -1 - k) for k, v in enumerate(txt_longs)]

    def total(own, arrived):
        for v in arrived:
            own = own + v.astype(f32)
        return own.astype(bf16)

    img_last = [
        plan.send(total(after(img_stay[a], *txt_hops, *txt_longs), [img_in[b, a] for b in range(1, col)]), "far", -a) for a in range(1, far)
    ]
    txt_last = [
        plan.send(total(txt_stay[a], [row_in[b, a] for b in range(1, row)]), "near", -a) for a in range(1, near)
    ]
    img_side = [
        plan.send(total(after(img_kept[b - 1], *row_in.values()), [v[b * rows : (b + 1) * rows] for v in long_in]), "col", -b)
        for b in range(1, col)
    ]
    txt_side = [
        plan.send(total(txt_kept[b - 1], [v[b * rows : (b + 1) * rows] for v in txt_long_in]), "row", -b)
        for b in range(1, row)
    ]
    col_ahead = list(row_in.values())
    row_ahead = list(img_in.values())
    img_ends = [plan.send(after(img_hops[(b - 1) * far], *col_ahead), "col", -b) for b in range(1, col)]
    txt_ends = [plan.send(after(txt_hops[(b - 1) * near], *row_ahead), "row", -b) for b in range(1, row)]
    image_grad = final(student_img, img_stay[0], img_ends + img_last, img_side + long_in, half)
    text_grad = final(student_txt, txt_stay[0], txt_ends + txt_last, txt_side + txt_long_in, half)
    return image_grad, text_grad


def solution(mesh):
    spec = P(AXES, None)
    return jax.shard_map(
        functools.partial(body, Plan(mesh)), mesh=mesh, in_specs=(spec,) * 4, out_specs=(spec,) * 2, check_vma=False
    )
```

```python
import functools
import math
import jax
import jax.numpy as jnp
from jax import lax
from jax.experimental import pallas as pl
from jax.experimental.pallas import tpu as pltpu
from jax.sharding import PartitionSpec as P

epsilon = 1e-06
logit_scale = 100.0
logit_bias = -4.0

AXES = ("blk", "narrow")
ANY = pl.BlockSpec(memory_space=pl.ANY)
VMEM = pl.BlockSpec(memory_space=pltpu.VMEM)
f32 = jnp.float32
bf16 = jnp.bfloat16


def split_two(size):
    fast = int(size**0.5)
    while size % fast:
        fast -= 1
    return max(fast, size // fast), min(fast, size // fast)


class Plan:
    def __init__(self, mesh):
        blk, narrow = mesh.shape["blk"], mesh.shape["narrow"]
        core = 2 if blk % 2 == 0 else 1
        far, near = split_two(blk // core)
        large, small = split_two(narrow)
        self.digits = {"far": far, "near": near, "core": core, "row": small, "col": large}
        self.order = ["far", "near", "core", "row", "col"]

    def __getitem__(self, name):
        return self.digits[name]

    def place(self, index):
        out = {}
        for name in reversed(self.order):
            out[name] = index % self.digits[name]
            index //= self.digits[name]
        return out

    def index(self, place):
        out = 0
        for name in self.order:
            out = out * self.digits[name] + place[name]
        return out

    def send(self, x, name, by):
        total = 1
        for size in self.digits.values():
            total *= size
        pairs = []
        for src in range(total):
            place = self.place(src)
            place[name] = (place[name] + by) % self.digits[name]
            pairs.append((src, self.index(place)))
        return lax.ppermute(x, AXES, pairs)


def params(*held):
    total = sum(math.prod(shape) * size for shape, size in held)
    return pltpu.CompilerParams(vmem_limit_bytes=int(total) + 8 * 2**20)


def tile_rows(rows, most):
    step = most
    while rows % step:
        step //= 2
    return step


def load_all(refs, targets, sems, columns=None):
    copies = []
    for k, (ref, target) in enumerate(zip(refs, targets)):
        if columns is not None and ref.shape[1] != target.shape[1]:
            ref = ref.at[:, pl.ds(columns, target.shape[1])]
        copies.append(pltpu.make_async_copy(ref, target, sems.at[k]))
        copies[-1].start()
    return copies


def unit_kernel(count, *refs):
    x_refs, out_refs, both_refs = refs[:count], refs[count : 2 * count], refs[2 * count : 2 * count + count // 2]
    held, sems = refs[2 * count + count // 2 : -1], refs[-1]
    copies = load_all(x_refs, held, sems)
    for k, (copy, x_ref, out_ref) in enumerate(zip(copies, held, out_refs)):
        copy.wait()
        x = x_ref[...].astype(f32)
        scale = 1.0 / jnp.sqrt(jnp.sum(x * x, axis=1, keepdims=True) + epsilon)
        unit = (x * scale).astype(bf16)
        out_ref[...] = unit
        both, width = both_refs[k % (count // 2)], x.shape[1]
        if k < count // 2:
            both[:, :width] = unit
        else:
            both[:, both.shape[1] - width :] = unit


def unit_rows(*arrays):
    half = len(arrays) // 2
    both = [(a.shape[0], a.shape[1] + b.shape[1]) for a, b in zip(arrays[:half], arrays[half:])]
    return pl.pallas_call(
        functools.partial(unit_kernel, len(arrays)),
        out_shape=[jax.ShapeDtypeStruct(a.shape, bf16) for a in arrays]
        + [jax.ShapeDtypeStruct(shape, bf16) for shape in both],
        in_specs=[ANY] * len(arrays),
        out_specs=[VMEM] * (len(arrays) + half),
        scratch_shapes=[pltpu.VMEM(a.shape, bf16) for a in arrays]
        + [pltpu.SemaphoreType.DMA((len(arrays),))],
        compiler_params=pltpu.CompilerParams(vmem_limit_bytes=int(60 * 2**20)),
        cost_estimate=pl.CostEstimate(
            flops=4 * sum(a.size for a in arrays),
            bytes_accessed=6 * sum(a.size for a in arrays),
            transcendentals=0,
        ),
        name="unit_rows",
    )(*arrays)


def pack(refs, target, columns):
    rows, width = refs[0].shape[0], target.shape[1]
    for k, ref in enumerate(refs):
        first = columns if ref.shape[1] != width else 0
        target[k * rows : (k + 1) * rows, :] = ref[:, first : first + width]


def teacher_kernel(images, texts, *refs):
    img_refs, txt_refs = refs[:images], refs[images : images + texts]
    p_ref, img, txt = refs[images + texts :]
    rows = img_refs[0].shape[0]
    pack(img_refs, img, 0)
    pack(txt_refs, txt, 0)
    step = tile_rows(texts * rows, 256)

    def one(j, carry):
        at = pl.ds(pl.multiple_of(j * step, step), step)
        dots = lax.dot_general(img[...], txt[at, :], (((1,), (1,)), ((), ())), preferred_element_type=f32)
        p_ref[:, at] = jax.nn.sigmoid(logit_scale * dots + logit_bias)
        return carry

    lax.fori_loop(0, texts * rows // step, one, 0)
    own = lax.broadcasted_iota(jnp.int32, (rows, rows), 0) == lax.broadcasted_iota(jnp.int32, (rows, rows), 1)
    p_ref[:rows, :rows] = p_ref[:rows, :rows] + jnp.where(own, 1.0, 0.0).astype(f32)


def teacher_targets(img_blocks, txt_blocks):
    images, texts = len(img_blocks), len(txt_blocks)
    rows, width = img_blocks[0].shape
    return pl.pallas_call(
        functools.partial(teacher_kernel, images, texts),
        out_shape=jax.ShapeDtypeStruct((images * rows, texts * rows), f32),
        in_specs=[VMEM] * (images + texts),
        out_specs=VMEM,
        scratch_shapes=[
            pltpu.VMEM((images * rows, width), bf16),
            pltpu.VMEM((texts * rows, width), bf16),
        ],
        compiler_params=params(((images + texts, rows, width), 2), ((images, rows, texts, rows), 4), *[(v.shape, 2) for v in (*img_blocks, *txt_blocks)]),
        cost_estimate=pl.CostEstimate(
            flops=2 * images * texts * rows * rows * width,
            bytes_accessed=2 * (images + texts) * rows * width + 4 * images * texts * rows * rows,
            transcendentals=images * texts * rows * rows,
        ),
        name="teacher_targets",
    )(*img_blocks, *txt_blocks)


def image_grads(pair, txt, rows, first, count):
    part = lax.dot_general(
        pair[first * rows : (first + count) * rows, :], txt, (((1,), (0,)), ((), ())), preferred_element_type=f32
    )
    return [part[k * rows : (k + 1) * rows, :] for k in range(count)]


def text_grads(pair, img, rows, first, count):
    part = lax.dot_general(
        pair[:, first * rows : (first + count) * rows], img, (((0,), (0,)), ((), ())), preferred_element_type=f32
    )
    return [part[k * rows : (k + 1) * rows, :] for k in range(count)]


def pair_kernel(images, texts, far, skip, half, own_txt, *refs):
    img_refs, txt_refs = refs[:images], refs[images : images + texts]
    p_ref, pair_ref, img, txt = refs[images + texts : images + texts + 4]
    outs = list(refs[images + texts + 4 :])
    rows, col = img_refs[0].shape[0], images // far
    pack(img_refs, img, skip)
    pack(txt_refs, txt, skip)
    step = tile_rows(texts * rows, 256)
    for j in range(texts * rows // step):
        at = slice(j * step, (j + 1) * step)
        dots = lax.dot_general(img[...], txt[at, :], (((1,), (1,)), ((), ())), preferred_element_type=f32)
        pair_ref[:, at] = (2.0 * jax.nn.sigmoid(logit_scale * dots + logit_bias) - p_ref[:, at]).astype(bf16)
    others = image_grads(pair_ref, txt[...], rows, far, far * (col - 1)) if col > 1 else []
    hops = [outs.pop(0) for _ in range(far * (col - 1))]
    kept = [outs.pop(0) for _ in range(col - 1)]
    longs = [outs.pop(0) for _ in range(far - 1)]
    for k, grad in enumerate(others):
        b, a = 1 + k // far, k % far
        hops[k][...] = grad[:, :half].astype(bf16)
        if a:
            longs[a - 1][b * rows : (b + 1) * rows, :] = grad[:, half:].astype(bf16)
        else:
            kept[b - 1][...] = grad[:, half:]
    if far > 1:
        for a, grad in enumerate(image_grads(pair_ref, txt[:, half:], rows, 1, far - 1)):
            longs[a][:rows, :] = grad.astype(bf16)
    if outs:
        count = outs[0].shape[0] // rows
        grads = text_grads(pair_ref, img[...], rows, own_txt, len(outs) * count)
        for k, grad in enumerate(grads):
            outs[k // count][(k % count) * rows : (k % count + 1) * rows, :] = grad.astype(bf16)


def pair_and_sent(img_blocks, txt_blocks, far, near, own_txt, skip, half, targets):
    images, texts = len(img_blocks), len(txt_blocks)
    rows, width = img_blocks[-1].shape
    col = images // far
    shapes = [((images * rows, texts * rows), bf16), ((images * rows, width), bf16), ((texts * rows, width), bf16)]
    shapes += [((rows, half), bf16)] * (far * (col - 1))
    shapes += [((rows, width - half), f32)] * (col - 1)
    shapes += [((col * rows, width - half), bf16)] * (far - 1)
    shapes += [((near * rows, width), bf16)] * ((texts - own_txt) // near)
    out = pl.pallas_call(
        functools.partial(pair_kernel, images, texts, far, skip, half, own_txt),
        out_shape=[jax.ShapeDtypeStruct(*shape) for shape in shapes],
        in_specs=[VMEM] * (images + texts + 1),
        out_specs=[VMEM] * len(shapes),
        compiler_params=params(
            ((images * rows, texts * rows), 6),
            ((images + texts, rows, width), 6),
            *[(v.shape, 2) for v in (*img_blocks, *txt_blocks)],
        ),
        cost_estimate=pl.CostEstimate(
            flops=4 * images * texts * rows * rows * width,
            bytes_accessed=2 * (images + texts) * rows * width + 8 * images * texts * rows * rows,
            transcendentals=images * texts * rows * rows,
        ),
        name="pair_and_sent",
    )(*img_blocks, *txt_blocks, targets)
    out = list(out)
    cut = [3, 3 + far * (col - 1), 3 + (far + 1) * (col - 1), 3 + (far + 1) * (col - 1) + far - 1]
    return out[:3], out[cut[0] : cut[1]], out[cut[1] : cut[2]], out[cut[2] : cut[3]], out[cut[3] :]


def kept_kernel(half, pair, img, txt, *outs):
    rows = outs[0].shape[0]
    far = len(outs) - 1
    outs[-1][...] = lax.dot_general(
        pair[:, : outs[-1].shape[0]], img[...], (((0,), (0,)), ((), ())), preferred_element_type=f32
    )
    for out, grad in zip(outs, image_grads(pair, txt[...], rows, 0, far)):
        out[...] = grad[:, : out.shape[1]]


def kept_grads(pair, img, txt, rows, far, own_txt, half):
    width = img.shape[1]
    shapes = [(rows, width)] + [(rows, half)] * (far - 1) + [(own_txt * rows, width)]
    return pl.pallas_call(
        functools.partial(kept_kernel, half),
        out_shape=[jax.ShapeDtypeStruct(shape, f32) for shape in shapes],
        in_specs=[VMEM] * 3,
        out_specs=[VMEM] * len(shapes),
        compiler_params=params((pair.shape, 2), (img.shape, 2), (txt.shape, 2), *[(v, 8) for v in shapes]),
        cost_estimate=pl.CostEstimate(
            flops=2 * pair.size * width,
            bytes_accessed=2 * (pair.size + img.size + txt.size) + 4 * own_txt * rows * width,
            transcendentals=0,
        ),
        name="kept",
    )(pair, img, txt)


def text_sums_kernel(row, near, half, cores, own_ref, *refs):
    arrived, outs = refs[: cores * row], list(refs[cores * row :])
    rows = own_ref.shape[0] // (row * near)
    hops = [outs.pop(0) for _ in range(near * (row - 1))]
    kept = [outs.pop(0) for _ in range(row - 1)]
    stay = [outs.pop(0) for _ in range(near)]
    for b in range(row):
        for a in range(near):
            k = b * near + a
            total = own_ref[k * rows : (k + 1) * rows, :]
            for c in range(cores):
                total = total + arrived[c * row + b][a * rows : (a + 1) * rows, :].astype(f32)
            if b:
                hops[(b - 1) * near + a][...] = total[:, :half].astype(bf16)
            else:
                stay[a][...] = total[:, : stay[a].shape[1]]
            if a:
                outs[a - 1][b * rows : (b + 1) * rows, :] = total[:, half:].astype(bf16)
            elif b:
                kept[b - 1][...] = total[:, half:]


def text_sums(own, arrived, rows, row, near, half):
    width = own.shape[1]
    shapes = [((rows, half), bf16)] * (near * (row - 1)) + [((rows, width - half), f32)] * (row - 1)
    shapes += [((rows, width), f32)] + [((rows, half), f32)] * (near - 1)
    shapes += [((row * rows, width - half), bf16)] * (near - 1)
    out = list(
        pl.pallas_call(
            functools.partial(text_sums_kernel, row, near, half, len(arrived) // row),
            out_shape=[jax.ShapeDtypeStruct(*shape) for shape in shapes],
            in_specs=[VMEM] * (1 + len(arrived)),
            out_specs=[VMEM] * len(shapes),
            compiler_params=params((own.shape, 16)),
            cost_estimate=pl.CostEstimate(flops=2 * own.size, bytes_accessed=10 * own.size, transcendentals=0),
            name="text_sums",
        )(own, *arrived)
    )
    cut = [near * (row - 1), (near + 1) * (row - 1), (near + 1) * (row - 1) + near]
    return out[: cut[0]], out[cut[0] : cut[1]], out[cut[1] : cut[2]], out[cut[2] :]


def final_kernel(half, counts, *refs):
    outs = refs[-len(counts) :]
    for (lows, highs), out_ref in zip(counts, outs):
        x_ref, own_ref, parts = refs[0], refs[1], refs[2 : 2 + lows + highs]
        refs = refs[2 + lows + highs :]
        rows = x_ref.shape[0]
        x = x_ref[...].astype(f32)
        inverse = 1.0 / jnp.sqrt(jnp.sum(x * x, axis=1, keepdims=True) + epsilon)
        sides, along = [], 0.0
        for at, refs_at in ((slice(0, half), parts[:lows]), (slice(half, None), parts[lows:])):
            unit = x[:, at] * inverse
            grad = own_ref[:, at]
            for part in refs_at:
                grad = grad + part[:rows, :].astype(f32)
            grad = logit_scale * grad
            along = along + jnp.sum(unit * grad, axis=1, keepdims=True)
            sides.append((at, unit, grad))
        for at, unit, grad in sides:
            out_ref[:, at] = (grad - unit * along) * inverse


def final(half, *sides):
    operands = [v for x, own, lows, highs in sides for v in (x, own, *lows, *highs)]
    return pl.pallas_call(
        functools.partial(final_kernel, half, tuple((len(lows), len(highs)) for _, _, lows, highs in sides)),
        out_shape=[jax.ShapeDtypeStruct(side[0].shape, f32) for side in sides],
        in_specs=[VMEM] * len(operands),
        out_specs=[VMEM] * len(sides),
        compiler_params=params(*[(v.shape, 8) for v in operands]),
        cost_estimate=pl.CostEstimate(
            flops=10 * sum(side[0].size for side in sides),
            bytes_accessed=12 * sum(side[0].size for side in sides),
            transcendentals=0,
        ),
        name="final",
    )(*operands)


def token_kernel(*refs):
    refs[-1][...] = jnp.zeros_like(refs[-1])


def token(*arrays, flops):
    return pl.pallas_call(
        token_kernel,
        out_shape=jax.ShapeDtypeStruct((8, 128), f32),
        in_specs=[ANY] * len(arrays),
        out_specs=VMEM,
        cost_estimate=pl.CostEstimate(flops=flops, bytes_accessed=0, transcendentals=0),
        name="token",
    )(*arrays)


def after(x, *others):
    others = [v for other in others for v in (other.values() if isinstance(other, dict) else [other])]
    return lax.optimization_barrier((x, *others))[0] if others else x


def body(plan, student_img, student_txt, teacher_img, teacher_txt):
    rows, width = student_img.shape
    far, near, core, row, col = (plan[k] for k in plan.order)

    def spread(x, name, *before):
        return {a: plan.send(after(x, *before), name, a) for a in range(1, plan[name])}

    def onward(blocks, name, *before):
        return {
            (b, a): plan.send(after(x, *before), name, b) for b in range(1, plan[name]) for a, x in blocks.items()
        }

    t_img, t_txt, s_img, s_txt, b_img, b_txt = unit_rows(teacher_img, teacher_txt, student_img, student_txt)
    t_far = spread(t_img, "far")
    t_near = spread(t_txt, "near")
    b_col = spread(b_img, "col")
    b_row = spread(b_txt, "row")
    b_core = spread(b_txt, "core")
    first = [b_col, b_row, b_core]
    teacher_z = token(*t_far.values(), *t_near.values(), flops=10000000000)
    s_far = spread(s_img, "far", teacher_z)
    s_near = spread(s_txt, "near", teacher_z)
    t_far_col = onward(t_far, "col", *first)
    t_near_row = onward(t_near, "row", *first)
    b_row_core = onward(b_row, "core", *first)
    second = [token(*s_far.values(), *s_near.values(), flops=10000000000), t_far_col, t_near_row, b_row_core]
    s_far_col = onward(s_far, "col", *second)
    s_near_row = onward(s_near, "row", *second)
    s_near_core = onward(s_near, "core", *second)
    t_near_core = onward(t_near, "core", *second)
    t_both_core = onward(t_near_row, "core", *second)

    def images(own, by_far, by_col, by_both):
        blocks = {(0, 0): own, **by_both}
        blocks.update({(0, a): x for a, x in by_far.items()})
        blocks.update({(b, 0): x for b, x in by_col.items()})
        return [blocks[b, a] for b in range(col) for a in range(far)]

    def texts(own, by_near, by_row, by_both, by_core, by_core_near, by_core_row, by_core_both):
        blocks = {(0, 0, 0): own}
        blocks.update({(0, 0, a): x for a, x in by_near.items()})
        blocks.update({(0, b, 0): x for b, x in by_row.items()})
        blocks.update({(0, *key): x for key, x in by_both.items()})
        blocks.update({(c, 0, 0): x for c, x in by_core.items()})
        blocks.update({(c, 0, a): x for (c, a), x in by_core_near.items()})
        blocks.update({(c, b, 0): x for (c, b), x in by_core_row.items()})
        blocks.update({(c, *key): x for (c, key), x in by_core_both.items()})
        return [blocks[c, b, a] for c in range(core) for b in range(row) for a in range(near)]

    targets = teacher_targets(
        images(t_img, t_far, b_col, t_far_col),
        texts(t_txt, t_near, b_row, t_near_row, b_core, t_near_core, b_row_core, t_both_core),
    )
    s_both_core = onward(s_near_row, "core", s_near_core, targets)
    s_imgs = images(s_img, s_far, b_col, s_far_col)
    s_txts = texts(s_txt, s_near, b_row, s_near_row, b_core, s_near_core, b_row_core, s_both_core)

    own_txt = row * near
    half = width // 128 * 2 // 3 * 128
    skip = teacher_img.shape[1]
    packed, img_hops, img_kept, img_longs, txt_out = pair_and_sent(
        s_imgs, s_txts, far, near, own_txt, skip, half, targets
    )
    pair, img_pack, txt_pack = packed
    img_in = {}
    for b in range(1, col):
        for a in range(1, far):
            img_in[b, a] = plan.send(img_hops[(b - 1) * far + a], "col", -b)
    long_in = [plan.send(v, "far", -1 - k) for k, v in enumerate(img_longs)]
    txt_in = [plan.send(v, "core", -1 - k // row) for k, v in enumerate(txt_out)]
    *img_stay, txt_own = kept_grads(pair, img_pack, txt_pack, rows, far, own_txt, half)
    txt_hops, txt_kept, txt_stay, txt_longs = text_sums(txt_own, txt_in, rows, row, near, half)

    row_in = {}
    for b in range(1, row):
        for a in range(1, near):
            row_in[b, a] = plan.send(txt_hops[(b - 1) * near + a], "row", -b)
    txt_long_in = [plan.send(v, "near", -1 - k) for k, v in enumerate(txt_longs)]

    def total(own, arrived):
        for v in arrived:
            own = own + v.astype(f32)
        return own.astype(bf16)

    img_last = [
        plan.send(total(after(img_stay[a], *txt_hops, *txt_longs), [img_in[b, a] for b in range(1, col)]), "far", -a) for a in range(1, far)
    ]
    txt_last = [
        plan.send(total(txt_stay[a], [row_in[b, a] for b in range(1, row)]), "near", -a) for a in range(1, near)
    ]
    img_side = [
        plan.send(total(after(img_kept[b - 1], *[*txt_long_in, *row_in.values()]), [v[b * rows : (b + 1) * rows] for v in long_in]), "col", -b)
        for b in range(1, col)
    ]
    txt_side = [
        plan.send(total(after(txt_kept[b - 1], *row_in.values()), [v[b * rows : (b + 1) * rows] for v in txt_long_in]), "row", -b)
        for b in range(1, row)
    ]
    col_ahead = list(row_in.values())
    row_ahead = list(img_in.values())
    img_ends = [plan.send(after(img_hops[(b - 1) * far], *col_ahead), "col", -b) for b in range(1, col)]
    txt_ends = [plan.send(after(txt_hops[(b - 1) * near], *row_ahead), "row", -b) for b in range(1, row)]
    image_side = (student_img, img_stay[0], img_ends + img_last, img_side + long_in)
    text_side = (student_txt, txt_stay[0], txt_ends + txt_last, txt_side + txt_long_in)
    return tuple(final(half, image_side, text_side))


def solution(mesh):
    spec = P(AXES, None)
    return jax.shard_map(
        functools.partial(body, Plan(mesh)), mesh=mesh, in_specs=(spec,) * 4, out_specs=(spec,) * 2, check_vma=False
    )
```

```python
import functools
import math
import jax
import jax.numpy as jnp
from jax import lax
from jax.experimental import pallas as pl
from jax.experimental.pallas import tpu as pltpu
from jax.sharding import PartitionSpec as P

epsilon = 1e-06
logit_scale = 100.0
logit_bias = -4.0

AXES = ("blk", "narrow")
ANY = pl.BlockSpec(memory_space=pl.ANY)
VMEM = pl.BlockSpec(memory_space=pltpu.VMEM)
f32 = jnp.float32
bf16 = jnp.bfloat16


def split_two(size):
    fast = int(size**0.5)
    while size % fast:
        fast -= 1
    return max(fast, size // fast), min(fast, size // fast)


class Plan:
    def __init__(self, mesh):
        blk, narrow = mesh.shape["blk"], mesh.shape["narrow"]
        core = 2 if blk % 2 == 0 else 1
        far, near = split_two(blk // core)
        large, small = split_two(narrow)
        self.digits = {"far": far, "near": near, "core": core, "row": small, "col": large}
        self.order = ["far", "near", "core", "row", "col"]

    def __getitem__(self, name):
        return self.digits[name]

    def place(self, index):
        out = {}
        for name in reversed(self.order):
            out[name] = index % self.digits[name]
            index //= self.digits[name]
        return out

    def index(self, place):
        out = 0
        for name in self.order:
            out = out * self.digits[name] + place[name]
        return out

    def send(self, x, name, by):
        total = 1
        for size in self.digits.values():
            total *= size
        pairs = []
        for src in range(total):
            place = self.place(src)
            place[name] = (place[name] + by) % self.digits[name]
            pairs.append((src, self.index(place)))
        return lax.ppermute(x, AXES, pairs)


def params(*held):
    total = sum(math.prod(shape) * size for shape, size in held)
    return pltpu.CompilerParams(vmem_limit_bytes=int(total) + 8 * 2**20)


def tile_rows(rows, most):
    step = most
    while rows % step:
        step //= 2
    return step


def load_all(refs, targets, sems, columns=None):
    copies = []
    for k, (ref, target) in enumerate(zip(refs, targets)):
        if columns is not None and ref.shape[1] != target.shape[1]:
            ref = ref.at[:, pl.ds(columns, target.shape[1])]
        copies.append(pltpu.make_async_copy(ref, target, sems.at[k]))
        copies[-1].start()
    return copies


def unit_kernel(count, *refs):
    x_refs, out_refs, both_refs = refs[:count], refs[count : 2 * count], refs[2 * count : 2 * count + count // 2]
    held, sems = refs[2 * count + count // 2 : -1], refs[-1]
    copies = load_all(x_refs, held, sems)
    for k, (copy, x_ref, out_ref) in enumerate(zip(copies, held, out_refs)):
        copy.wait()
        x = x_ref[...].astype(f32)
        scale = 1.0 / jnp.sqrt(jnp.sum(x * x, axis=1, keepdims=True) + epsilon)
        unit = (x * scale).astype(bf16)
        out_ref[...] = unit
        both, width = both_refs[k % (count // 2)], x.shape[1]
        if k < count // 2:
            both[:, :width] = unit
        else:
            both[:, both.shape[1] - width :] = unit


def unit_rows(*arrays):
    half = len(arrays) // 2
    both = [(a.shape[0], a.shape[1] + b.shape[1]) for a, b in zip(arrays[:half], arrays[half:])]
    return pl.pallas_call(
        functools.partial(unit_kernel, len(arrays)),
        out_shape=[jax.ShapeDtypeStruct(a.shape, bf16) for a in arrays]
        + [jax.ShapeDtypeStruct(shape, bf16) for shape in both],
        in_specs=[ANY] * len(arrays),
        out_specs=[VMEM] * (len(arrays) + half),
        scratch_shapes=[pltpu.VMEM(a.shape, bf16) for a in arrays]
        + [pltpu.SemaphoreType.DMA((len(arrays),))],
        compiler_params=pltpu.CompilerParams(vmem_limit_bytes=int(60 * 2**20)),
        cost_estimate=pl.CostEstimate(
            flops=4 * sum(a.size for a in arrays),
            bytes_accessed=6 * sum(a.size for a in arrays),
            transcendentals=0,
        ),
        name="unit_rows",
    )(*arrays)


def pack(refs, target, columns):
    rows, width = refs[0].shape[0], target.shape[1]
    for k, ref in enumerate(refs):
        first = columns if ref.shape[1] != width else 0
        target[k * rows : (k + 1) * rows, :] = ref[:, first : first + width]


def teacher_kernel(images, texts, *refs):
    img_refs, txt_refs = refs[:images], refs[images : images + texts]
    p_ref, img, txt = refs[images + texts :]
    rows = img_refs[0].shape[0]
    pack(img_refs, img, 0)
    pack(txt_refs, txt, 0)
    step = tile_rows(texts * rows, 256)

    def one(j, carry):
        at = pl.ds(pl.multiple_of(j * step, step), step)
        dots = lax.dot_general(img[...], txt[at, :], (((1,), (1,)), ((), ())), preferred_element_type=f32)
        p_ref[:, at] = jax.nn.sigmoid(logit_scale * dots + logit_bias)
        return carry

    lax.fori_loop(0, texts * rows // step, one, 0)
    own = lax.broadcasted_iota(jnp.int32, (rows, rows), 0) == lax.broadcasted_iota(jnp.int32, (rows, rows), 1)
    p_ref[:rows, :rows] = p_ref[:rows, :rows] + jnp.where(own, 1.0, 0.0).astype(f32)


def teacher_targets(img_blocks, txt_blocks):
    images, texts = len(img_blocks), len(txt_blocks)
    rows, width = img_blocks[0].shape
    return pl.pallas_call(
        functools.partial(teacher_kernel, images, texts),
        out_shape=jax.ShapeDtypeStruct((images * rows, texts * rows), f32),
        in_specs=[VMEM] * (images + texts),
        out_specs=VMEM,
        scratch_shapes=[
            pltpu.VMEM((images * rows, width), bf16),
            pltpu.VMEM((texts * rows, width), bf16),
        ],
        compiler_params=params(((images + texts, rows, width), 2), ((images, rows, texts, rows), 4), *[(v.shape, 2) for v in (*img_blocks, *txt_blocks)]),
        cost_estimate=pl.CostEstimate(
            flops=2 * images * texts * rows * rows * width,
            bytes_accessed=2 * (images + texts) * rows * width + 4 * images * texts * rows * rows,
            transcendentals=images * texts * rows * rows,
        ),
        name="teacher_targets",
    )(*img_blocks, *txt_blocks)


def image_grads(pair, txt, rows, first, count):
    part = lax.dot_general(
        pair[first * rows : (first + count) * rows, :], txt, (((1,), (0,)), ((), ())), preferred_element_type=f32
    )
    return [part[k * rows : (k + 1) * rows, :] for k in range(count)]


def text_grads(pair, img, rows, first, count):
    part = lax.dot_general(
        pair[:, first * rows : (first + count) * rows], img, (((0,), (0,)), ((), ())), preferred_element_type=f32
    )
    return [part[k * rows : (k + 1) * rows, :] for k in range(count)]


def pair_kernel(images, texts, far, skip, half, own_txt, *refs):
    img_refs, txt_refs = refs[:images], refs[images : images + texts]
    p_ref, pair_ref, img, txt = refs[images + texts : images + texts + 4]
    outs = list(refs[images + texts + 4 :])
    rows, col = img_refs[0].shape[0], images // far
    pack(img_refs, img, skip)
    pack(txt_refs, txt, skip)
    step = tile_rows(texts * rows, 256)
    for j in range(texts * rows // step):
        at = slice(j * step, (j + 1) * step)
        dots = lax.dot_general(img[...], txt[at, :], (((1,), (1,)), ((), ())), preferred_element_type=f32)
        pair_ref[:, at] = (2.0 * jax.nn.sigmoid(logit_scale * dots + logit_bias) - p_ref[:, at]).astype(bf16)
    others = image_grads(pair_ref, txt[...], rows, far, far * (col - 1)) if col > 1 else []
    hops = [outs.pop(0) for _ in range(far * (col - 1))]
    kept = [outs.pop(0) for _ in range(col - 1)]
    longs = [outs.pop(0) for _ in range(far - 1)]
    for k, grad in enumerate(others):
        b, a = 1 + k // far, k % far
        hops[k][...] = grad[:, :half].astype(bf16)
        if a:
            longs[a - 1][b * rows : (b + 1) * rows, :] = grad[:, half:].astype(bf16)
        else:
            kept[b - 1][...] = grad[:, half:]
    if far > 1:
        for a, grad in enumerate(image_grads(pair_ref, txt[:, half:], rows, 1, far - 1)):
            longs[a][:rows, :] = grad.astype(bf16)
    if outs:
        count = outs[0].shape[0] // rows
        grads = text_grads(pair_ref, img[...], rows, own_txt, len(outs) * count)
        for k, grad in enumerate(grads):
            outs[k // count][(k % count) * rows : (k % count + 1) * rows, :] = grad.astype(bf16)


def pair_and_sent(img_blocks, txt_blocks, far, near, own_txt, skip, half, targets):
    images, texts = len(img_blocks), len(txt_blocks)
    rows, width = img_blocks[-1].shape
    col = images // far
    shapes = [((images * rows, texts * rows), bf16), ((images * rows, width), bf16), ((texts * rows, width), bf16)]
    shapes += [((rows, half), bf16)] * (far * (col - 1))
    shapes += [((rows, width - half), f32)] * (col - 1)
    shapes += [((col * rows, width - half), bf16)] * (far - 1)
    shapes += [((near * rows, width), bf16)] * ((texts - own_txt) // near)
    out = pl.pallas_call(
        functools.partial(pair_kernel, images, texts, far, skip, half, own_txt),
        out_shape=[jax.ShapeDtypeStruct(*shape) for shape in shapes],
        in_specs=[VMEM] * (images + texts + 1),
        out_specs=[VMEM] * len(shapes),
        compiler_params=params(
            ((images * rows, texts * rows), 6),
            ((images + texts, rows, width), 6),
            *[(v.shape, 2) for v in (*img_blocks, *txt_blocks)],
        ),
        cost_estimate=pl.CostEstimate(
            flops=4 * images * texts * rows * rows * width,
            bytes_accessed=2 * (images + texts) * rows * width + 8 * images * texts * rows * rows,
            transcendentals=images * texts * rows * rows,
        ),
        name="pair_and_sent",
    )(*img_blocks, *txt_blocks, targets)
    out = list(out)
    cut = [3, 3 + far * (col - 1), 3 + (far + 1) * (col - 1), 3 + (far + 1) * (col - 1) + far - 1]
    return out[:3], out[cut[0] : cut[1]], out[cut[1] : cut[2]], out[cut[2] : cut[3]], out[cut[3] :]


def kept_kernel(of_texts, pair, other, *outs):
    rows = outs[0].shape[0]
    if of_texts:
        outs[0][...] = lax.dot_general(
            pair[:, :rows], other[...], (((0,), (0,)), ((), ())), preferred_element_type=f32
        )
    else:
        for out, grad in zip(outs, image_grads(pair, other[...], rows, 0, len(outs))):
            out[...] = grad[:, : out.shape[1]]


def kept_grads(pair, other, shapes, of_texts):
    return pl.pallas_call(
        functools.partial(kept_kernel, of_texts),
        out_shape=[jax.ShapeDtypeStruct(shape, f32) for shape in shapes],
        in_specs=[VMEM] * 2,
        out_specs=[VMEM] * len(shapes),
        compiler_params=params((pair.shape, 2), (other.shape, 2), *[(v, 8) for v in shapes]),
        cost_estimate=pl.CostEstimate(
            flops=pair.size * other.shape[1],
            bytes_accessed=2 * (pair.size + other.size) + 4 * sum(math.prod(v) for v in shapes),
            transcendentals=0,
        ),
        name="kept_texts" if of_texts else "kept_images",
    )(pair, other)


def text_sums_kernel(row, near, half, cores, own_ref, *refs):
    arrived, outs = refs[: cores * row], list(refs[cores * row :])
    rows = own_ref.shape[0] // (row * near)
    hops = [outs.pop(0) for _ in range(near * (row - 1))]
    kept = [outs.pop(0) for _ in range(row - 1)]
    stay = [outs.pop(0) for _ in range(near)]
    for b in range(row):
        for a in range(near):
            k = b * near + a
            total = own_ref[k * rows : (k + 1) * rows, :]
            for c in range(cores):
                total = total + arrived[c * row + b][a * rows : (a + 1) * rows, :].astype(f32)
            if b:
                hops[(b - 1) * near + a][...] = total[:, :half].astype(bf16)
            else:
                stay[a][...] = total[:, : stay[a].shape[1]]
            if a:
                outs[a - 1][b * rows : (b + 1) * rows, :] = total[:, half:].astype(bf16)
            elif b:
                kept[b - 1][...] = total[:, half:]


def text_sums(own, arrived, rows, row, near, half):
    width = own.shape[1]
    shapes = [((rows, half), bf16)] * (near * (row - 1)) + [((rows, width - half), f32)] * (row - 1)
    shapes += [((rows, width), f32)] + [((rows, half), f32)] * (near - 1)
    shapes += [((row * rows, width - half), bf16)] * (near - 1)
    out = list(
        pl.pallas_call(
            functools.partial(text_sums_kernel, row, near, half, len(arrived) // row),
            out_shape=[jax.ShapeDtypeStruct(*shape) for shape in shapes],
            in_specs=[VMEM] * (1 + len(arrived)),
            out_specs=[VMEM] * len(shapes),
            compiler_params=params((own.shape, 16)),
            cost_estimate=pl.CostEstimate(flops=2 * own.size, bytes_accessed=10 * own.size, transcendentals=0),
            name="text_sums",
        )(own, *arrived)
    )
    cut = [near * (row - 1), (near + 1) * (row - 1), (near + 1) * (row - 1) + near]
    return out[: cut[0]], out[cut[0] : cut[1]], out[cut[1] : cut[2]], out[cut[2] :]


def final_kernel(half, counts, *refs):
    outs = refs[-len(counts) :]
    for (lows, highs), out_ref in zip(counts, outs):
        x_ref, own_ref, parts = refs[0], refs[1], refs[2 : 2 + lows + highs]
        refs = refs[2 + lows + highs :]
        rows = x_ref.shape[0]
        x = x_ref[...].astype(f32)
        inverse = 1.0 / jnp.sqrt(jnp.sum(x * x, axis=1, keepdims=True) + epsilon)
        sides, along = [], 0.0
        for at, refs_at in ((slice(0, half), parts[:lows]), (slice(half, None), parts[lows:])):
            unit = x[:, at] * inverse
            grad = own_ref[:, at]
            for part in refs_at:
                grad = grad + part[:rows, :].astype(f32)
            grad = logit_scale * grad
            along = along + jnp.sum(unit * grad, axis=1, keepdims=True)
            sides.append((at, unit, grad))
        for at, unit, grad in sides:
            out_ref[:, at] = (grad - unit * along) * inverse


def final(half, *sides):
    operands = [v for x, own, lows, highs in sides for v in (x, own, *lows, *highs)]
    return pl.pallas_call(
        functools.partial(final_kernel, half, tuple((len(lows), len(highs)) for _, _, lows, highs in sides)),
        out_shape=[jax.ShapeDtypeStruct(side[0].shape, f32) for side in sides],
        in_specs=[VMEM] * len(operands),
        out_specs=[VMEM] * len(sides),
        compiler_params=params(*[(v.shape, 8) for v in operands]),
        cost_estimate=pl.CostEstimate(
            flops=10 * sum(side[0].size for side in sides),
            bytes_accessed=12 * sum(side[0].size for side in sides),
            transcendentals=0,
        ),
        name="final",
    )(*operands)


def token_kernel(*refs):
    refs[-1][...] = jnp.zeros_like(refs[-1])


def token(*arrays, flops):
    return pl.pallas_call(
        token_kernel,
        out_shape=jax.ShapeDtypeStruct((8, 128), f32),
        in_specs=[ANY] * len(arrays),
        out_specs=VMEM,
        cost_estimate=pl.CostEstimate(flops=flops, bytes_accessed=0, transcendentals=0),
        name="token",
    )(*arrays)


def after(x, *others):
    others = [v for other in others for v in (other.values() if isinstance(other, dict) else [other])]
    return lax.optimization_barrier((x, *others))[0] if others else x


def body(plan, student_img, student_txt, teacher_img, teacher_txt):
    rows, width = student_img.shape
    far, near, core, row, col = (plan[k] for k in plan.order)

    def spread(x, name, *before):
        return {a: plan.send(after(x, *before), name, a) for a in range(1, plan[name])}

    def onward(blocks, name, *before):
        return {
            (b, a): plan.send(after(x, *before), name, b) for b in range(1, plan[name]) for a, x in blocks.items()
        }

    t_img, t_txt, s_img, s_txt, b_img, b_txt = unit_rows(teacher_img, teacher_txt, student_img, student_txt)
    t_far = spread(t_img, "far")
    t_near = spread(t_txt, "near")
    b_col = spread(b_img, "col")
    b_row = spread(b_txt, "row")
    b_core = spread(b_txt, "core")
    first = [b_col, b_row, b_core]
    teacher_z = token(*t_far.values(), *t_near.values(), flops=10000000000)
    s_far = spread(s_img, "far", teacher_z)
    s_near = spread(s_txt, "near", teacher_z)
    t_far_col = onward(t_far, "col", *first)
    t_near_row = onward(t_near, "row", *first)
    b_row_core = onward(b_row, "core", *first)
    second = [token(*s_far.values(), *s_near.values(), flops=10000000000), t_far_col, t_near_row, b_row_core]
    s_far_col = onward(s_far, "col", *second)
    s_near_row = onward(s_near, "row", *second)
    s_near_core = onward(s_near, "core", *second)
    t_near_core = onward(t_near, "core", *second)
    t_both_core = onward(t_near_row, "core", *second)

    def images(own, by_far, by_col, by_both):
        blocks = {(0, 0): own, **by_both}
        blocks.update({(0, a): x for a, x in by_far.items()})
        blocks.update({(b, 0): x for b, x in by_col.items()})
        return [blocks[b, a] for b in range(col) for a in range(far)]

    def texts(own, by_near, by_row, by_both, by_core, by_core_near, by_core_row, by_core_both):
        blocks = {(0, 0, 0): own}
        blocks.update({(0, 0, a): x for a, x in by_near.items()})
        blocks.update({(0, b, 0): x for b, x in by_row.items()})
        blocks.update({(0, *key): x for key, x in by_both.items()})
        blocks.update({(c, 0, 0): x for c, x in by_core.items()})
        blocks.update({(c, 0, a): x for (c, a), x in by_core_near.items()})
        blocks.update({(c, b, 0): x for (c, b), x in by_core_row.items()})
        blocks.update({(c, *key): x for (c, key), x in by_core_both.items()})
        return [blocks[c, b, a] for c in range(core) for b in range(row) for a in range(near)]

    targets = teacher_targets(
        images(t_img, t_far, b_col, t_far_col),
        texts(t_txt, t_near, b_row, t_near_row, b_core, t_near_core, b_row_core, t_both_core),
    )
    s_both_core = onward(s_near_row, "core", s_near_core, targets)
    s_imgs = images(s_img, s_far, b_col, s_far_col)
    s_txts = texts(s_txt, s_near, b_row, s_near_row, b_core, s_near_core, b_row_core, s_both_core)

    own_txt = row * near
    half = width // 128 * 2 // 3 * 128
    skip = teacher_img.shape[1]
    packed, img_hops, img_kept, img_longs, txt_out = pair_and_sent(
        s_imgs, s_txts, far, near, own_txt, skip, half, targets
    )
    pair, img_pack, txt_pack = packed
    img_in = {}
    for b in range(1, col):
        for a in range(1, far):
            img_in[b, a] = plan.send(img_hops[(b - 1) * far + a], "col", -b)
    long_in = [plan.send(v, "far", -1 - k) for k, v in enumerate(img_longs)]
    txt_in = [plan.send(v, "core", -1 - k // row) for k, v in enumerate(txt_out)]
    (txt_own,) = kept_grads(pair, img_pack, [(own_txt * rows, width)], True)
    txt_hops, txt_kept, txt_stay, txt_longs = text_sums(txt_own, txt_in, rows, row, near, half)
    img_stay = kept_grads(pair, txt_pack, [(rows, width)] + [(rows, half)] * (far - 1), False)

    row_in = {}
    for b in range(1, row):
        for a in range(1, near):
            row_in[b, a] = plan.send(txt_hops[(b - 1) * near + a], "row", -b)
    txt_long_in = [plan.send(v, "near", -1 - k) for k, v in enumerate(txt_longs)]

    def total(own, arrived):
        for v in arrived:
            own = own + v.astype(f32)
        return own.astype(bf16)

    img_last = [
        plan.send(total(after(img_stay[a], *txt_hops, *txt_longs), [img_in[b, a] for b in range(1, col)]), "far", -a) for a in range(1, far)
    ]
    txt_last = [
        plan.send(total(txt_stay[a], [row_in[b, a] for b in range(1, row)]), "near", -a) for a in range(1, near)
    ]
    img_side = [
        plan.send(total(after(img_kept[b - 1], *row_in.values()), [v[b * rows : (b + 1) * rows] for v in long_in]), "col", -b)
        for b in range(1, col)
    ]
    txt_side = [
        plan.send(total(txt_kept[b - 1], [v[b * rows : (b + 1) * rows] for v in txt_long_in]), "row", -b)
        for b in range(1, row)
    ]
    col_ahead = list(row_in.values())
    row_ahead = list(img_in.values())
    img_ends = [plan.send(after(img_hops[(b - 1) * far], *col_ahead), "col", -b) for b in range(1, col)]
    txt_ends = [plan.send(after(txt_hops[(b - 1) * near], *row_ahead), "row", -b) for b in range(1, row)]
    image_side = (student_img, img_stay[0], img_ends + img_last, img_side + long_in)
    text_side = (student_txt, txt_stay[0], txt_ends + txt_last, txt_side + txt_long_in)
    return tuple(final(half, image_side, text_side))


def solution(mesh):
    spec = P(AXES, None)
    return jax.shard_map(
        functools.partial(body, Plan(mesh)), mesh=mesh, in_specs=(spec,) * 4, out_specs=(spec,) * 2, check_vma=False
    )
```

```python
import functools
import math
import jax
import jax.numpy as jnp
from jax import lax
from jax.experimental import pallas as pl
from jax.experimental.pallas import tpu as pltpu
from jax.sharding import PartitionSpec as P

epsilon = 1e-06
logit_scale = 100.0
logit_bias = -4.0

AXES = ("blk", "narrow")
ANY = pl.BlockSpec(memory_space=pl.ANY)
VMEM = pl.BlockSpec(memory_space=pltpu.VMEM)
f32 = jnp.float32
bf16 = jnp.bfloat16


def split_two(size):
    fast = int(size**0.5)
    while size % fast:
        fast -= 1
    return max(fast, size // fast), min(fast, size // fast)


class Plan:
    def __init__(self, mesh):
        blk, narrow = mesh.shape["blk"], mesh.shape["narrow"]
        core = 2 if blk % 2 == 0 else 1
        far, near = split_two(blk // core)
        large, small = split_two(narrow)
        self.digits = {"far": far, "near": near, "core": core, "row": small, "col": large}
        self.order = ["far", "near", "core", "row", "col"]

    def __getitem__(self, name):
        return self.digits[name]

    def place(self, index):
        out = {}
        for name in reversed(self.order):
            out[name] = index % self.digits[name]
            index //= self.digits[name]
        return out

    def index(self, place):
        out = 0
        for name in self.order:
            out = out * self.digits[name] + place[name]
        return out

    def send(self, x, name, by):
        total = 1
        for size in self.digits.values():
            total *= size
        pairs = []
        for src in range(total):
            place = self.place(src)
            place[name] = (place[name] + by) % self.digits[name]
            pairs.append((src, self.index(place)))
        return lax.ppermute(x, AXES, pairs)


def params(*held):
    total = sum(math.prod(shape) * size for shape, size in held)
    return pltpu.CompilerParams(vmem_limit_bytes=int(total) + 8 * 2**20)


def tile_rows(rows, most):
    step = most
    while rows % step:
        step //= 2
    return step


def load_all(refs, targets, sems, columns=None):
    copies = []
    for k, (ref, target) in enumerate(zip(refs, targets)):
        if columns is not None and ref.shape[1] != target.shape[1]:
            ref = ref.at[:, pl.ds(columns, target.shape[1])]
        copies.append(pltpu.make_async_copy(ref, target, sems.at[k]))
        copies[-1].start()
    return copies


def unit_kernel(count, *refs):
    x_refs, out_refs, both_refs = refs[:count], refs[count : 2 * count], refs[2 * count : 2 * count + count // 2]
    held, sems = refs[2 * count + count // 2 : -1], refs[-1]
    copies = load_all(x_refs, held, sems)
    for k, (copy, x_ref, out_ref) in enumerate(zip(copies, held, out_refs)):
        copy.wait()
        x = x_ref[...].astype(f32)
        scale = 1.0 / jnp.sqrt(jnp.sum(x * x, axis=1, keepdims=True) + epsilon)
        unit = (x * scale).astype(bf16)
        out_ref[...] = unit
        both, width = both_refs[k % (count // 2)], x.shape[1]
        if k < count // 2:
            both[:, :width] = unit
        else:
            both[:, both.shape[1] - width :] = unit


def unit_rows(*arrays):
    half = len(arrays) // 2
    both = [(a.shape[0], a.shape[1] + b.shape[1]) for a, b in zip(arrays[:half], arrays[half:])]
    return pl.pallas_call(
        functools.partial(unit_kernel, len(arrays)),
        out_shape=[jax.ShapeDtypeStruct(a.shape, bf16) for a in arrays]
        + [jax.ShapeDtypeStruct(shape, bf16) for shape in both],
        in_specs=[ANY] * len(arrays),
        out_specs=[VMEM] * (len(arrays) + half),
        scratch_shapes=[pltpu.VMEM(a.shape, bf16) for a in arrays]
        + [pltpu.SemaphoreType.DMA((len(arrays),))],
        compiler_params=pltpu.CompilerParams(vmem_limit_bytes=int(60 * 2**20)),
        cost_estimate=pl.CostEstimate(
            flops=4 * sum(a.size for a in arrays),
            bytes_accessed=6 * sum(a.size for a in arrays),
            transcendentals=0,
        ),
        name="unit_rows",
    )(*arrays)


def pack(refs, target, columns):
    rows, width = refs[0].shape[0], target.shape[1]
    for k, ref in enumerate(refs):
        first = columns if ref.shape[1] != width else 0
        target[k * rows : (k + 1) * rows, :] = ref[:, first : first + width]


def teacher_kernel(images, texts, *refs):
    img_refs, txt_refs = refs[:images], refs[images : images + texts]
    p_ref, img, txt = refs[images + texts :]
    rows = img_refs[0].shape[0]
    pack(img_refs, img, 0)
    pack(txt_refs, txt, 0)
    step = tile_rows(texts * rows, 256)

    def one(j, carry):
        at = pl.ds(pl.multiple_of(j * step, step), step)
        dots = lax.dot_general(img[...], txt[at, :], (((1,), (1,)), ((), ())), preferred_element_type=f32)
        p_ref[:, at] = jax.nn.sigmoid(logit_scale * dots + logit_bias)
        return carry

    lax.fori_loop(0, texts * rows // step, one, 0)
    own = lax.broadcasted_iota(jnp.int32, (rows, rows), 0) == lax.broadcasted_iota(jnp.int32, (rows, rows), 1)
    p_ref[:rows, :rows] = p_ref[:rows, :rows] + jnp.where(own, 1.0, 0.0).astype(f32)


def teacher_targets(img_blocks, txt_blocks):
    images, texts = len(img_blocks), len(txt_blocks)
    rows, width = img_blocks[0].shape
    return pl.pallas_call(
        functools.partial(teacher_kernel, images, texts),
        out_shape=jax.ShapeDtypeStruct((images * rows, texts * rows), f32),
        in_specs=[VMEM] * (images + texts),
        out_specs=VMEM,
        scratch_shapes=[
            pltpu.VMEM((images * rows, width), bf16),
            pltpu.VMEM((texts * rows, width), bf16),
        ],
        compiler_params=params(((images + texts, rows, width), 2), ((images, rows, texts, rows), 4), *[(v.shape, 2) for v in (*img_blocks, *txt_blocks)]),
        cost_estimate=pl.CostEstimate(
            flops=2 * images * texts * rows * rows * width,
            bytes_accessed=2 * (images + texts) * rows * width + 4 * images * texts * rows * rows,
            transcendentals=images * texts * rows * rows,
        ),
        name="teacher_targets",
    )(*img_blocks, *txt_blocks)


def image_grads(pair, txt, rows, first, count):
    part = lax.dot_general(
        pair[first * rows : (first + count) * rows, :], txt, (((1,), (0,)), ((), ())), preferred_element_type=f32
    )
    return [part[k * rows : (k + 1) * rows, :] for k in range(count)]


def text_grads(pair, img, rows, first, count):
    part = lax.dot_general(
        pair[:, first * rows : (first + count) * rows], img, (((0,), (0,)), ((), ())), preferred_element_type=f32
    )
    return [part[k * rows : (k + 1) * rows, :] for k in range(count)]


def pair_kernel(images, texts, far, skip, half, own_txt, *refs):
    img_refs, txt_refs = refs[:images], refs[images : images + texts]
    p_ref, pair_ref, img, txt = refs[images + texts : images + texts + 4]
    outs = list(refs[images + texts + 4 :])
    rows, col = img_refs[0].shape[0], images // far
    pack(img_refs, img, skip)
    pack(txt_refs, txt, skip)
    step = tile_rows(texts * rows, 256)
    for j in range(texts * rows // step):
        at = slice(j * step, (j + 1) * step)
        dots = lax.dot_general(img[...], txt[at, :], (((1,), (1,)), ((), ())), preferred_element_type=f32)
        pair_ref[:, at] = (2.0 * jax.nn.sigmoid(logit_scale * dots + logit_bias) - p_ref[:, at]).astype(bf16)
    others = image_grads(pair_ref, txt[...], rows, far, far * (col - 1)) if col > 1 else []
    hops = [outs.pop(0) for _ in range(far * (col - 1))]
    kept = [outs.pop(0) for _ in range(col - 1)]
    longs = [outs.pop(0) for _ in range(far - 1)]
    for k, grad in enumerate(others):
        b, a = 1 + k // far, k % far
        hops[k][...] = grad[:, :half].astype(bf16)
        if a:
            longs[a - 1][b * rows : (b + 1) * rows, :] = grad[:, half:].astype(bf16)
        else:
            kept[b - 1][...] = grad[:, half:]
    if far > 1:
        for a, grad in enumerate(image_grads(pair_ref, txt[:, half:], rows, 1, far - 1)):
            longs[a][:rows, :] = grad.astype(bf16)
    if outs:
        count = outs[0].shape[0] // rows
        grads = text_grads(pair_ref, img[...], rows, own_txt, len(outs) * count)
        for k, grad in enumerate(grads):
            outs[k // count][(k % count) * rows : (k % count + 1) * rows, :] = grad.astype(bf16)


def pair_and_sent(img_blocks, txt_blocks, far, near, own_txt, skip, half, targets):
    images, texts = len(img_blocks), len(txt_blocks)
    rows, width = img_blocks[-1].shape
    col = images // far
    shapes = [((images * rows, texts * rows), bf16), ((images * rows, width), bf16), ((texts * rows, width), bf16)]
    shapes += [((rows, half), bf16)] * (far * (col - 1))
    shapes += [((rows, width - half), f32)] * (col - 1)
    shapes += [((col * rows, width - half), bf16)] * (far - 1)
    shapes += [((near * rows, width), bf16)] * ((texts - own_txt) // near)
    out = pl.pallas_call(
        functools.partial(pair_kernel, images, texts, far, skip, half, own_txt),
        out_shape=[jax.ShapeDtypeStruct(*shape) for shape in shapes],
        in_specs=[VMEM] * (images + texts + 1),
        out_specs=[VMEM] * len(shapes),
        compiler_params=params(
            ((images * rows, texts * rows), 6),
            ((images + texts, rows, width), 6),
            *[(v.shape, 2) for v in (*img_blocks, *txt_blocks)],
        ),
        cost_estimate=pl.CostEstimate(
            flops=4 * images * texts * rows * rows * width,
            bytes_accessed=2 * (images + texts) * rows * width + 8 * images * texts * rows * rows,
            transcendentals=images * texts * rows * rows,
        ),
        name="pair_and_sent",
    )(*img_blocks, *txt_blocks, targets)
    out = list(out)
    cut = [3, 3 + far * (col - 1), 3 + (far + 1) * (col - 1), 3 + (far + 1) * (col - 1) + far - 1]
    return out[:3], out[cut[0] : cut[1]], out[cut[1] : cut[2]], out[cut[2] : cut[3]], out[cut[3] :]


def kept_kernel(half, pair, img, txt, *outs):
    rows = outs[0].shape[0]
    far = len(outs) - 1
    outs[-1][...] = lax.dot_general(
        pair[:, : outs[-1].shape[0]], img[...], (((0,), (0,)), ((), ())), preferred_element_type=f32
    )
    for out, grad in zip(outs, image_grads(pair, txt[...], rows, 0, far)):
        out[...] = grad[:, : out.shape[1]]


def kept_grads(pair, img, txt, rows, far, own_txt, half):
    width = img.shape[1]
    shapes = [(rows, width)] + [(rows, half)] * (far - 1) + [(own_txt * rows, width)]
    return pl.pallas_call(
        functools.partial(kept_kernel, half),
        out_shape=[jax.ShapeDtypeStruct(shape, f32) for shape in shapes],
        in_specs=[VMEM] * 3,
        out_specs=[VMEM] * len(shapes),
        compiler_params=params((pair.shape, 2), (img.shape, 2), (txt.shape, 2), *[(v, 8) for v in shapes]),
        cost_estimate=pl.CostEstimate(
            flops=2 * pair.size * width,
            bytes_accessed=2 * (pair.size + img.size + txt.size) + 4 * own_txt * rows * width,
            transcendentals=0,
        ),
        name="kept",
    )(pair, img, txt)


def text_sums_kernel(row, near, half, cores, own_ref, *refs):
    arrived, outs = refs[: cores * row], list(refs[cores * row :])
    rows = own_ref.shape[0] // (row * near)
    hops = [outs.pop(0) for _ in range(near * (row - 1))]
    kept = [outs.pop(0) for _ in range(row - 1)]
    stay = [outs.pop(0) for _ in range(near)]
    for b in range(row):
        for a in range(near):
            k = b * near + a
            total = own_ref[k * rows : (k + 1) * rows, :]
            for c in range(cores):
                total = total + arrived[c * row + b][a * rows : (a + 1) * rows, :].astype(f32)
            if b:
                hops[(b - 1) * near + a][...] = total[:, :half].astype(bf16)
            else:
                stay[a][...] = total[:, : stay[a].shape[1]]
            if a:
                outs[a - 1][b * rows : (b + 1) * rows, :] = total[:, half:].astype(bf16)
            elif b:
                kept[b - 1][...] = total[:, half:]


def text_sums(own, arrived, rows, row, near, half):
    width = own.shape[1]
    shapes = [((rows, half), bf16)] * (near * (row - 1)) + [((rows, width - half), f32)] * (row - 1)
    shapes += [((rows, width), f32)] + [((rows, half), f32)] * (near - 1)
    shapes += [((row * rows, width - half), bf16)] * (near - 1)
    out = list(
        pl.pallas_call(
            functools.partial(text_sums_kernel, row, near, half, len(arrived) // row),
            out_shape=[jax.ShapeDtypeStruct(*shape) for shape in shapes],
            in_specs=[VMEM] * (1 + len(arrived)),
            out_specs=[VMEM] * len(shapes),
            compiler_params=params((own.shape, 16)),
            cost_estimate=pl.CostEstimate(flops=2 * own.size, bytes_accessed=10 * own.size, transcendentals=0),
            name="text_sums",
        )(own, *arrived)
    )
    cut = [near * (row - 1), (near + 1) * (row - 1), (near + 1) * (row - 1) + near]
    return out[: cut[0]], out[cut[0] : cut[1]], out[cut[1] : cut[2]], out[cut[2] :]


def final_kernel(half, counts, *refs):
    outs = refs[-len(counts) :]
    for (lows, highs), out_ref in zip(counts, outs):
        x_ref, own_ref, parts = refs[0], refs[1], refs[2 : 2 + lows + highs]
        refs = refs[2 + lows + highs :]
        rows = x_ref.shape[0]
        x = x_ref[...].astype(f32)
        inverse = 1.0 / jnp.sqrt(jnp.sum(x * x, axis=1, keepdims=True) + epsilon)
        sides, along = [], 0.0
        for at, refs_at in ((slice(0, half), parts[:lows]), (slice(half, None), parts[lows:])):
            unit = x[:, at] * inverse
            grad = own_ref[:, at]
            for part in refs_at:
                grad = grad + part[:rows, :].astype(f32)
            grad = logit_scale * grad
            along = along + jnp.sum(unit * grad, axis=1, keepdims=True)
            sides.append((at, unit, grad))
        for at, unit, grad in sides:
            out_ref[:, at] = (grad - unit * along) * inverse


def final(half, *sides):
    operands = [v for x, own, lows, highs in sides for v in (x, own, *lows, *highs)]
    return pl.pallas_call(
        functools.partial(final_kernel, half, tuple((len(lows), len(highs)) for _, _, lows, highs in sides)),
        out_shape=[jax.ShapeDtypeStruct(side[0].shape, f32) for side in sides],
        in_specs=[VMEM] * len(operands),
        out_specs=[VMEM] * len(sides),
        compiler_params=params(*[(v.shape, 8) for v in operands]),
        cost_estimate=pl.CostEstimate(
            flops=10 * sum(side[0].size for side in sides),
            bytes_accessed=12 * sum(side[0].size for side in sides),
            transcendentals=0,
        ),
        name="final",
    )(*operands)


def token_kernel(*refs):
    refs[-1][...] = jnp.zeros_like(refs[-1])


def token(*arrays, flops):
    return pl.pallas_call(
        token_kernel,
        out_shape=jax.ShapeDtypeStruct((8, 128), f32),
        in_specs=[ANY] * len(arrays),
        out_specs=VMEM,
        cost_estimate=pl.CostEstimate(flops=flops, bytes_accessed=0, transcendentals=0),
        name="token",
    )(*arrays)


def after(x, *others):
    others = [v for other in others for v in (other.values() if isinstance(other, dict) else [other])]
    return lax.optimization_barrier((x, *others))[0] if others else x


def body(plan, student_img, student_txt, teacher_img, teacher_txt):
    rows, width = student_img.shape
    far, near, core, row, col = (plan[k] for k in plan.order)

    def spread(x, name, *before):
        return {a: plan.send(after(x, *before), name, a) for a in range(1, plan[name])}

    def onward(blocks, name, *before):
        return {
            (b, a): plan.send(after(x, *before), name, b) for b in range(1, plan[name]) for a, x in blocks.items()
        }

    t_img, t_txt, s_img, s_txt, b_img, b_txt = unit_rows(teacher_img, teacher_txt, student_img, student_txt)
    t_far = spread(t_img, "far")
    t_near = spread(t_txt, "near")
    b_col = spread(b_img, "col")
    b_row = spread(b_txt, "row")
    b_core = spread(b_txt, "core")
    first = [b_col, b_row, b_core]
    teacher_z = token(*t_far.values(), *t_near.values(), flops=10000000000)
    s_far = spread(s_img, "far", teacher_z)
    s_near = spread(s_txt, "near", teacher_z)
    t_far_col = onward(t_far, "col", *first)
    t_near_row = onward(t_near, "row", *first)
    b_row_core = onward(b_row, "core", *first)
    second = [token(*s_far.values(), *s_near.values(), flops=10000000000), t_far_col, t_near_row, b_row_core]
    s_far_col = onward(s_far, "col", *second)
    s_near_row = onward(s_near, "row", *second)
    s_near_core = onward(s_near, "core", *second)
    t_near_core = onward(t_near, "core", *second)
    t_both_core = onward(t_near_row, "core", *second)

    def images(own, by_far, by_col, by_both):
        blocks = {(0, 0): own, **by_both}
        blocks.update({(0, a): x for a, x in by_far.items()})
        blocks.update({(b, 0): x for b, x in by_col.items()})
        return [blocks[b, a] for b in range(col) for a in range(far)]

    def texts(own, by_near, by_row, by_both, by_core, by_core_near, by_core_row, by_core_both):
        blocks = {(0, 0, 0): own}
        blocks.update({(0, 0, a): x for a, x in by_near.items()})
        blocks.update({(0, b, 0): x for b, x in by_row.items()})
        blocks.update({(0, *key): x for key, x in by_both.items()})
        blocks.update({(c, 0, 0): x for c, x in by_core.items()})
        blocks.update({(c, 0, a): x for (c, a), x in by_core_near.items()})
        blocks.update({(c, b, 0): x for (c, b), x in by_core_row.items()})
        blocks.update({(c, *key): x for (c, key), x in by_core_both.items()})
        return [blocks[c, b, a] for c in range(core) for b in range(row) for a in range(near)]

    targets = teacher_targets(
        images(t_img, t_far, b_col, t_far_col),
        texts(t_txt, t_near, b_row, t_near_row, b_core, t_near_core, b_row_core, t_both_core),
    )
    s_both_core = onward(s_near_row, "core", s_near_core, targets)
    s_imgs = images(s_img, s_far, b_col, s_far_col)
    s_txts = texts(s_txt, s_near, b_row, s_near_row, b_core, s_near_core, b_row_core, s_both_core)

    own_txt = row * near
    half = width // 128 * 7 // 9 * 128
    skip = teacher_img.shape[1]
    packed, img_hops, img_kept, img_longs, txt_out = pair_and_sent(
        s_imgs, s_txts, far, near, own_txt, skip, half, targets
    )
    pair, img_pack, txt_pack = packed
    img_in = {}
    for b in range(1, col):
        for a in range(1, far):
            img_in[b, a] = plan.send(img_hops[(b - 1) * far + a], "col", -b)
    long_in = [plan.send(v, "far", -1 - k) for k, v in enumerate(img_longs)]
    txt_in = [plan.send(v, "core", -1 - k // row) for k, v in enumerate(txt_out)]
    *img_stay, txt_own = kept_grads(pair, img_pack, txt_pack, rows, far, own_txt, half)
    txt_hops, txt_kept, txt_stay, txt_longs = text_sums(txt_own, txt_in, rows, row, near, half)

    row_in = {}
    for b in range(1, row):
        for a in range(1, near):
            row_in[b, a] = plan.send(txt_hops[(b - 1) * near + a], "row", -b)
    txt_long_in = [plan.send(v, "near", -1 - k) for k, v in enumerate(txt_longs)]

    def total(own, arrived):
        for v in arrived:
            own = own + v.astype(f32)
        return own.astype(bf16)

    img_last = [
        plan.send(total(after(img_stay[a], *txt_hops, *txt_longs), [img_in[b, a] for b in range(1, col)]), "far", -a) for a in range(1, far)
    ]
    txt_last = [
        plan.send(total(txt_stay[a], [row_in[b, a] for b in range(1, row)]), "near", -a) for a in range(1, near)
    ]
    img_side = [
        plan.send(total(after(img_kept[b - 1], *[*txt_long_in, *row_in.values()]), [v[b * rows : (b + 1) * rows] for v in long_in]), "col", -b)
        for b in range(1, col)
    ]
    txt_side = [
        plan.send(total(after(txt_kept[b - 1], *row_in.values()), [v[b * rows : (b + 1) * rows] for v in txt_long_in]), "row", -b)
        for b in range(1, row)
    ]
    col_ahead = list(txt_long_in)
    row_ahead = list(txt_long_in)
    img_ends = [plan.send(after(img_hops[(b - 1) * far], *col_ahead), "col", -b) for b in range(1, col)]
    txt_ends = [plan.send(after(txt_hops[(b - 1) * near], *row_ahead), "row", -b) for b in range(1, row)]
    image_side = (student_img, img_stay[0], img_ends + img_last, img_side + long_in)
    text_side = (student_txt, txt_stay[0], txt_ends + txt_last, txt_side + txt_long_in)
    return tuple(final(half, image_side, text_side))


def solution(mesh):
    spec = P(AXES, None)
    return jax.shard_map(
        functools.partial(body, Plan(mesh)), mesh=mesh, in_specs=(spec,) * 4, out_specs=(spec,) * 2, check_vma=False
    )
```

```python
import functools
import math
import jax
import jax.numpy as jnp
from jax import lax
from jax.experimental import pallas as pl
from jax.experimental.pallas import tpu as pltpu
from jax.sharding import PartitionSpec as P

epsilon = 1e-06
logit_scale = 100.0
logit_bias = -4.0

AXES = ("blk", "narrow")
ANY = pl.BlockSpec(memory_space=pl.ANY)
VMEM = pl.BlockSpec(memory_space=pltpu.VMEM)
f32 = jnp.float32
bf16 = jnp.bfloat16


def split_two(size):
    fast = int(size**0.5)
    while size % fast:
        fast -= 1
    return max(fast, size // fast), min(fast, size // fast)


class Plan:
    def __init__(self, mesh):
        blk, narrow = mesh.shape["blk"], mesh.shape["narrow"]
        core = 2 if blk % 2 == 0 else 1
        far, near = split_two(blk // core)
        large, small = split_two(narrow)
        self.digits = {"far": far, "near": near, "core": core, "row": small, "col": large}
        self.order = ["far", "near", "core", "row", "col"]

    def __getitem__(self, name):
        return self.digits[name]

    def place(self, index):
        out = {}
        for name in reversed(self.order):
            out[name] = index % self.digits[name]
            index //= self.digits[name]
        return out

    def index(self, place):
        out = 0
        for name in self.order:
            out = out * self.digits[name] + place[name]
        return out

    def send(self, x, name, by):
        total = 1
        for size in self.digits.values():
            total *= size
        pairs = []
        for src in range(total):
            place = self.place(src)
            place[name] = (place[name] + by) % self.digits[name]
            pairs.append((src, self.index(place)))
        return lax.ppermute(x, AXES, pairs)


def params(*held):
    total = sum(math.prod(shape) * size for shape, size in held)
    return pltpu.CompilerParams(vmem_limit_bytes=int(total) + 8 * 2**20)


def tile_rows(rows, most):
    step = most
    while rows % step:
        step //= 2
    return step


def load_all(refs, targets, sems, columns=None):
    copies = []
    for k, (ref, target) in enumerate(zip(refs, targets)):
        if columns is not None and ref.shape[1] != target.shape[1]:
            ref = ref.at[:, pl.ds(columns, target.shape[1])]
        copies.append(pltpu.make_async_copy(ref, target, sems.at[k]))
        copies[-1].start()
    return copies


def unit_kernel(count, *refs):
    x_refs, out_refs, both_refs = refs[:count], refs[count : 2 * count], refs[2 * count : 2 * count + count // 2]
    held, sems = refs[2 * count + count // 2 : -1], refs[-1]
    copies = load_all(x_refs, held, sems)
    for k, (copy, x_ref, out_ref) in enumerate(zip(copies, held, out_refs)):
        copy.wait()
        x = x_ref[...].astype(f32)
        scale = 1.0 / jnp.sqrt(jnp.sum(x * x, axis=1, keepdims=True) + epsilon)
        unit = (x * scale).astype(bf16)
        out_ref[...] = unit
        both, width = both_refs[k % (count // 2)], x.shape[1]
        if k < count // 2:
            both[:, :width] = unit
        else:
            both[:, both.shape[1] - width :] = unit


def unit_rows(*arrays):
    half = len(arrays) // 2
    both = [(a.shape[0], a.shape[1] + b.shape[1]) for a, b in zip(arrays[:half], arrays[half:])]
    return pl.pallas_call(
        functools.partial(unit_kernel, len(arrays)),
        out_shape=[jax.ShapeDtypeStruct(a.shape, bf16) for a in arrays]
        + [jax.ShapeDtypeStruct(shape, bf16) for shape in both],
        in_specs=[ANY] * len(arrays),
        out_specs=[VMEM] * (len(arrays) + half),
        scratch_shapes=[pltpu.VMEM(a.shape, bf16) for a in arrays]
        + [pltpu.SemaphoreType.DMA((len(arrays),))],
        compiler_params=pltpu.CompilerParams(vmem_limit_bytes=int(60 * 2**20)),
        cost_estimate=pl.CostEstimate(
            flops=4 * sum(a.size for a in arrays),
            bytes_accessed=6 * sum(a.size for a in arrays),
            transcendentals=0,
        ),
        name="unit_rows",
    )(*arrays)


def pack(refs, target, columns):
    rows, width = refs[0].shape[0], target.shape[1]
    for k, ref in enumerate(refs):
        first = columns if ref.shape[1] != width else 0
        target[k * rows : (k + 1) * rows, :] = ref[:, first : first + width]


def teacher_kernel(images, texts, *refs):
    img_refs, txt_refs = refs[:images], refs[images : images + texts]
    p_ref, img, txt = refs[images + texts :]
    rows = img_refs[0].shape[0]
    pack(img_refs, img, 0)
    pack(txt_refs, txt, 0)
    step = tile_rows(texts * rows, 256)

    def one(j, carry):
        at = pl.ds(pl.multiple_of(j * step, step), step)
        dots = lax.dot_general(img[...], txt[at, :], (((1,), (1,)), ((), ())), preferred_element_type=f32)
        p_ref[:, at] = jax.nn.sigmoid(logit_scale * dots + logit_bias)
        return carry

    lax.fori_loop(0, texts * rows // step, one, 0)
    own = lax.broadcasted_iota(jnp.int32, (rows, rows), 0) == lax.broadcasted_iota(jnp.int32, (rows, rows), 1)
    p_ref[:rows, :rows] = p_ref[:rows, :rows] + jnp.where(own, 1.0, 0.0).astype(f32)


def teacher_targets(img_blocks, txt_blocks):
    images, texts = len(img_blocks), len(txt_blocks)
    rows, width = img_blocks[0].shape
    return pl.pallas_call(
        functools.partial(teacher_kernel, images, texts),
        out_shape=jax.ShapeDtypeStruct((images * rows, texts * rows), f32),
        in_specs=[VMEM] * (images + texts),
        out_specs=VMEM,
        scratch_shapes=[
            pltpu.VMEM((images * rows, width), bf16),
            pltpu.VMEM((texts * rows, width), bf16),
        ],
        compiler_params=params(((images + texts, rows, width), 2), ((images, rows, texts, rows), 4), *[(v.shape, 2) for v in (*img_blocks, *txt_blocks)]),
        cost_estimate=pl.CostEstimate(
            flops=2 * images * texts * rows * rows * width,
            bytes_accessed=2 * (images + texts) * rows * width + 4 * images * texts * rows * rows,
            transcendentals=images * texts * rows * rows,
        ),
        name="teacher_targets",
    )(*img_blocks, *txt_blocks)


def image_grads(pair, txt, rows, first, count):
    part = lax.dot_general(
        pair[first * rows : (first + count) * rows, :], txt, (((1,), (0,)), ((), ())), preferred_element_type=f32
    )
    return [part[k * rows : (k + 1) * rows, :] for k in range(count)]


def text_grads(pair, img, rows, first, count):
    part = lax.dot_general(
        pair[:, first * rows : (first + count) * rows], img, (((0,), (0,)), ((), ())), preferred_element_type=f32
    )
    return [part[k * rows : (k + 1) * rows, :] for k in range(count)]


def pair_kernel(images, texts, far, skip, half, own_txt, *refs):
    img_refs, txt_refs = refs[:images], refs[images : images + texts]
    p_ref, pair_ref, img, txt = refs[images + texts : images + texts + 4]
    outs = list(refs[images + texts + 4 :])
    rows, col = img_refs[0].shape[0], images // far
    pack(img_refs, img, skip)
    pack(txt_refs, txt, skip)
    step = tile_rows(texts * rows, 256)
    for j in range(texts * rows // step):
        at = slice(j * step, (j + 1) * step)
        dots = lax.dot_general(img[...], txt[at, :], (((1,), (1,)), ((), ())), preferred_element_type=f32)
        pair_ref[:, at] = (2.0 * jax.nn.sigmoid(logit_scale * dots + logit_bias) - p_ref[:, at]).astype(bf16)
    others = image_grads(pair_ref, txt[...], rows, far, far * (col - 1)) if col > 1 else []
    hops = [outs.pop(0) for _ in range(far * (col - 1))]
    kept = [outs.pop(0) for _ in range(col - 1)]
    longs = [outs.pop(0) for _ in range(far - 1)]
    for k, grad in enumerate(others):
        b, a = 1 + k // far, k % far
        hops[k][...] = grad[:, :half].astype(bf16)
        if a:
            longs[a - 1][b * rows : (b + 1) * rows, :] = grad[:, half:].astype(bf16)
        else:
            kept[b - 1][...] = grad[:, half:]
    if far > 1:
        for a, grad in enumerate(image_grads(pair_ref, txt[:, half:], rows, 1, far - 1)):
            longs[a][:rows, :] = grad.astype(bf16)
    if outs:
        count = outs[0].shape[0] // rows
        grads = text_grads(pair_ref, img[...], rows, own_txt, len(outs) * count)
        for k, grad in enumerate(grads):
            outs[k // count][(k % count) * rows : (k % count + 1) * rows, :] = grad.astype(bf16)


def pair_and_sent(img_blocks, txt_blocks, far, near, own_txt, skip, half, targets):
    images, texts = len(img_blocks), len(txt_blocks)
    rows, width = img_blocks[-1].shape
    col = images // far
    shapes = [((images * rows, texts * rows), bf16), ((images * rows, width), bf16), ((texts * rows, width), bf16)]
    shapes += [((rows, half), bf16)] * (far * (col - 1))
    shapes += [((rows, width - half), f32)] * (col - 1)
    shapes += [((col * rows, width - half), bf16)] * (far - 1)
    shapes += [((near * rows, width), bf16)] * ((texts - own_txt) // near)
    out = pl.pallas_call(
        functools.partial(pair_kernel, images, texts, far, skip, half, own_txt),
        out_shape=[jax.ShapeDtypeStruct(*shape) for shape in shapes],
        in_specs=[VMEM] * (images + texts + 1),
        out_specs=[VMEM] * len(shapes),
        compiler_params=params(
            ((images * rows, texts * rows), 6),
            ((images + texts, rows, width), 6),
            *[(v.shape, 2) for v in (*img_blocks, *txt_blocks)],
        ),
        cost_estimate=pl.CostEstimate(
            flops=4 * images * texts * rows * rows * width,
            bytes_accessed=2 * (images + texts) * rows * width + 8 * images * texts * rows * rows,
            transcendentals=images * texts * rows * rows,
        ),
        name="pair_and_sent",
    )(*img_blocks, *txt_blocks, targets)
    out = list(out)
    cut = [3, 3 + far * (col - 1), 3 + (far + 1) * (col - 1), 3 + (far + 1) * (col - 1) + far - 1]
    return out[:3], out[cut[0] : cut[1]], out[cut[1] : cut[2]], out[cut[2] : cut[3]], out[cut[3] :]


def kept_kernel(of_texts, pair, other, *outs):
    rows = outs[0].shape[0]
    if of_texts:
        outs[0][...] = lax.dot_general(
            pair[:, :rows], other[...], (((0,), (0,)), ((), ())), preferred_element_type=f32
        )
    else:
        for out, grad in zip(outs, image_grads(pair, other[...], rows, 0, len(outs))):
            out[...] = grad[:, : out.shape[1]]


def kept_grads(pair, other, shapes, of_texts):
    return pl.pallas_call(
        functools.partial(kept_kernel, of_texts),
        out_shape=[jax.ShapeDtypeStruct(shape, f32) for shape in shapes],
        in_specs=[VMEM] * 2,
        out_specs=[VMEM] * len(shapes),
        compiler_params=params((pair.shape, 2), (other.shape, 2), *[(v, 8) for v in shapes]),
        cost_estimate=pl.CostEstimate(
            flops=pair.size * other.shape[1],
            bytes_accessed=2 * (pair.size + other.size) + 4 * sum(math.prod(v) for v in shapes),
            transcendentals=0,
        ),
        name="kept_texts" if of_texts else "kept_images",
    )(pair, other)


def text_sums_kernel(row, near, half, cores, own_ref, *refs):
    arrived, outs = refs[: cores * row], list(refs[cores * row :])
    rows = own_ref.shape[0] // (row * near)
    hops = [outs.pop(0) for _ in range(near * (row - 1))]
    kept = [outs.pop(0) for _ in range(row - 1)]
    stay = [outs.pop(0) for _ in range(near)]
    for b in range(row):
        for a in range(near):
            k = b * near + a
            total = own_ref[k * rows : (k + 1) * rows, :]
            for c in range(cores):
                total = total + arrived[c * row + b][a * rows : (a + 1) * rows, :].astype(f32)
            if b:
                hops[(b - 1) * near + a][...] = total[:, :half].astype(bf16)
            else:
                stay[a][...] = total[:, : stay[a].shape[1]]
            if a:
                outs[a - 1][b * rows : (b + 1) * rows, :] = total[:, half:].astype(bf16)
            elif b:
                kept[b - 1][...] = total[:, half:]


def text_sums(own, arrived, rows, row, near, half):
    width = own.shape[1]
    shapes = [((rows, half), bf16)] * (near * (row - 1)) + [((rows, width - half), f32)] * (row - 1)
    shapes += [((rows, width), f32)] + [((rows, half), f32)] * (near - 1)
    shapes += [((row * rows, width - half), bf16)] * (near - 1)
    out = list(
        pl.pallas_call(
            functools.partial(text_sums_kernel, row, near, half, len(arrived) // row),
            out_shape=[jax.ShapeDtypeStruct(*shape) for shape in shapes],
            in_specs=[VMEM] * (1 + len(arrived)),
            out_specs=[VMEM] * len(shapes),
            compiler_params=params((own.shape, 16)),
            cost_estimate=pl.CostEstimate(flops=2 * own.size, bytes_accessed=10 * own.size, transcendentals=0),
            name="text_sums",
        )(own, *arrived)
    )
    cut = [near * (row - 1), (near + 1) * (row - 1), (near + 1) * (row - 1) + near]
    return out[: cut[0]], out[cut[0] : cut[1]], out[cut[1] : cut[2]], out[cut[2] :]


def final_kernel(half, counts, *refs):
    outs = refs[-len(counts) :]
    for (lows, highs), out_ref in zip(counts, outs):
        x_ref, own_ref, parts = refs[0], refs[1], refs[2 : 2 + lows + highs]
        refs = refs[2 + lows + highs :]
        rows = x_ref.shape[0]
        x = x_ref[...].astype(f32)
        inverse = 1.0 / jnp.sqrt(jnp.sum(x * x, axis=1, keepdims=True) + epsilon)
        sides, along = [], 0.0
        for at, refs_at in ((slice(0, half), parts[:lows]), (slice(half, None), parts[lows:])):
            unit = x[:, at] * inverse
            grad = own_ref[:, at]
            for part in refs_at:
                grad = grad + part[:rows, :].astype(f32)
            grad = logit_scale * grad
            along = along + jnp.sum(unit * grad, axis=1, keepdims=True)
            sides.append((at, unit, grad))
        for at, unit, grad in sides:
            out_ref[:, at] = (grad - unit * along) * inverse


def final(half, *sides):
    operands = [v for x, own, lows, highs in sides for v in (x, own, *lows, *highs)]
    return pl.pallas_call(
        functools.partial(final_kernel, half, tuple((len(lows), len(highs)) for _, _, lows, highs in sides)),
        out_shape=[jax.ShapeDtypeStruct(side[0].shape, f32) for side in sides],
        in_specs=[VMEM] * len(operands),
        out_specs=[VMEM] * len(sides),
        compiler_params=params(*[(v.shape, 8) for v in operands]),
        cost_estimate=pl.CostEstimate(
            flops=10 * sum(side[0].size for side in sides),
            bytes_accessed=12 * sum(side[0].size for side in sides),
            transcendentals=0,
        ),
        name="final",
    )(*operands)


def token_kernel(*refs):
    refs[-1][...] = jnp.zeros_like(refs[-1])


def token(*arrays, flops):
    return pl.pallas_call(
        token_kernel,
        out_shape=jax.ShapeDtypeStruct((8, 128), f32),
        in_specs=[ANY] * len(arrays),
        out_specs=VMEM,
        cost_estimate=pl.CostEstimate(flops=flops, bytes_accessed=0, transcendentals=0),
        name="token",
    )(*arrays)


def after(x, *others):
    others = [v for other in others for v in (other.values() if isinstance(other, dict) else [other])]
    return lax.optimization_barrier((x, *others))[0] if others else x


def body(plan, student_img, student_txt, teacher_img, teacher_txt):
    rows, width = student_img.shape
    far, near, core, row, col = (plan[k] for k in plan.order)

    def spread(x, name, *before):
        return {a: plan.send(after(x, *before), name, a) for a in range(1, plan[name])}

    def onward(blocks, name, *before):
        return {
            (b, a): plan.send(after(x, *before), name, b) for b in range(1, plan[name]) for a, x in blocks.items()
        }

    t_img, t_txt, s_img, s_txt, b_img, b_txt = unit_rows(teacher_img, teacher_txt, student_img, student_txt)
    t_far = spread(t_img, "far")
    t_near = spread(t_txt, "near")
    b_col = spread(b_img, "col")
    b_row = spread(b_txt, "row")
    b_core = spread(b_txt, "core")
    first = [b_col, b_row, b_core]
    teacher_z = token(*t_far.values(), *t_near.values(), flops=10000000000)
    s_far = spread(s_img, "far", teacher_z)
    s_near = spread(s_txt, "near", teacher_z)
    t_far_col = onward(t_far, "col", *first)
    t_near_row = onward(t_near, "row", *first)
    b_row_core = onward(b_row, "core", *first)
    second = [token(*s_far.values(), *s_near.values(), flops=10000000000), t_far_col, t_near_row, b_row_core]
    s_far_col = onward(s_far, "col", *second)
    s_near_row = onward(s_near, "row", *second)
    s_near_core = onward(s_near, "core", *second)
    t_near_core = onward(t_near, "core", *second)
    t_both_core = onward(t_near_row, "core", *second)

    def images(own, by_far, by_col, by_both):
        blocks = {(0, 0): own, **by_both}
        blocks.update({(0, a): x for a, x in by_far.items()})
        blocks.update({(b, 0): x for b, x in by_col.items()})
        return [blocks[b, a] for b in range(col) for a in range(far)]

    def texts(own, by_near, by_row, by_both, by_core, by_core_near, by_core_row, by_core_both):
        blocks = {(0, 0, 0): own}
        blocks.update({(0, 0, a): x for a, x in by_near.items()})
        blocks.update({(0, b, 0): x for b, x in by_row.items()})
        blocks.update({(0, *key): x for key, x in by_both.items()})
        blocks.update({(c, 0, 0): x for c, x in by_core.items()})
        blocks.update({(c, 0, a): x for (c, a), x in by_core_near.items()})
        blocks.update({(c, b, 0): x for (c, b), x in by_core_row.items()})
        blocks.update({(c, *key): x for (c, key), x in by_core_both.items()})
        return [blocks[c, b, a] for c in range(core) for b in range(row) for a in range(near)]

    targets = teacher_targets(
        images(t_img, t_far, b_col, t_far_col),
        texts(t_txt, t_near, b_row, t_near_row, b_core, t_near_core, b_row_core, t_both_core),
    )
    s_both_core = onward(s_near_row, "core", s_near_core, targets)
    s_imgs = images(s_img, s_far, b_col, s_far_col)
    s_txts = texts(s_txt, s_near, b_row, s_near_row, b_core, s_near_core, b_row_core, s_both_core)

    own_txt = row * near
    half = width // 128 * 7 // 9 * 128
    skip = teacher_img.shape[1]
    packed, img_hops, img_kept, img_longs, txt_out = pair_and_sent(
        s_imgs, s_txts, far, near, own_txt, skip, half, targets
    )
    pair, img_pack, txt_pack = packed
    img_in = {}
    for b in range(1, col):
        for a in range(1, far):
            img_in[b, a] = plan.send(img_hops[(b - 1) * far + a], "col", -b)
    long_in = [plan.send(v, "far", -1 - k) for k, v in enumerate(img_longs)]
    txt_in = [plan.send(v, "core", -1 - k // row) for k, v in enumerate(txt_out)]
    (txt_own,) = kept_grads(pair, img_pack, [(own_txt * rows, width)], True)
    txt_hops, txt_kept, txt_stay, txt_longs = text_sums(txt_own, txt_in, rows, row, near, half)
    img_stay = kept_grads(after(pair, *txt_hops), txt_pack, [(rows, width)] + [(rows, half)] * (far - 1), False)

    row_in = {}
    for b in range(1, row):
        for a in range(1, near):
            row_in[b, a] = plan.send(txt_hops[(b - 1) * near + a], "row", -b)
    txt_long_in = [plan.send(v, "near", -1 - k) for k, v in enumerate(txt_longs)]

    def total(own, arrived):
        for v in arrived:
            own = own + v.astype(f32)
        return own.astype(bf16)

    img_last = [
        plan.send(total(after(img_stay[a], *txt_hops, *txt_longs), [img_in[b, a] for b in range(1, col)]), "far", -a) for a in range(1, far)
    ]
    txt_last = [
        plan.send(total(txt_stay[a], [row_in[b, a] for b in range(1, row)]), "near", -a) for a in range(1, near)
    ]
    img_side = [
        plan.send(total(after(img_kept[b - 1], *[*txt_long_in, *row_in.values()]), [v[b * rows : (b + 1) * rows] for v in long_in]), "col", -b)
        for b in range(1, col)
    ]
    txt_side = [
        plan.send(total(after(txt_kept[b - 1], *row_in.values()), [v[b * rows : (b + 1) * rows] for v in txt_long_in]), "row", -b)
        for b in range(1, row)
    ]
    col_ahead = list(txt_long_in)
    row_ahead = list(txt_long_in)
    img_ends = [plan.send(after(img_hops[(b - 1) * far], *col_ahead), "col", -b) for b in range(1, col)]
    txt_ends = [plan.send(after(txt_hops[(b - 1) * near], *row_ahead), "row", -b) for b in range(1, row)]
    image_side = (student_img, img_stay[0], img_ends + img_last, img_side + long_in)
    text_side = (student_txt, txt_stay[0], txt_ends + txt_last, txt_side + txt_long_in)
    return tuple(final(half, image_side, text_side))


def solution(mesh):
    spec = P(AXES, None)
    return jax.shard_map(
        functools.partial(body, Plan(mesh)), mesh=mesh, in_specs=(spec,) * 4, out_specs=(spec,) * 2, check_vma=False
    )
```

```python
import functools
import math
import jax
import jax.numpy as jnp
from jax import lax
from jax.experimental import pallas as pl
from jax.experimental.pallas import tpu as pltpu
from jax.sharding import PartitionSpec as P

epsilon = 1e-06
logit_scale = 100.0
logit_bias = -4.0

AXES = ("blk", "narrow")
ANY = pl.BlockSpec(memory_space=pl.ANY)
VMEM = pl.BlockSpec(memory_space=pltpu.VMEM)
f32 = jnp.float32
bf16 = jnp.bfloat16


def split_two(size):
    fast = int(size**0.5)
    while size % fast:
        fast -= 1
    return max(fast, size // fast), min(fast, size // fast)


class Plan:
    def __init__(self, mesh):
        blk, narrow = mesh.shape["blk"], mesh.shape["narrow"]
        core = 2 if blk % 2 == 0 else 1
        far, near = split_two(blk // core)
        large, small = split_two(narrow)
        self.digits = {"far": far, "near": near, "core": core, "row": small, "col": large}
        self.order = ["far", "near", "core", "row", "col"]

    def __getitem__(self, name):
        return self.digits[name]

    def place(self, index):
        out = {}
        for name in reversed(self.order):
            out[name] = index % self.digits[name]
            index //= self.digits[name]
        return out

    def index(self, place):
        out = 0
        for name in self.order:
            out = out * self.digits[name] + place[name]
        return out

    def send(self, x, name, by):
        total = 1
        for size in self.digits.values():
            total *= size
        pairs = []
        for src in range(total):
            place = self.place(src)
            place[name] = (place[name] + by) % self.digits[name]
            pairs.append((src, self.index(place)))
        return lax.ppermute(x, AXES, pairs)


def params(*held):
    total = sum(math.prod(shape) * size for shape, size in held)
    return pltpu.CompilerParams(vmem_limit_bytes=int(total) + 8 * 2**20)


def tile_rows(rows, most):
    step = most
    while rows % step:
        step //= 2
    return step


def load_all(refs, targets, sems, columns=None):
    copies = []
    for k, (ref, target) in enumerate(zip(refs, targets)):
        if columns is not None and ref.shape[1] != target.shape[1]:
            ref = ref.at[:, pl.ds(columns, target.shape[1])]
        copies.append(pltpu.make_async_copy(ref, target, sems.at[k]))
        copies[-1].start()
    return copies


def unit_kernel(count, *refs):
    x_refs, out_refs, both_refs = refs[:count], refs[count : 2 * count], refs[2 * count : 2 * count + count // 2]
    held, sems = refs[2 * count + count // 2 : -1], refs[-1]
    copies = load_all(x_refs, held, sems)
    for k, (copy, x_ref, out_ref) in enumerate(zip(copies, held, out_refs)):
        copy.wait()
        x = x_ref[...].astype(f32)
        scale = 1.0 / jnp.sqrt(jnp.sum(x * x, axis=1, keepdims=True) + epsilon)
        unit = (x * scale).astype(bf16)
        out_ref[...] = unit
        both, width = both_refs[k % (count // 2)], x.shape[1]
        if k < count // 2:
            both[:, :width] = unit
        else:
            both[:, both.shape[1] - width :] = unit


def unit_rows(*arrays):
    half = len(arrays) // 2
    both = [(a.shape[0], a.shape[1] + b.shape[1]) for a, b in zip(arrays[:half], arrays[half:])]
    return pl.pallas_call(
        functools.partial(unit_kernel, len(arrays)),
        out_shape=[jax.ShapeDtypeStruct(a.shape, bf16) for a in arrays]
        + [jax.ShapeDtypeStruct(shape, bf16) for shape in both],
        in_specs=[ANY] * len(arrays),
        out_specs=[VMEM] * (len(arrays) + half),
        scratch_shapes=[pltpu.VMEM(a.shape, bf16) for a in arrays]
        + [pltpu.SemaphoreType.DMA((len(arrays),))],
        compiler_params=pltpu.CompilerParams(vmem_limit_bytes=int(60 * 2**20)),
        cost_estimate=pl.CostEstimate(
            flops=4 * sum(a.size for a in arrays),
            bytes_accessed=6 * sum(a.size for a in arrays),
            transcendentals=0,
        ),
        name="unit_rows",
    )(*arrays)


def pack(refs, target, columns):
    rows, width = refs[0].shape[0], target.shape[1]
    for k, ref in enumerate(refs):
        first = columns if ref.shape[1] != width else 0
        target[k * rows : (k + 1) * rows, :] = ref[:, first : first + width]


def teacher_kernel(images, texts, *refs):
    img_refs, txt_refs = refs[:images], refs[images : images + texts]
    p_ref, img, txt = refs[images + texts :]
    rows = img_refs[0].shape[0]
    pack(img_refs, img, 0)
    pack(txt_refs, txt, 0)
    step = tile_rows(texts * rows, 256)

    def one(j, carry):
        at = pl.ds(pl.multiple_of(j * step, step), step)
        dots = lax.dot_general(img[...], txt[at, :], (((1,), (1,)), ((), ())), preferred_element_type=f32)
        p_ref[:, at] = jax.nn.sigmoid(logit_scale * dots + logit_bias)
        return carry

    lax.fori_loop(0, texts * rows // step, one, 0)
    own = lax.broadcasted_iota(jnp.int32, (rows, rows), 0) == lax.broadcasted_iota(jnp.int32, (rows, rows), 1)
    p_ref[:rows, :rows] = p_ref[:rows, :rows] + jnp.where(own, 1.0, 0.0).astype(f32)


def teacher_targets(img_blocks, txt_blocks):
    images, texts = len(img_blocks), len(txt_blocks)
    rows, width = img_blocks[0].shape
    return pl.pallas_call(
        functools.partial(teacher_kernel, images, texts),
        out_shape=jax.ShapeDtypeStruct((images * rows, texts * rows), f32),
        in_specs=[VMEM] * (images + texts),
        out_specs=VMEM,
        scratch_shapes=[
            pltpu.VMEM((images * rows, width), bf16),
            pltpu.VMEM((texts * rows, width), bf16),
        ],
        compiler_params=params(((images + texts, rows, width), 2), ((images, rows, texts, rows), 4), *[(v.shape, 2) for v in (*img_blocks, *txt_blocks)]),
        cost_estimate=pl.CostEstimate(
            flops=2 * images * texts * rows * rows * width,
            bytes_accessed=2 * (images + texts) * rows * width + 4 * images * texts * rows * rows,
            transcendentals=images * texts * rows * rows,
        ),
        name="teacher_targets",
    )(*img_blocks, *txt_blocks)


def image_grads(pair, txt, rows, first, count):
    part = lax.dot_general(
        pair[first * rows : (first + count) * rows, :], txt, (((1,), (0,)), ((), ())), preferred_element_type=f32
    )
    return [part[k * rows : (k + 1) * rows, :] for k in range(count)]


def text_grads(pair, img, rows, first, count):
    part = lax.dot_general(
        pair[:, first * rows : (first + count) * rows], img, (((0,), (0,)), ((), ())), preferred_element_type=f32
    )
    return [part[k * rows : (k + 1) * rows, :] for k in range(count)]


def pair_kernel(images, texts, far, skip, half, own_txt, *refs):
    img_refs, txt_refs = refs[:images], refs[images : images + texts]
    p_ref, pair_ref, img, txt = refs[images + texts : images + texts + 4]
    outs = list(refs[images + texts + 4 :])
    rows, col = img_refs[0].shape[0], images // far
    pack(img_refs, img, skip)
    pack(txt_refs, txt, skip)
    step = tile_rows(texts * rows, 256)
    for j in range(texts * rows // step):
        at = slice(j * step, (j + 1) * step)
        dots = lax.dot_general(img[...], txt[at, :], (((1,), (1,)), ((), ())), preferred_element_type=f32)
        pair_ref[:, at] = (2.0 * jax.nn.sigmoid(logit_scale * dots + logit_bias) - p_ref[:, at]).astype(bf16)
    others = image_grads(pair_ref, txt[...], rows, far, far * (col - 1)) if col > 1 else []
    hops = [outs.pop(0) for _ in range(far * (col - 1))]
    kept = [outs.pop(0) for _ in range(col - 1)]
    longs = [outs.pop(0) for _ in range(far - 1)]
    for k, grad in enumerate(others):
        b, a = 1 + k // far, k % far
        hops[k][...] = grad[:, :half].astype(bf16)
        if a:
            longs[a - 1][b * rows : (b + 1) * rows, :] = grad[:, half:].astype(bf16)
        else:
            kept[b - 1][...] = grad[:, half:]
    if far > 1:
        for a, grad in enumerate(image_grads(pair_ref, txt[:, half:], rows, 1, far - 1)):
            longs[a][:rows, :] = grad.astype(bf16)
    if outs:
        count = outs[0].shape[0] // rows
        grads = text_grads(pair_ref, img[...], rows, own_txt, len(outs) * count)
        for k, grad in enumerate(grads):
            outs[k // count][(k % count) * rows : (k % count + 1) * rows, :] = grad.astype(bf16)


def pair_and_sent(img_blocks, txt_blocks, far, near, own_txt, skip, half, targets):
    images, texts = len(img_blocks), len(txt_blocks)
    rows, width = img_blocks[-1].shape
    col = images // far
    shapes = [((images * rows, texts * rows), bf16), ((images * rows, width), bf16), ((texts * rows, width), bf16)]
    shapes += [((rows, half), bf16)] * (far * (col - 1))
    shapes += [((rows, width - half), f32)] * (col - 1)
    shapes += [((col * rows, width - half), bf16)] * (far - 1)
    shapes += [((near * rows, width), bf16)] * ((texts - own_txt) // near)
    out = pl.pallas_call(
        functools.partial(pair_kernel, images, texts, far, skip, half, own_txt),
        out_shape=[jax.ShapeDtypeStruct(*shape) for shape in shapes],
        in_specs=[VMEM] * (images + texts + 1),
        out_specs=[VMEM] * len(shapes),
        compiler_params=params(
            ((images * rows, texts * rows), 6),
            ((images + texts, rows, width), 6),
            *[(v.shape, 2) for v in (*img_blocks, *txt_blocks)],
        ),
        cost_estimate=pl.CostEstimate(
            flops=4 * images * texts * rows * rows * width,
            bytes_accessed=2 * (images + texts) * rows * width + 8 * images * texts * rows * rows,
            transcendentals=images * texts * rows * rows,
        ),
        name="pair_and_sent",
    )(*img_blocks, *txt_blocks, targets)
    out = list(out)
    cut = [3, 3 + far * (col - 1), 3 + (far + 1) * (col - 1), 3 + (far + 1) * (col - 1) + far - 1]
    return out[:3], out[cut[0] : cut[1]], out[cut[1] : cut[2]], out[cut[2] : cut[3]], out[cut[3] :]


def kept_kernel(half, pair, img, txt, *outs):
    rows = outs[0].shape[0]
    far = len(outs) - 1
    outs[-1][...] = lax.dot_general(
        pair[:, : outs[-1].shape[0]], img[...], (((0,), (0,)), ((), ())), preferred_element_type=f32
    )
    for out, grad in zip(outs, image_grads(pair, txt[...], rows, 0, far)):
        out[...] = grad[:, : out.shape[1]]


def kept_grads(pair, img, txt, rows, far, own_txt, half):
    width = img.shape[1]
    shapes = [(rows, width)] + [(rows, half)] * (far - 1) + [(own_txt * rows, width)]
    return pl.pallas_call(
        functools.partial(kept_kernel, half),
        out_shape=[jax.ShapeDtypeStruct(shape, f32) for shape in shapes],
        in_specs=[VMEM] * 3,
        out_specs=[VMEM] * len(shapes),
        compiler_params=params((pair.shape, 2), (img.shape, 2), (txt.shape, 2), *[(v, 8) for v in shapes]),
        cost_estimate=pl.CostEstimate(
            flops=2 * pair.size * width,
            bytes_accessed=2 * (pair.size + img.size + txt.size) + 4 * own_txt * rows * width,
            transcendentals=0,
        ),
        name="kept",
    )(pair, img, txt)


def text_sums_kernel(row, near, half, cores, own_ref, *refs):
    arrived, outs = refs[: cores * row], list(refs[cores * row :])
    rows = own_ref.shape[0] // (row * near)
    hops = [outs.pop(0) for _ in range(near * (row - 1))]
    kept = [outs.pop(0) for _ in range(row - 1)]
    stay = [outs.pop(0) for _ in range(near)]
    for b in range(row):
        for a in range(near):
            k = b * near + a
            total = own_ref[k * rows : (k + 1) * rows, :]
            for c in range(cores):
                total = total + arrived[c * row + b][a * rows : (a + 1) * rows, :].astype(f32)
            if b:
                hops[(b - 1) * near + a][...] = total[:, :half].astype(bf16)
            else:
                stay[a][...] = total[:, : stay[a].shape[1]]
            if a:
                outs[a - 1][b * rows : (b + 1) * rows, :] = total[:, half:].astype(bf16)
            elif b:
                kept[b - 1][...] = total[:, half:]


def text_sums(own, arrived, rows, row, near, half):
    width = own.shape[1]
    shapes = [((rows, half), bf16)] * (near * (row - 1)) + [((rows, width - half), f32)] * (row - 1)
    shapes += [((rows, width), f32)] + [((rows, half), f32)] * (near - 1)
    shapes += [((row * rows, width - half), bf16)] * (near - 1)
    out = list(
        pl.pallas_call(
            functools.partial(text_sums_kernel, row, near, half, len(arrived) // row),
            out_shape=[jax.ShapeDtypeStruct(*shape) for shape in shapes],
            in_specs=[VMEM] * (1 + len(arrived)),
            out_specs=[VMEM] * len(shapes),
            compiler_params=params((own.shape, 16)),
            cost_estimate=pl.CostEstimate(flops=2 * own.size, bytes_accessed=10 * own.size, transcendentals=0),
            name="text_sums",
        )(own, *arrived)
    )
    cut = [near * (row - 1), (near + 1) * (row - 1), (near + 1) * (row - 1) + near]
    return out[: cut[0]], out[cut[0] : cut[1]], out[cut[1] : cut[2]], out[cut[2] :]


def final_kernel(half, lows, x_ref, own_ref, *refs):
    parts, out_ref = refs[:-1], refs[-1]
    rows = x_ref.shape[0]
    x = x_ref[...].astype(f32)
    inverse = 1.0 / jnp.sqrt(jnp.sum(x * x, axis=1, keepdims=True) + epsilon)
    sides, along = [], 0.0
    for at, refs_at in ((slice(0, half), parts[:lows]), (slice(half, None), parts[lows:])):
        unit = x[:, at] * inverse
        grad = own_ref[:, at]
        for part in refs_at:
            grad = grad + part[:rows, :].astype(f32)
        grad = logit_scale * grad
        along = along + jnp.sum(unit * grad, axis=1, keepdims=True)
        sides.append((at, unit, grad))
    for at, unit, grad in sides:
        out_ref[:, at] = (grad - unit * along) * inverse


def final(x, own, lows, highs, half):
    operands = [x, own, *lows, *highs]
    return pl.pallas_call(
        functools.partial(final_kernel, half, len(lows)),
        out_shape=jax.ShapeDtypeStruct(x.shape, f32),
        in_specs=[VMEM] * len(operands),
        out_specs=VMEM,
        compiler_params=params((x.shape, 4 * (4 + len(operands)))),
        cost_estimate=pl.CostEstimate(flops=10 * x.size, bytes_accessed=12 * x.size, transcendentals=0),
        name="final",
    )(*operands)


def token_kernel(*refs):
    refs[-1][...] = jnp.zeros_like(refs[-1])


def token(*arrays, flops):
    return pl.pallas_call(
        token_kernel,
        out_shape=jax.ShapeDtypeStruct((8, 128), f32),
        in_specs=[ANY] * len(arrays),
        out_specs=VMEM,
        cost_estimate=pl.CostEstimate(flops=flops, bytes_accessed=0, transcendentals=0),
        name="token",
    )(*arrays)


def after(x, *others):
    others = [v for other in others for v in (other.values() if isinstance(other, dict) else [other])]
    return lax.optimization_barrier((x, *others))[0] if others else x


def body(plan, student_img, student_txt, teacher_img, teacher_txt):
    rows, width = student_img.shape
    far, near, core, row, col = (plan[k] for k in plan.order)

    def spread(x, name, *before):
        return {a: plan.send(after(x, *before), name, a) for a in range(1, plan[name])}

    def onward(blocks, name, *before):
        return {
            (b, a): plan.send(after(x, *before), name, b) for b in range(1, plan[name]) for a, x in blocks.items()
        }

    t_img, t_txt, s_img, s_txt, b_img, b_txt = unit_rows(teacher_img, teacher_txt, student_img, student_txt)
    t_far = spread(t_img, "far")
    t_near = spread(t_txt, "near")
    b_col = spread(b_img, "col")
    b_row = spread(b_txt, "row")
    b_core = spread(b_txt, "core")
    first = [b_col, b_row, b_core]
    teacher_z = token(*t_far.values(), *t_near.values(), flops=10000000000)
    s_far = spread(s_img, "far", teacher_z)
    s_near = spread(s_txt, "near", teacher_z)
    t_far_col = onward(t_far, "col", *first)
    t_near_row = onward(t_near, "row", *first)
    b_row_core = onward(b_row, "core", *first)
    second = [token(*s_far.values(), *s_near.values(), flops=10000000000), t_far_col, t_near_row, b_row_core]
    s_far_col = onward(s_far, "col", *second)
    s_near_row = onward(s_near, "row", *second)
    s_near_core = onward(s_near, "core", *second)
    t_near_core = onward(t_near, "core", *second)
    t_both_core = onward(t_near_row, "core", *second)

    def images(own, by_far, by_col, by_both):
        blocks = {(0, 0): own, **by_both}
        blocks.update({(0, a): x for a, x in by_far.items()})
        blocks.update({(b, 0): x for b, x in by_col.items()})
        return [blocks[b, a] for b in range(col) for a in range(far)]

    def texts(own, by_near, by_row, by_both, by_core, by_core_near, by_core_row, by_core_both):
        blocks = {(0, 0, 0): own}
        blocks.update({(0, 0, a): x for a, x in by_near.items()})
        blocks.update({(0, b, 0): x for b, x in by_row.items()})
        blocks.update({(0, *key): x for key, x in by_both.items()})
        blocks.update({(c, 0, 0): x for c, x in by_core.items()})
        blocks.update({(c, 0, a): x for (c, a), x in by_core_near.items()})
        blocks.update({(c, b, 0): x for (c, b), x in by_core_row.items()})
        blocks.update({(c, *key): x for (c, key), x in by_core_both.items()})
        return [blocks[c, b, a] for c in range(core) for b in range(row) for a in range(near)]

    targets = teacher_targets(
        images(t_img, t_far, b_col, t_far_col),
        texts(t_txt, t_near, b_row, t_near_row, b_core, t_near_core, b_row_core, t_both_core),
    )
    s_both_core = onward(s_near_row, "core", s_near_core, targets)
    s_imgs = images(s_img, s_far, b_col, s_far_col)
    s_txts = texts(s_txt, s_near, b_row, s_near_row, b_core, s_near_core, b_row_core, s_both_core)

    own_txt = row * near
    half = width // 128 * 7 // 9 * 128
    skip = teacher_img.shape[1]
    packed, img_hops, img_kept, img_longs, txt_out = pair_and_sent(
        s_imgs, s_txts, far, near, own_txt, skip, half, targets
    )
    pair, img_pack, txt_pack = packed
    img_in = {}
    for b in range(1, col):
        for a in range(1, far):
            img_in[b, a] = plan.send(img_hops[(b - 1) * far + a], "col", -b)
    long_in = [plan.send(v, "far", -1 - k) for k, v in enumerate(img_longs)]
    txt_in = [plan.send(v, "core", -1 - k // row) for k, v in enumerate(txt_out)]
    *img_stay, txt_own = kept_grads(pair, img_pack, txt_pack, rows, far, own_txt, half)
    txt_hops, txt_kept, txt_stay, txt_longs = text_sums(txt_own, txt_in, rows, row, near, half)

    row_in = {}
    for b in range(1, row):
        for a in range(1, near):
            row_in[b, a] = plan.send(txt_hops[(b - 1) * near + a], "row", -b)
    txt_long_in = [plan.send(v, "near", -1 - k) for k, v in enumerate(txt_longs)]

    def total(own, arrived):
        for v in arrived:
            own = own + v.astype(f32)
        return own.astype(bf16)

    img_last = [
        plan.send(total(after(img_stay[a], *txt_hops, *txt_longs), [img_in[b, a] for b in range(1, col)]), "far", -a) for a in range(1, far)
    ]
    txt_last = [
        plan.send(total(txt_stay[a], [row_in[b, a] for b in range(1, row)]), "near", -a) for a in range(1, near)
    ]
    img_side = [
        plan.send(total(after(img_kept[b - 1], *[*txt_long_in, *row_in.values()]), [v[b * rows : (b + 1) * rows] for v in long_in]), "col", -b)
        for b in range(1, col)
    ]
    txt_side = [
        plan.send(total(after(txt_kept[b - 1], *row_in.values()), [v[b * rows : (b + 1) * rows] for v in txt_long_in]), "row", -b)
        for b in range(1, row)
    ]
    col_ahead = list(txt_long_in)
    row_ahead = list(txt_long_in)
    img_ends = [plan.send(after(img_hops[(b - 1) * far], *col_ahead), "col", -b) for b in range(1, col)]
    txt_ends = [plan.send(after(txt_hops[(b - 1) * near], *row_ahead), "row", -b) for b in range(1, row)]
    image_grad = final(student_img, img_stay[0], img_ends + img_last, img_side + long_in, half)
    text_grad = final(student_txt, txt_stay[0], txt_ends + txt_last, txt_side + txt_long_in, half)
    return image_grad, text_grad


def solution(mesh):
    spec = P(AXES, None)
    return jax.shard_map(
        functools.partial(body, Plan(mesh)), mesh=mesh, in_specs=(spec,) * 4, out_specs=(spec,) * 2, check_vma=False
    )
```
